32 devices in a mesh: dp: 8 (over y, x, core), mp: 4 (over z).
Axes of the slice: x: 2, y: 2, z: 4, core: 2. Of those that a mesh axis runs over, the one named last changes fastest.
Arguments:
- tokens: bfloat16 [8192, 2048], P('dp'), may hold values from -6 to 6
- lengths: int32 [8, 8], P('dp'), may hold values from 1 to 768, 1024 in all within a row
- attn_gain: float32 [2048], replicated, may hold values from 0.1 to 1.9
- attn_shift: float32 [2048], replicated, may hold values from -4 to 4
- mlp_gain: float32 [2048], replicated, may hold values from 0.1 to 1.9
- mlp_shift: float32 [2048], replicated, may hold values from -4 to 4
- qkv_weight: bfloat16 [2048, 6144], P(None, 'mp'), may hold values from -0.125 to 0.125
- qkv_bias: float32 [6144], P('mp'), may hold values from -4 to 4
- dense_weight: bfloat16 [2048, 2048], P('mp'), may hold values from -0.5 to 0.5
- up_weight: bfloat16 [2048, 8192], P(None, 'mp'), may hold values from -0.125 to 0.125
- up_bias: float32 [8192], P('mp'), may hold values from -6 to 6
- down_weight: bfloat16 [8192, 2048], P('mp'), may hold values from -0.0625 to 0.0625
- out_bias: float32 [2048], replicated, may hold values from -6 to 6
- cotangent: bfloat16 [8192, 2048], P('dp'), may hold values from -6 to 6
Outputs:
- layer_output: bfloat16 [8192, 2048], P('dp')
- input_grad: bfloat16 [8192, 2048], P('dp')
- attn_gain_grad: float32 [2048], P('dp')
- attn_shift_grad: float32 [2048], P('dp')
- mlp_gain_grad: float32 [2048], P('dp')
- mlp_shift_grad: float32 [2048], P('dp')
- qkv_weight_grad: float32 [2048, 6144], P('dp', 'mp')
- qkv_bias_grad: float32 [6144], P(('mp', 'dp'))
- dense_weight_grad: float32 [2048, 2048], P('mp', 'dp')
- up_weight_grad: float32 [2048, 8192], P('dp', 'mp')
- up_bias_grad: float32 [8192], P(('mp', 'dp'))
- down_weight_grad: float32 [8192, 2048], P('mp', 'dp')
- out_bias_grad: float32 [2048], P('dp')
The draws below stay inside these ranges and needn't reach their ends.
Inputs may be any that keep to these rules, and one draw needn't show every extreme that they name: Each row holds 8 sequence lengths that add up to 1024; in every row the longest is exactly 768.
All inputs are finite; a program needn't handle non-finite values.
Results may differ from the reference program's by a relative error of at most 0.0095.
Values sent between devices are 32-bit elements; how exact they have to be, the bound alone decides.
A program may use at most 256 MiB of HBM per device.

```python
import math
import jax
import jax.numpy as jnp
import numpy as np
from jax import lax

D = 2048
HEADS = 8
HEAD_DIM = 256
FF = 8192
ROT = 64
TOK_DEV = 1024
SEQS = 8
MAXLEN = 768
TOKENS = 8192
N_DP = 8


def with_spikes(array, key, source, target, blocks, factor):
    def block_of(dim):
        return (jnp.arange(array.shape[dim]) // (array.shape[dim] // blocks)).reshape((-1,) + (1,) * (array.ndim - 1 - dim))

    near = jax.random.permutation(key, blocks)[block_of(target)]
    second = (block_of(target) + blocks // 2) % blocks
    return jnp.where((block_of(source) == near) | (block_of(source) == second), factor * array, array)


def block_levels(own_key, dims, pieces, low, largest):
    level = 1.0
    for axis_at, parts in pieces:
        steps = jax.random.uniform(jax.random.fold_in(jax.random.fold_in(own_key, 6), axis_at), (parts,), jnp.float32, low / len(pieces), largest / len(pieces))
        level = level * jnp.repeat(jnp.exp(steps), dims[axis_at] // parts).reshape((-1,) + (1,) * (len(dims) - 1 - axis_at))
    return level


def split_up(amount, total, bound, skew):
    portions = [(1 << 20) // math.isqrt(rank ** skew) + 1 for rank in range(2, amount + 1)]
    rest, holding = total - bound - (amount - 1), [1] * (amount - 1)
    while rest > 0:
        movable = [i for i in range(amount - 1) if holding[i] < bound]
        mass, budget = sum([portions[i] for i in movable]), rest
        for i in movable:
            extra = min(bound - holding[i], max(1, budget * portions[i] // mass), rest)
            holding[i] = holding[i] + extra
            rest = rest - extra
    return np.array([bound] + holding)


def ragged_sizes(rng, number_of, total, reach, slope):
    if number_of == 2:
        one = jax.random.randint(rng, (), max(1, total - reach), min(reach, total - 1) + 1)
        return jnp.stack([one, total - one])
    tallies = jnp.asarray(split_up(number_of, total, reach, slope), jnp.int32)
    pairs = (number_of - 1) // 2
    source_of, taker = tallies[1:1 + 2 * pairs:2], tallies[2:2 + 2 * pairs:2]
    slack = jnp.minimum(source_of - 1, reach - taker)
    moved = jax.random.randint(jax.random.fold_in(rng, 1), (pairs,), 0, 1 << 20) % (slack + 1)
    tallies = tallies.at[1:1 + 2 * pairs:2].set(source_of - moved).at[2:2 + 2 * pairs:2].set(taker + moved)
    return tallies[jax.random.permutation(jax.random.fold_in(rng, 2), number_of)]


def scatter_about(own_key, extent, scale, limit, shards=(), held_as=jnp.bfloat16):
    factor_of = block_levels(own_key, extent, shards, -0.22, 0.18) if shards else 1.0
    drawn = jax.random.normal(own_key, extent, jnp.float32) * scale * factor_of
    return jnp.minimum(jnp.maximum(drawn, -limit), limit).astype(held_as)


def bell_draw_with(rng, shape, scale, reach, pieces, heavy, held_as=jnp.bfloat16):
    values = scale * jax.random.normal(rng, shape, jnp.float32)
    if pieces:
        values = values * block_levels(rng, shape, pieces, -0.22, 0.18)
    return jnp.clip(with_spikes(values, jax.random.fold_in(rng, 3), *heavy), -reach, reach).astype(held_as)


def setup_inputs(seed: int = 0) -> dict:
    keys = jax.random.split(jax.random.key(seed), 15)
    return {
        "tokens": scatter_about(keys[0], (TOKENS, D), 1.0, 6.0, ((0, 8),)),
        "lengths": jax.vmap(lambda own: ragged_sizes(own, SEQS, TOK_DEV, MAXLEN, 2))(jax.random.split(keys[1], N_DP)).reshape((N_DP, SEQS)).astype(jnp.int32),
        "attn_gain": jnp.clip(1.0 + 0.18 * jax.random.normal(keys[2], (D,), jnp.float32), 0.1, 1.9),
        "attn_shift": scatter_about(keys[3], (D,), 0.3, 4.0, (), jnp.float32),
        "mlp_gain": jnp.clip(1.0 + 0.18 * jax.random.normal(keys[4], (D,), jnp.float32), 0.1, 1.9),
        "mlp_shift": scatter_about(keys[5], (D,), 0.3, 4.0, (), jnp.float32),
        "qkv_weight": scatter_about(keys[6], (D, 3 * D), D ** -0.5, 0.125, ((1, 4),)),
        "qkv_bias": scatter_about(keys[7], (3 * D,), 0.3, 4.0, ((0, 4),), jnp.float32),
        "dense_weight": scatter_about(keys[8], (D, D), (D // 16) ** -0.5, 0.5, ((0, 4),)),
        "up_weight": scatter_about(keys[9], (D, FF), D ** -0.5, 0.125, ((1, 4),)),
        "up_bias": scatter_about(keys[10], (FF,), 0.5, 6.0, ((0, 4),), jnp.float32),
        "down_weight": scatter_about(keys[11], (FF, D), FF ** -0.5, 0.0625, ((0, 4),)),
        "out_bias": scatter_about(keys[12], (D,), 0.5, 6.0, (), jnp.float32),
        "cotangent": bell_draw_with(keys[13], (TOKENS, D), 1.0, 6.0, ((0, 8),), (0, 1, 8, 2.0)),
    }


@jax.custom_vjp
def low(v):
    return lax.optimization_barrier(v.astype(jnp.bfloat16)).astype(jnp.float32)

@jax.custom_vjp
def low_back(v):
    return v

def low_keep(v):
    return (low(v), None)

def low_pass(kept, grad):
    return (grad,)

def back_keep(v):
    return (v, None)

def back_low(kept, grad):
    return (low(grad),)
low.defvjp(low_keep, low_pass)
low_back.defvjp(back_keep, back_low)
HIGHEST = lax.Precision.HIGHEST
EPSILON = 1e-05

def layer_norm(matrix, gain, shift):
    centred = matrix - lax.optimization_barrier(jnp.mean(matrix, axis=-1, keepdims=True))
    spread = lax.optimization_barrier(jnp.mean(centred * centred, axis=-1, keepdims=True))
    return centred * lax.rsqrt(spread + EPSILON) * gain + shift

def rotate(field, position):
    half = ROT // 2
    steps = jnp.arange(half, dtype=jnp.float32)
    freqs = jnp.exp(steps * (-2.0 * math.log(10000.0) / ROT))
    angle = position.astype(jnp.float32)[:, None] * freqs[None, :]
    cosine = jnp.concatenate([jnp.cos(angle), jnp.cos(angle)], axis=-1)[:, None, :]
    sine = jnp.concatenate([jnp.sin(angle), jnp.sin(angle)], axis=-1)[:, None, :]
    turned = field[..., :ROT]
    swapped = jnp.concatenate([-turned[..., half:], turned[..., :half]], axis=-1)
    return jnp.concatenate([turned * cosine + swapped * sine, field[..., ROT:]], axis=-1)

def layout(lengths_row):
    ends = jnp.cumsum(lengths_row).astype(jnp.int32)
    places = jnp.arange(TOK_DEV, dtype=jnp.int32)
    passed = (places[:, None] >= ends[None, :]).astype(jnp.int32)
    segment = lax.optimization_barrier(jnp.sum(passed, axis=1)).astype(jnp.int32)
    position = (places - lax.optimization_barrier(jnp.sum(passed * lengths_row[None, :], axis=1))).astype(jnp.int32)
    return (segment, position)

def row_forward(params, matrix, segment, position):
    attn_gain, attn_shift, mlp_gain, mlp_shift, qkv_weight, qkv_bias, dense_weight, up_weight, up_bias, down_weight, out_bias = params
    count = matrix.shape[0]
    attn_entry = low(layer_norm(matrix, attn_gain, attn_shift))
    mlp_entry = low(layer_norm(matrix, mlp_gain, mlp_shift))
    joined = low_back(jnp.dot(attn_entry, qkv_weight, precision=HIGHEST) + qkv_bias)
    joined = joined.reshape(count, HEADS, 3, HEAD_DIM)
    queries = low(rotate(joined[:, :, 0], position))
    keys_turned = low(rotate(joined[:, :, 1], position))
    values = low(joined[:, :, 2])
    scale = 1.0 / math.sqrt(HEAD_DIM)
    scores = low_back(jnp.einsum('thd,shd->hts', queries, keys_turned, precision=HIGHEST) * scale)
    places = jnp.arange(count)
    allowed = (segment[:, None] == segment[None, :]) & (places[:, None] >= places[None, :])
    scores = jnp.where(allowed[None], scores, -1e+30)
    peak = lax.optimization_barrier(jnp.max(scores, axis=-1, keepdims=True))
    expo = jnp.exp(scores - peak)
    probs = expo / lax.optimization_barrier(jnp.sum(expo, axis=-1, keepdims=True))
    attended = jnp.einsum('hts,shd->thd', low(probs), values, precision=HIGHEST)
    attended = low_back(low(attended)).reshape(count, D)
    hidden = low(jax.nn.gelu(low_back(jnp.dot(mlp_entry, up_weight, precision=HIGHEST) + up_bias), approximate=False))
    branch = jnp.dot(attended, dense_weight, precision=HIGHEST) + jnp.dot(hidden, down_weight, precision=HIGHEST)
    return matrix + branch + out_bias

def reference(tokens, lengths, attn_gain, attn_shift, mlp_gain, mlp_shift, qkv_weight, qkv_bias, dense_weight, up_weight, up_bias, down_weight, out_bias, cotangent):
    params = tuple((item.astype(jnp.float32) for item in (attn_gain, attn_shift, mlp_gain, mlp_shift, qkv_weight, qkv_bias, dense_weight, up_weight, up_bias, down_weight, out_bias)))
    matrices = tokens.astype(jnp.float32).reshape(N_DP, TOK_DEV, D)
    segments, positions = jax.vmap(layout)(lengths)

    def forward(params, matrices):
        single = jax.checkpoint(lambda matrix, segment, position: row_forward(params, matrix, segment, position))

        def scan_step(carry, item):
            return (carry, single(item[0], item[1], item[2]))
        return lax.scan(scan_step, jnp.zeros((), jnp.float32), (matrices, segments, positions))[1]
    result, pullback = jax.vjp(forward, params, matrices)
    grads, input_rows = pullback(cotangent.astype(jnp.float32).reshape(N_DP, TOK_DEV, D))
    return (result.reshape(TOKENS, D).astype(jnp.bfloat16), input_rows.reshape(TOKENS, D).astype(jnp.bfloat16), grads[0], grads[1], grads[2], grads[3], grads[4], grads[5], grads[6], grads[7], grads[8], grads[9], grads[10])
```

```python
import functools
import math

import jax
import jax.numpy as jnp
from jax import lax
from jax.sharding import PartitionSpec as P

HEAD_DIM = 256
ROT = 64


EPSILON = 1e-05


def rotate(field, position):
    half = ROT // 2
    steps = jnp.arange(half, dtype=jnp.float32)
    freqs = jnp.exp(steps * (-2.0 * math.log(10000.0) / ROT))
    angle = position.astype(jnp.float32)[:, None] * freqs[None, :]
    cosine = jnp.concatenate([jnp.cos(angle), jnp.cos(angle)], axis=-1)[:, None, :]
    sine = jnp.concatenate([jnp.sin(angle), jnp.sin(angle)], axis=-1)[:, None, :]
    turned = field[..., :ROT]
    swapped = jnp.concatenate([-turned[..., half:], turned[..., :half]], axis=-1)
    return jnp.concatenate([turned * cosine + swapped * sine, field[..., ROT:]], axis=-1)


def layout(lengths_row, count):
    ends = jnp.cumsum(lengths_row)
    places = jnp.arange(count, dtype=jnp.int32)
    passed = (places[:, None] >= ends[None, :]).astype(jnp.int32)
    segment = jnp.sum(passed, axis=1)
    position = places - jnp.sum(passed * lengths_row[None, :], axis=1)
    return (segment, position)


def contract_rows(left, right):
    return lax.dot_general(
        left, right, (((0,), (0,)), ((), ())), preferred_element_type=jnp.float32
    )


def contract_cols(left, right):
    return lax.dot_general(
        left, right, (((1,), (1,)), ((), ())), preferred_element_type=jnp.float32
    )


def line_sum(part, size):
    if size == 1:
        return part
    if size % 2:
        return lax.psum(part, "mp")
    index = lax.axis_index("mp")
    half = size // 2
    total = part
    for hop in range(half - 1):
        pairs = [(hop, hop + 1), (size - 1 - hop, size - 2 - hop)]
        total = total + lax.ppermute(total, "mp", pairs)
    total = total + lax.ppermute(total, "mp", [(half - 1, half), (half, half - 1)])
    for hop in reversed(range(half - 1)):
        pairs = [(hop + 1, hop), (size - 2 - hop, size - 1 - hop)]
        came = lax.ppermute(total, "mp", pairs)
        total = jnp.where((index == hop) | (index == size - 1 - hop), came, total)
    return total


CHUNK = 128


def per_device(
    mp_size,
    tokens,
    lengths,
    attn_gain,
    attn_shift,
    mlp_gain,
    mlp_shift,
    qkv_weight,
    qkv_bias,
    dense_weight,
    up_weight,
    up_bias,
    down_weight,
    out_bias,
    cotangent,
):
    count = tokens.shape[0]
    local_heads = qkv_weight.shape[1] // (3 * HEAD_DIM)
    width = local_heads * HEAD_DIM
    segment, position = layout(lengths[0], count)
    block = min(512, count)
    blocks = count // block
    scale = 1.0 / math.sqrt(HEAD_DIM)
    places = jnp.arange(count, dtype=jnp.int32)
    inputs = tokens.astype(jnp.float32)
    centred = inputs - jnp.mean(inputs, axis=-1, keepdims=True)
    factor = lax.rsqrt(jnp.mean(centred * centred, axis=-1, keepdims=True) + EPSILON)
    xhat = centred * factor
    attn_entry = (xhat * attn_gain + attn_shift).astype(jnp.bfloat16)
    mlp_entry = (xhat * mlp_gain + mlp_shift).astype(jnp.bfloat16)
    joined = jnp.dot(attn_entry, qkv_weight, preferred_element_type=jnp.float32) + qkv_bias
    joined = joined.reshape(count, local_heads, 3, HEAD_DIM)
    turned_query, query_back = jax.vjp(lambda field: rotate(field, position), joined[:, :, 0])
    turned_key, key_back = jax.vjp(lambda field: rotate(field, position), joined[:, :, 1])
    queries = turned_query.astype(jnp.bfloat16)
    keys_low = turned_key.astype(jnp.bfloat16)
    values_low = joined[:, :, 2].astype(jnp.bfloat16)

    def masked_scores(start):
        query_block = lax.dynamic_slice_in_dim(queries, start, block, 0)
        scores = (
            jnp.einsum("bhd,shd->hbs", query_block, keys_low, preferred_element_type=jnp.float32)
            * scale
        )
        rows_here = start + jnp.arange(block, dtype=jnp.int32)
        segment_block = lax.dynamic_slice_in_dim(segment, start, block, 0)
        allowed = (segment_block[:, None] == segment[None, :]) & (
            rows_here[:, None] >= places[None, :]
        )
        return (jnp.where(allowed[None], scores, -1e30), query_block)

    def forward_block(index):
        scores, query_block = masked_scores(index * block)
        peak = jnp.max(scores, axis=-1, keepdims=True)
        expo = jnp.exp(scores - peak)
        total = jnp.sum(expo, axis=-1, keepdims=True)
        probs = expo / total
        result = jnp.einsum(
            "hbs,shd->bhd",
            probs.astype(jnp.bfloat16),
            values_low,
            preferred_element_type=jnp.float32,
        )
        return (result, peak[..., 0] + jnp.log(total[..., 0]))

    attended, log_total = lax.map(forward_block, jnp.arange(blocks, dtype=jnp.int32))
    attended_low = attended.reshape(count, width).astype(jnp.bfloat16)

    chunk = min(CHUNK, count)
    outputs, pres, hiddens = [], [], []
    for first in range(0, count, chunk):
        rows = slice(first, first + chunk)
        pre = jnp.dot(mlp_entry[rows], up_weight, preferred_element_type=jnp.float32) + up_bias
        hidden = jax.nn.gelu(pre, approximate=False).astype(jnp.bfloat16)
        part = jnp.dot(
            attended_low[rows], dense_weight, preferred_element_type=jnp.float32
        ) + jnp.dot(hidden, down_weight, preferred_element_type=jnp.float32)
        branch = line_sum(part, mp_size)
        outputs.append((inputs[rows] + branch + out_bias).astype(jnp.bfloat16))
        pres.append(pre)
        hiddens.append(hidden)
    layer_output = jnp.concatenate(outputs)
    hidden_pre = jnp.concatenate(pres)
    hidden_low = jnp.concatenate(hiddens)
    _, gelu_back = jax.vjp(lambda field: jax.nn.gelu(field, approximate=False), hidden_pre)

    out_bias_grad = jnp.sum(cotangent.astype(jnp.float32), axis=0)
    dense_grad = contract_rows(attended_low, cotangent)
    down_grad = contract_rows(hidden_low, cotangent)
    hidden_grad = gelu_back(contract_cols(cotangent, down_weight))[0].astype(jnp.bfloat16)
    up_grad = contract_rows(mlp_entry, hidden_grad)
    up_bias_grad = jnp.sum(hidden_grad.astype(jnp.float32), axis=0)
    mlp_entry_grad = contract_cols(hidden_grad, up_weight)
    attended_grad = (
        contract_cols(cotangent, dense_weight)
        .reshape(count, local_heads, HEAD_DIM)
        .astype(jnp.bfloat16)
    )

    def backward_block(carry, index):
        key_total, value_total = carry
        start = index * block
        scores, query_block = masked_scores(start)
        probs = jnp.exp(scores - log_total[index][:, :, None])
        grad_block = lax.dynamic_slice_in_dim(attended_grad, start, block, 0)
        prob_grad = jnp.einsum(
            "bhd,shd->hbs", grad_block, values_low, preferred_element_type=jnp.float32
        )
        inner = jnp.sum(probs * prob_grad, axis=-1, keepdims=True)
        score_grad = (probs * (prob_grad - inner)).astype(jnp.bfloat16)
        query_part = (
            jnp.einsum("hbs,shd->bhd", score_grad, keys_low, preferred_element_type=jnp.float32)
            * scale
        )
        key_total = (
            key_total
            + jnp.einsum(
                "hbs,bhd->shd", score_grad, query_block, preferred_element_type=jnp.float32
            )
            * scale
        )
        value_total = value_total + jnp.einsum(
            "hbs,bhd->shd",
            probs.astype(jnp.bfloat16),
            grad_block,
            preferred_element_type=jnp.float32,
        )
        return ((key_total, value_total), query_part)

    empty = jnp.zeros((count, local_heads, HEAD_DIM), jnp.float32)
    (key_grad, value_grad), query_grad = lax.scan(
        backward_block, (empty, empty), jnp.arange(blocks, dtype=jnp.int32)
    )
    query_grad = query_grad.reshape(count, local_heads, HEAD_DIM)
    joined_grad = jnp.stack([query_back(query_grad)[0], key_back(key_grad)[0], value_grad], axis=2)
    joined_grad = joined_grad.reshape(count, 3 * width).astype(jnp.bfloat16)
    qkv_grad = contract_rows(attn_entry, joined_grad)
    qkv_bias_grad = jnp.sum(joined_grad.astype(jnp.float32), axis=0)
    attn_entry_grad = contract_cols(joined_grad, qkv_weight)

    both = attn_entry_grad * attn_gain + mlp_entry_grad * mlp_gain
    norm_grads = jnp.stack(
        [
            jnp.sum(attn_entry_grad * xhat, axis=0),
            jnp.sum(attn_entry_grad, axis=0),
            jnp.sum(mlp_entry_grad * xhat, axis=0),
            jnp.sum(mlp_entry_grad, axis=0),
        ]
    )
    grads_in = []
    for first in range(0, count, chunk):
        rows = slice(first, first + chunk)
        entry = line_sum(both[rows], mp_size)
        hat = xhat[rows]
        inner = (
            entry
            - jnp.mean(entry, axis=-1, keepdims=True)
            - hat * jnp.mean(entry * hat, axis=-1, keepdims=True)
        )
        grads_in.append(
            (cotangent[rows].astype(jnp.float32) + factor[rows] * inner).astype(jnp.bfloat16)
        )
    input_grad = jnp.concatenate(grads_in)

    def scattered(array, dimension):
        return lax.psum_scatter(array, "dp", scatter_dimension=dimension, tiled=True)

    norm_total = lax.psum(scattered(norm_grads, 1), "mp")
    return (
        layer_output,
        input_grad,
        norm_total[0],
        norm_total[1],
        norm_total[2],
        norm_total[3],
        scattered(qkv_grad, 0),
        scattered(qkv_bias_grad, 0),
        scattered(dense_grad, 1),
        scattered(up_grad, 0),
        scattered(up_bias_grad, 0),
        scattered(down_grad, 1),
        scattered(out_bias_grad, 0),
    )


def solution(mesh):
    in_specs = (
        P("dp", None),
        P("dp", None),
        P(),
        P(),
        P(),
        P(),
        P(None, "mp"),
        P("mp"),
        P("mp", None),
        P(None, "mp"),
        P("mp"),
        P("mp", None),
        P(),
        P("dp", None),
    )
    out_specs = (
        P("dp", None),
        P("dp", None),
        P("dp"),
        P("dp"),
        P("dp"),
        P("dp"),
        P("dp", "mp"),
        P(("mp", "dp")),
        P("mp", "dp"),
        P("dp", "mp"),
        P(("mp", "dp")),
        P("mp", "dp"),
        P("dp"),
    )
    return jax.shard_map(
        functools.partial(per_device, mesh.shape["mp"]), mesh=mesh, in_specs=in_specs, out_specs=out_specs, check_vma=False
    )
```

```python
import functools
import math

import jax
import jax.numpy as jnp
from jax import lax
from jax.experimental import pallas as pl
from jax.experimental.pallas import tpu as pltpu
from jax.sharding import PartitionSpec as P

HEAD_DIM = 256
ROT = 64


EPSILON = 1e-05


def rotate(field, position):
    half = ROT // 2
    steps = jnp.arange(half, dtype=jnp.float32)
    freqs = jnp.exp(steps * (-2.0 * math.log(10000.0) / ROT))
    angle = position.astype(jnp.float32)[:, None] * freqs[None, :]
    cosine = jnp.concatenate([jnp.cos(angle), jnp.cos(angle)], axis=-1)[:, None, :]
    sine = jnp.concatenate([jnp.sin(angle), jnp.sin(angle)], axis=-1)[:, None, :]
    turned = field[..., :ROT]
    swapped = jnp.concatenate([-turned[..., half:], turned[..., :half]], axis=-1)
    return jnp.concatenate([turned * cosine + swapped * sine, field[..., ROT:]], axis=-1)


def layout(lengths_row, count):
    ends = jnp.cumsum(lengths_row)
    places = jnp.arange(count, dtype=jnp.int32)
    passed = (places[:, None] >= ends[None, :]).astype(jnp.int32)
    segment = jnp.sum(passed, axis=1)
    position = places - jnp.sum(passed * lengths_row[None, :], axis=1)
    return (segment, position)


def contract_rows(left, right):
    return lax.dot_general(
        left, right, (((0,), (0,)), ((), ())), preferred_element_type=jnp.float32
    )


def contract_cols(left, right):
    return lax.dot_general(
        left, right, (((1,), (1,)), ((), ())), preferred_element_type=jnp.float32
    )


MESH = pl.DeviceIdType.MESH
ROWS = 64
CHUNK = 256


def gelu_parts(v):
    cdf = 0.5 + 0.5 * lax.erf(v * math.sqrt(0.5))
    return v * cdf, cdf + v * jnp.exp(-0.5 * v * v) * (1.0 / math.sqrt(2.0 * math.pi))


def layer_kernel(
    size,
    tokens,
    cotangent,
    mlp_entry,
    attended,
    up_weight,
    down_weight,
    dense_weight,
    up_bias,
    out_bias,
    layer_out,
    hidden_out,
    hidden_grad_out,
    part,
    from_outer,
    from_inner,
    token_rows,
    out_rows,
    send_in,
    send_out,
    recv_outer,
    recv_inner,
    row_sems,
    out_sems,
):
    count, width = tokens.shape
    inner_width = up_weight.shape[1]
    messages = count // ROWS
    half = size // 2
    index = lax.axis_index("mp")
    upper = index // half
    level = index * (1 - upper) + (size - 1 - index) * upper
    inner = index + 1 - 2 * upper
    outer = index - 1 + 2 * upper
    lag = half - level
    is_end = level == 0
    is_middle = level == half - 1

    barrier = pltpu.get_barrier_semaphore()
    pl.semaphore_signal(barrier, inc=1, device_id={"mp": inner}, device_id_type=MESH)

    @pl.when(level > 0)
    def _():
        pl.semaphore_signal(barrier, inc=1, device_id={"mp": outer}, device_id_type=MESH)
        pl.semaphore_wait(barrier, 2)

    @pl.when(level == 0)
    def _():
        pl.semaphore_wait(barrier, 1)

    def rows_of(ref, k):
        return ref.at[pl.ds(pl.multiple_of(lax.rem(k, messages) * ROWS, ROWS), ROWS)]

    def to_inner(k, landing, sem):
        return pltpu.make_async_remote_copy(
            src_ref=rows_of(part, k),
            dst_ref=rows_of(landing, k),
            send_sem=send_in.at[k],
            recv_sem=sem.at[k],
            device_id={"mp": inner},
            device_id_type=MESH,
        )

    def to_outer(k, source):
        return pltpu.make_async_remote_copy(
            src_ref=rows_of(source, k),
            dst_ref=rows_of(from_inner, k),
            send_sem=send_out.at[k],
            recv_sem=recv_inner.at[k],
            device_id={"mp": outer},
            device_id_type=MESH,
        )

    def send_inward(k):
        @pl.when(is_middle)
        def _():
            to_inner(k, from_inner, recv_inner).start()

        if half > 1:

            @pl.when(level < half - 1)
            def _():
                to_inner(k, from_outer, recv_outer).start()

    def emit(k):
        @pl.when(is_end)
        def _():
            send_inward(k)

    def load_rows(k):
        return pltpu.make_async_copy(
            tokens.at[pl.ds(pl.multiple_of(k * ROWS, ROWS), ROWS)],
            token_rows.at[lax.rem(k, 2)],
            row_sems.at[lax.rem(k, 2)],
        )

    def store_rows(k):
        return pltpu.make_async_copy(
            out_rows.at[lax.rem(k, 2)],
            layer_out.at[pl.ds(pl.multiple_of(k * ROWS, ROWS), ROWS)],
            out_sems.at[lax.rem(k, 2)],
        )

    def finish(k, source):
        total = rows_of(source, k)[...]
        out_rows[lax.rem(k, 2)] = (
            token_rows[lax.rem(k, 2)].astype(jnp.float32) + total + out_bias[...]
        ).astype(jnp.bfloat16)

    def service(j):
        @pl.when((level > 0) & (j < messages))
        def _():
            to_inner(j, from_outer, recv_outer).wait_recv()
            rows_of(part, j)[...] += rows_of(from_outer, j)[...]
            send_inward(j)

        k = j - lag

        @pl.when((k >= 0) & (k < messages))
        def _():
            to_outer(k, part).wait_recv()
            to_inner(k, from_inner, recv_inner).wait_send()

            @pl.when(k + 1 < messages)
            def _():
                load_rows(k + 1).start()

            load_rows(k).wait()

            @pl.when(k >= 2)
            def _():
                store_rows(k - 2).wait()

            @pl.when(is_middle)
            def _():
                rows_of(part, k)[...] += rows_of(from_inner, k)[...]

            if half > 1:

                @pl.when(level > 0)
                def _():
                    @pl.when(k >= 1)
                    def _():
                        to_outer(k - 1, part).wait_send()

                    @pl.when(is_middle)
                    def _():
                        to_outer(k, part).start()

                    @pl.when(level < half - 1)
                    def _():
                        to_outer(k, from_inner).start()

            @pl.when(is_middle)
            def _():
                finish(k, part)

            if half > 1:

                @pl.when(level < half - 1)
                def _():
                    finish(k, from_inner)

            store_rows(k).start()

    load_rows(0).start()

    def feed_forward(up, down, dense, entry, cot, att, hid, hgrad, slope, w_sems, in_sems, h_sems):
        up_copy = pltpu.make_async_copy(up_weight, up, w_sems.at[0])
        down_copy = pltpu.make_async_copy(down_weight, down, w_sems.at[1])
        dense_copy = pltpu.make_async_copy(dense_weight, dense, w_sems.at[2])
        steps = count // CHUNK
        tile = min(512, inner_width)
        wide = min(512, width)

        def loads(c):
            slot = lax.rem(c, 2)
            rows = pl.ds(pl.multiple_of(c * CHUNK, CHUNK), CHUNK)
            return [
                pltpu.make_async_copy(source.at[rows], target.at[slot], in_sems.at[slot, i])
                for i, (source, target) in enumerate(
                    ((mlp_entry, entry), (attended, att), (cotangent, cot))
                )
            ]

        def stores(c):
            rows = pl.ds(pl.multiple_of(c * CHUNK, CHUNK), CHUNK)
            return [
                pltpu.make_async_copy(hid, hidden_out.at[rows], h_sems.at[0]),
                pltpu.make_async_copy(hgrad, hidden_grad_out.at[rows], h_sems.at[1]),
            ]

        for copy in loads(0):
            copy.start()
        up_copy.start()
        down_copy.start()
        dense_copy.start()

        @pl.loop(0, steps)
        def _(c):
            slot = lax.rem(c, 2)

            @pl.when(c + 1 < steps)
            def _():
                for copy in loads(c + 1):
                    copy.start()

            for copy in loads(c):
                copy.wait()

            @pl.when(c == 0)
            def _():
                up_copy.wait()

            @pl.when(c > 0)
            def _():
                stores(c - 1)[0].wait()

            @pl.loop(0, inner_width // tile)
            def _(t):
                cols = pl.ds(pl.multiple_of(t * tile, tile), tile)
                pre = (
                    jnp.dot(entry[slot], up[:, cols], preferred_element_type=jnp.float32)
                    + up_bias[:, cols]
                )
                value, der = gelu_parts(pre)
                hid[:, cols] = value.astype(jnp.bfloat16)
                slope[:, cols] = der

            @pl.when(c == 0)
            def _():
                down_copy.wait()
                dense_copy.wait()

            rows = pl.ds(pl.multiple_of(c * CHUNK, CHUNK), CHUNK)

            @pl.loop(0, width // wide)
            def _(t):
                cols = pl.ds(pl.multiple_of(t * wide, wide), wide)
                part[rows, cols] = jnp.dot(
                    hid[...], down[:, cols], preferred_element_type=jnp.float32
                ) + jnp.dot(att[slot], dense[:, cols], preferred_element_type=jnp.float32)

            @pl.loop(0, CHUNK // ROWS)
            def _(m):
                emit(c * (CHUNK // ROWS) + m)

            stores(c)[0].start()

            @pl.when(c > 0)
            def _():
                stores(c - 1)[1].wait()

            @pl.loop(0, inner_width // tile)
            def _(t):
                cols = pl.ds(pl.multiple_of(t * tile, tile), tile)
                back = lax.dot_general(
                    cot[slot],
                    down[cols, :],
                    (((1,), (1,)), ((), ())),
                    preferred_element_type=jnp.float32,
                )
                hgrad[:, cols] = (back * slope[:, cols]).astype(jnp.bfloat16)

            stores(c)[1].start()
            service(c)

        for copy in stores(steps - 1):
            copy.wait()

    pl.run_scoped(
        feed_forward,
        pltpu.VMEM(up_weight.shape, jnp.bfloat16),
        pltpu.VMEM(down_weight.shape, jnp.bfloat16),
        pltpu.VMEM(dense_weight.shape, jnp.bfloat16),
        pltpu.VMEM((2, CHUNK, width), jnp.bfloat16),
        pltpu.VMEM((2, CHUNK, width), jnp.bfloat16),
        pltpu.VMEM((2, CHUNK, dense_weight.shape[0]), jnp.bfloat16),
        pltpu.VMEM((CHUNK, inner_width), jnp.bfloat16),
        pltpu.VMEM((CHUNK, inner_width), jnp.bfloat16),
        pltpu.VMEM((CHUNK, inner_width), jnp.float32),
        pltpu.SemaphoreType.DMA((3,)),
        pltpu.SemaphoreType.DMA((2, 3)),
        pltpu.SemaphoreType.DMA((2,)),
    )

    @pl.loop(count // CHUNK, messages + half)
    def _(j):
        service(j)

    if half > 1:

        @pl.when(level > 0)
        def _():
            to_outer(messages - 1, part).wait_send()

    store_rows(messages - 2).wait()
    store_rows(messages - 1).wait()


def layer_call(size, tokens, cotangent, mlp_entry, attended, up, down, dense, up_bias, out_bias):
    count, width = tokens.shape
    messages = count // ROWS
    anywhere = pl.BlockSpec(memory_space=pl.ANY)
    vmem = pl.BlockSpec(memory_space=pltpu.VMEM)
    return pl.pallas_call(
        functools.partial(layer_kernel, size),
        out_shape=(
            jax.ShapeDtypeStruct((count, width), jnp.bfloat16),
            jax.ShapeDtypeStruct((count, up.shape[1]), jnp.bfloat16),
            jax.ShapeDtypeStruct((count, up.shape[1]), jnp.bfloat16),
        ),
        in_specs=[anywhere] * 7 + [vmem] * 2,
        out_specs=(anywhere,) * 3,
        scratch_shapes=[
            pltpu.VMEM((count, width), jnp.float32),
            pltpu.VMEM((count, width), jnp.float32),
            pltpu.VMEM((count, width), jnp.float32),
            pltpu.VMEM((2, ROWS, width), jnp.bfloat16),
            pltpu.VMEM((2, ROWS, width), jnp.bfloat16),
            pltpu.SemaphoreType.DMA((messages,)),
            pltpu.SemaphoreType.DMA((messages,)),
            pltpu.SemaphoreType.DMA((messages,)),
            pltpu.SemaphoreType.DMA((messages,)),
            pltpu.SemaphoreType.DMA((2,)),
            pltpu.SemaphoreType.DMA((2,)),
        ],
        compiler_params=pltpu.CompilerParams(
            collective_id=0, has_side_effects=True, vmem_limit_bytes=60 * 1024 * 1024
        ),
        cost_estimate=pl.CostEstimate(
            flops=6 * count * width * up.shape[1], bytes_accessed=40 << 20, transcendentals=0
        ),
    )(tokens, cotangent, mlp_entry, attended, up, down, dense, up_bias[None], out_bias[None])


def per_device(
    mp_size,
    tokens,
    lengths,
    attn_gain,
    attn_shift,
    mlp_gain,
    mlp_shift,
    qkv_weight,
    qkv_bias,
    dense_weight,
    up_weight,
    up_bias,
    down_weight,
    out_bias,
    cotangent,
):
    count = tokens.shape[0]
    local_heads = qkv_weight.shape[1] // (3 * HEAD_DIM)
    width = local_heads * HEAD_DIM
    segment, position = layout(lengths[0], count)
    block = min(512, count)
    blocks = count // block
    scale = 1.0 / math.sqrt(HEAD_DIM)
    places = jnp.arange(count, dtype=jnp.int32)
    inputs = tokens.astype(jnp.float32)
    centred = inputs - jnp.mean(inputs, axis=-1, keepdims=True)
    factor = lax.rsqrt(jnp.mean(centred * centred, axis=-1, keepdims=True) + EPSILON)
    xhat = centred * factor
    attn_entry = (xhat * attn_gain + attn_shift).astype(jnp.bfloat16)
    mlp_entry = (xhat * mlp_gain + mlp_shift).astype(jnp.bfloat16)
    joined = jnp.dot(attn_entry, qkv_weight, preferred_element_type=jnp.float32) + qkv_bias
    joined = joined.reshape(count, local_heads, 3, HEAD_DIM)
    turned_query, query_back = jax.vjp(lambda field: rotate(field, position), joined[:, :, 0])
    turned_key, key_back = jax.vjp(lambda field: rotate(field, position), joined[:, :, 1])
    queries = turned_query.astype(jnp.bfloat16)
    keys_low = turned_key.astype(jnp.bfloat16)
    values_low = joined[:, :, 2].astype(jnp.bfloat16)

    def masked_scores(start):
        query_block = lax.dynamic_slice_in_dim(queries, start, block, 0)
        scores = (
            jnp.einsum("bhd,shd->hbs", query_block, keys_low, preferred_element_type=jnp.float32)
            * scale
        )
        rows_here = start + jnp.arange(block, dtype=jnp.int32)
        segment_block = lax.dynamic_slice_in_dim(segment, start, block, 0)
        allowed = (segment_block[:, None] == segment[None, :]) & (
            rows_here[:, None] >= places[None, :]
        )
        return (jnp.where(allowed[None], scores, -1e30), query_block)

    def forward_block(index):
        scores, query_block = masked_scores(index * block)
        peak = jnp.max(scores, axis=-1, keepdims=True)
        expo = jnp.exp(scores - peak)
        total = jnp.sum(expo, axis=-1, keepdims=True)
        probs = expo / total
        result = jnp.einsum(
            "hbs,shd->bhd",
            probs.astype(jnp.bfloat16),
            values_low,
            preferred_element_type=jnp.float32,
        )
        return (result, peak[..., 0] + jnp.log(total[..., 0]))

    attended, log_total = lax.map(forward_block, jnp.arange(blocks, dtype=jnp.int32))
    attended_low = attended.reshape(count, width).astype(jnp.bfloat16)

    layer_output, hidden_low, hidden_grad = layer_call(
        mp_size,
        tokens,
        cotangent,
        mlp_entry,
        attended_low,
        up_weight,
        down_weight,
        dense_weight,
        up_bias,
        out_bias,
    )
    out_bias_grad = jnp.sum(cotangent.astype(jnp.float32), axis=0)
    dense_grad = contract_rows(attended_low, cotangent)
    down_grad = contract_rows(hidden_low, cotangent)
    up_grad = contract_rows(mlp_entry, hidden_grad)
    up_bias_grad = jnp.sum(hidden_grad.astype(jnp.float32), axis=0)
    mlp_entry_grad = contract_cols(hidden_grad, up_weight)
    attended_grad = (
        contract_cols(cotangent, dense_weight)
        .reshape(count, local_heads, HEAD_DIM)
        .astype(jnp.bfloat16)
    )

    def backward_block(carry, index):
        key_total, value_total = carry
        start = index * block
        scores, query_block = masked_scores(start)
        probs = jnp.exp(scores - log_total[index][:, :, None])
        grad_block = lax.dynamic_slice_in_dim(attended_grad, start, block, 0)
        prob_grad = jnp.einsum(
            "bhd,shd->hbs", grad_block, values_low, preferred_element_type=jnp.float32
        )
        inner = jnp.sum(probs * prob_grad, axis=-1, keepdims=True)
        score_grad = (probs * (prob_grad - inner)).astype(jnp.bfloat16)
        query_part = (
            jnp.einsum("hbs,shd->bhd", score_grad, keys_low, preferred_element_type=jnp.float32)
            * scale
        )
        key_total = (
            key_total
            + jnp.einsum(
                "hbs,bhd->shd", score_grad, query_block, preferred_element_type=jnp.float32
            )
            * scale
        )
        value_total = value_total + jnp.einsum(
            "hbs,bhd->shd",
            probs.astype(jnp.bfloat16),
            grad_block,
            preferred_element_type=jnp.float32,
        )
        return ((key_total, value_total), query_part)

    empty = jnp.zeros((count, local_heads, HEAD_DIM), jnp.float32)
    (key_grad, value_grad), query_grad = lax.scan(
        backward_block, (empty, empty), jnp.arange(blocks, dtype=jnp.int32)
    )
    query_grad = query_grad.reshape(count, local_heads, HEAD_DIM)
    joined_grad = jnp.stack([query_back(query_grad)[0], key_back(key_grad)[0], value_grad], axis=2)
    joined_grad = joined_grad.reshape(count, 3 * width).astype(jnp.bfloat16)
    qkv_grad = contract_rows(attn_entry, joined_grad)
    qkv_bias_grad = jnp.sum(joined_grad.astype(jnp.float32), axis=0)
    attn_entry_grad = contract_cols(joined_grad, qkv_weight)

    both = attn_entry_grad * attn_gain + mlp_entry_grad * mlp_gain
    norm_grads = jnp.stack(
        [
            jnp.sum(attn_entry_grad * xhat, axis=0),
            jnp.sum(attn_entry_grad, axis=0),
            jnp.sum(mlp_entry_grad * xhat, axis=0),
            jnp.sum(mlp_entry_grad, axis=0),
        ]
    )
    entry = lax.psum(both, "mp")
    inner = (
        entry
        - jnp.mean(entry, axis=-1, keepdims=True)
        - xhat * jnp.mean(entry * xhat, axis=-1, keepdims=True)
    )
    input_grad = (cotangent.astype(jnp.float32) + factor * inner).astype(jnp.bfloat16)
    def scattered(array, dimension):
        return lax.psum_scatter(array, "dp", scatter_dimension=dimension, tiled=True)

    norm_total = lax.psum(scattered(norm_grads, 1), "mp")
    return (
        layer_output,
        input_grad,
        norm_total[0],
        norm_total[1],
        norm_total[2],
        norm_total[3],
        scattered(qkv_grad, 0),
        scattered(qkv_bias_grad, 0),
        scattered(dense_grad, 1),
        scattered(up_grad, 0),
        scattered(up_bias_grad, 0),
        scattered(down_grad, 1),
        scattered(out_bias_grad, 0),
    )


def solution(mesh):
    in_specs = (
        P("dp", None),
        P("dp", None),
        P(),
        P(),
        P(),
        P(),
        P(None, "mp"),
        P("mp"),
        P("mp", None),
        P(None, "mp"),
        P("mp"),
        P("mp", None),
        P(),
        P("dp", None),
    )
    out_specs = (
        P("dp", None),
        P("dp", None),
        P("dp"),
        P("dp"),
        P("dp"),
        P("dp"),
        P("dp", "mp"),
        P(("mp", "dp")),
        P("mp", "dp"),
        P("dp", "mp"),
        P(("mp", "dp")),
        P("mp", "dp"),
        P("dp"),
    )
    return jax.shard_map(
        functools.partial(per_device, mesh.shape["mp"]), mesh=mesh, in_specs=in_specs, out_specs=out_specs, check_vma=False
    )
```

```python
import functools
import math

import jax
import jax.numpy as jnp
from jax import lax
from jax.experimental import pallas as pl
from jax.experimental.pallas import tpu as pltpu
from jax.sharding import PartitionSpec as P

HEAD_DIM = 256
ROT = 64
EPSILON = 1e-05
LANES = 128

MESH = pl.DeviceIdType.MESH
ROWS = 64
SLOTS = 6
AHEAD = 2
CHUNK = 256
BLOCK = 32

F32 = jnp.float32
BF16 = jnp.bfloat16

VECTORS = 8
ATTN_GAIN, ATTN_SHIFT, MLP_GAIN, MLP_SHIFT, OUT_BIAS, UP_BIAS, QKV_BIAS = range(7)


def layout(lengths_row, count):
    ends = jnp.cumsum(lengths_row)
    places = jnp.arange(count, dtype=jnp.int32)
    passed = (places[:, None] >= ends[None, :]).astype(jnp.int32)
    return jnp.sum(passed * lengths_row[None, :], axis=1)


def rotary_tables(start, count):
    lane = jnp.arange(LANES, dtype=jnp.int32)[None, :]
    half = ROT // 2
    steps = (lane % half).astype(F32)
    freqs = jnp.exp(steps * (-2.0 * math.log(10000.0) / ROT))
    position = jnp.arange(count, dtype=jnp.int32) - start
    angle = position.astype(F32)[:, None] * freqs
    cosine = jnp.where(lane < ROT, jnp.cos(angle), 1.0)
    sine = jnp.sin(angle)
    sine = jnp.where(lane < half, -sine, jnp.where(lane < ROT, sine, 0.0))
    return cosine, sine


def normalize(rows):
    centred = rows - jnp.mean(rows, axis=-1, keepdims=True)
    factor = lax.rsqrt(jnp.mean(centred * centred, axis=-1, keepdims=True) + EPSILON)
    return centred * factor, factor


def gelu_parts(v):
    cdf = 0.5 + 0.5 * lax.erf(v * math.sqrt(0.5))
    return v * cdf, cdf + v * jnp.exp(-0.5 * v * v) * (1.0 / math.sqrt(2.0 * math.pi))


def dot(left, right):
    return jnp.dot(left, right, preferred_element_type=F32)


def dot_cols(left, right):
    return lax.dot_general(left, right, (((1,), (1,)), ((), ())), preferred_element_type=F32)


def dot_rows(left, right):
    return lax.dot_general(left, right, (((0,), (0,)), ((), ())), preferred_element_type=F32)


def column_sum(x):
    return jnp.sum(x, axis=0, keepdims=True)


def span(start, size):
    return pl.ds(pl.multiple_of(start, size), size)


class Spread:
    def __init__(self, bits, rows, cols):
        self.bits, self.rows, self.cols = bits, rows, cols
        self.tiles = 1 << bits
        self.orders = ([0] + list(range(1, bits)), [0] + list(range(bits - 1, 0, -1)))
        count = self.tiles // 2
        self.first = {}
        for stage in range(1, bits):
            for side in range(2):
                self.first[stage, side] = count
                count += self.tiles >> (stage + 1)
        self.sems = count

    def masks(self, side, stage):
        order = self.orders[side]
        return [m for m in range(self.tiles) if not any((m >> b) & 1 for b in order[:stage])]

    def place(self, mask, side, stage):
        return self.masks(side, stage + 1).index(mask)

    def shapes(self):
        shapes = [(self.tiles // 2, self.rows, self.cols)]
        for stage in range(self.bits):
            shapes.append((self.tiles >> (stage + 1), self.rows, self.cols))
        return shapes


def layer_kernel(mp_size, plans, *refs):
    refs = list(refs)

    def take(number):
        taken = refs[:number]
        del refs[:number]
        return taken

    tokens, cotangent, qkv_weight, dense_weight, up_weight, down_weight = take(6)
    attn_gain, attn_shift, mlp_gain, mlp_shift, qkv_bias, up_bias, out_bias = take(7)
    cosine, sine, start = take(3)
    layer_out, input_grad, vectors_out, parts = take(4)
    attn_entry, mlp_entry, attended, hidden, hidden_grad = take(5)
    spreads = [(plan, take(1 + plan.bits)) for plan in plans]
    from_outer, from_inner, sums, token_rows, cot_rows, out_rows = take(6)
    vectors, vectors_in, joined_grad = take(3)
    send_in, send_out, recv_outer, recv_inner, part_sems, row_sems, out_sems = take(7)
    vec_send, vec_recv = take(2)
    spread_sems = [take(2) for _ in plans]

    count, width = tokens.shape
    inner_width = up_weight.shape[1]
    heads_width = dense_weight.shape[0]
    local_heads = heads_width // HEAD_DIM
    bits = plans[0].bits
    steps = count // CHUNK
    scale = 1.0 / math.sqrt(HEAD_DIM)
    branch_messages = count // ROWS
    messages = 2 * branch_messages
    chunk_messages = CHUNK // ROWS
    half = mp_size // 2

    index = lax.axis_index("mp")
    upper = index // half
    level = index * (1 - upper) + (mp_size - 1 - index) * upper
    inner = index + 1 - 2 * upper
    outer = index - 1 + 2 * upper
    lag = half - level
    is_middle = level == half - 1
    device = lax.axis_index("dp")

    def partner(bit):
        return device + (1 - 2 * ((device // (1 << bit)) % 2)) * (1 << bit)

    def owner(mask):
        total = 0
        for bit in range(bits):
            total = total + ((device // (1 << bit) + mask // (1 << bit)) % 2) * (1 << bit)
        return total

    barrier = pltpu.get_barrier_semaphore()
    pl.semaphore_signal(barrier, inc=1, device_id={"mp": inner}, device_id_type=MESH)
    for bit in range(bits):
        pl.semaphore_signal(barrier, inc=1, device_id={"dp": partner(bit)}, device_id_type=MESH)
    if half > 1:

        @pl.when(level > 0)
        def _():
            pl.semaphore_signal(barrier, inc=1, device_id={"mp": outer}, device_id_type=MESH)
            pl.semaphore_wait(barrier, 2 + bits)

        @pl.when(level == 0)
        def _():
            pl.semaphore_wait(barrier, 1 + bits)

    else:
        pl.semaphore_wait(barrier, 1 + bits)


    def slot(ref, k):
        return ref.at[lax.rem(k, SLOTS)]

    def message(ref, k):
        return ref.at[span(k * ROWS, ROWS)]

    def to_inner(k, source, landing, sem):
        return pltpu.make_async_remote_copy(
            src_ref=source,
            dst_ref=slot(landing, k),
            send_sem=send_in.at[k],
            recv_sem=sem.at[k],
            device_id={"mp": inner},
            device_id_type=MESH,
        )

    def to_outer(k, source):
        return pltpu.make_async_remote_copy(
            src_ref=slot(source, k),
            dst_ref=slot(from_inner, k),
            send_sem=send_out.at[k],
            recv_sem=recv_inner.at[k],
            device_id={"mp": outer},
            device_id_type=MESH,
        )

    def load_part(k):
        return pltpu.make_async_copy(message(parts, k), slot(sums, k), part_sems.at[lax.rem(k, 2)])

    def load_rows(k):
        row, place = lax.rem(k, branch_messages), lax.rem(k, 2)
        return [
            pltpu.make_async_copy(
                message(tokens, row), token_rows.at[place], row_sems.at[0, place]
            ),
            pltpu.make_async_copy(
                message(cotangent, row), cot_rows.at[place], row_sems.at[1, place]
            ),
        ]

    def store_rows(k, target):
        place = lax.rem(k, 2)
        return pltpu.make_async_copy(
            out_rows.at[place], message(target, lax.rem(k, branch_messages)), out_sems.at[place]
        )

    def send_ahead(k):
        if half > 1:

            @pl.when((level == 0) & (k < messages))
            def _():
                to_inner(k, message(parts, k), from_outer, recv_outer).start()

    def begin_messages():
        for k in range(AHEAD):
            send_ahead(k)
        for copy in load_rows(0):
            copy.start()
        if half > 1:

            @pl.when(level > 0)
            def _():
                load_part(0).start()

        else:
            load_part(0).start()

    def add_inward(j):
        @pl.when(j < messages)
        def _():
            load_part(j).wait()

            @pl.when(j + 1 < messages)
            def _():
                load_part(j + 1).start()

            mine = slot(sums, j)
            if half > 1:
                to_inner(j, mine, from_outer, recv_outer).wait_recv()
                mine[...] += slot(from_outer, j)[...]

            @pl.when(is_middle)
            def _():
                to_inner(j, mine, from_inner, recv_inner).start()

            if half > 2:

                @pl.when(level < half - 1)
                def _():
                    to_inner(j, mine, from_outer, recv_outer).start()

    def finish(k, source):
        place = lax.rem(k, 2)

        @pl.when(k < branch_messages)
        def _():
            @pl.loop(0, ROWS // BLOCK)
            def _(b):
                rows = span(b * BLOCK, BLOCK)
                out_rows[place, rows] = (
                    token_rows[place, rows].astype(F32) + source[rows] + out_bias[...]
                ).astype(BF16)

        @pl.when(k >= branch_messages)
        def _():
            @pl.loop(0, ROWS // BLOCK)
            def _(b):
                rows = span(b * BLOCK, BLOCK)
                hat, factor = normalize(token_rows[place, rows].astype(F32))
                entry = source[rows]
                part = (
                    entry
                    - jnp.mean(entry, axis=-1, keepdims=True)
                    - hat * jnp.mean(entry * hat, axis=-1, keepdims=True)
                )
                out_rows[place, rows] = (
                    cot_rows[place, rows].astype(F32) + factor * part
                ).astype(BF16)

    def pass_outward(k):
        @pl.when((k >= 0) & (k < messages))
        def _():
            landed = slot(from_inner, k)
            total = slot(sums, k)
            to_outer(k, sums).wait_recv()
            to_inner(k, total, from_inner, recv_inner).wait_send()

            @pl.when(is_middle)
            def _():
                total[...] += landed[...]

            if half > 1:

                @pl.when(level > 0)
                def _():
                    @pl.when(k >= 1)
                    def _():
                        to_outer(k - 1, sums).wait_send()

                    @pl.when(is_middle)
                    def _():
                        to_outer(k, sums).start()

                    if half > 2:

                        @pl.when(level < half - 1)
                        def _():
                            to_outer(k, from_inner).start()

            @pl.when(k + 1 < messages)
            def _():
                for copy in load_rows(k + 1):
                    copy.start()

            for copy in load_rows(k):
                copy.wait()

            @pl.when(k >= 2)
            def _():
                store_rows(k - 2, layer_out).wait()

            @pl.when(is_middle)
            def _():
                finish(k, total)

            if half > 1:

                @pl.when(level < half - 1)
                def _():
                    finish(k, landed)

            @pl.when(k < branch_messages)
            def _():
                store_rows(k, layer_out).start()

            @pl.when(k >= branch_messages)
            def _():
                store_rows(k, input_grad).start()

    def service(j):
        send_ahead(j + AHEAD)
        if half > 1:

            @pl.when(level > 0)
            def _():
                add_inward(j)

        else:
            add_inward(j)
        pass_outward(j - lag)

    def end_messages():
        if half > 1:

            @pl.when(level > 0)
            def _():
                to_outer(messages - 1, sums).wait_send()

        for k in (messages - 2, messages - 1):
            store_rows(k, input_grad).wait()


    def spread_copy(number, stage, side, source, target, sem, bit):
        sends, recvs = spread_sems[number]
        return pltpu.make_async_remote_copy(
            src_ref=source,
            dst_ref=target,
            send_sem=sends.at[sem],
            recv_sem=recvs.at[sem],
            device_id={"dp": partner(bit)},
            device_id_type=MESH,
        )

    def side_rows(plan, side):
        return pl.ds(side * (plan.rows // 2), plan.rows // 2)

    def stage_copies(number, stage, side):
        plan, buffers = spreads[number]
        keep, landing = buffers[0], buffers[1 + stage]
        bit = plan.orders[side][stage]
        copies = []
        for mask in plan.masks(side, stage):
            if (mask >> bit) & 1:
                place = plan.place(mask ^ (1 << bit), side, stage)
                copies.append(
                    spread_copy(
                        number,
                        stage,
                        side,
                        keep.at[mask // 2, side_rows(plan, side)],
                        landing.at[place, side_rows(plan, side)],
                        plan.first[stage, side] + place,
                        bit,
                    )
                )
        return copies

    def tiles_out(number, compute, tile, sems):
        plan, buffers = spreads[number]
        half_tiles = plan.tiles // 2

        def copy(i):
            return spread_copy(
                number, 0, 0, tile.at[lax.rem(i, 2)], buffers[1].at[i], i, 0
            )

        @pl.loop(0, half_tiles)
        def _(i):
            @pl.when(i >= 2)
            def _():
                copy(i - 2).wait_send()

            compute(owner(2 * i + 1), tile.at[lax.rem(i, 2)])
            copy(i).start()

        for i in (half_tiles - 2, half_tiles - 1):
            copy(i).wait_send()

    def tiles_kept(number, compute, tile, landed, sems):
        plan, buffers = spreads[number]
        half_tiles = plan.tiles // 2

        def load(i):
            return pltpu.make_async_copy(buffers[1].at[i], landed, sems.at[0])

        def store(i):
            return pltpu.make_async_copy(
                tile.at[lax.rem(i, 2)], buffers[0].at[i], sems.at[1 + lax.rem(i, 2)]
            )

        @pl.loop(0, half_tiles)
        def _(i):
            spread_copy(
                number, 0, 0, tile.at[0], buffers[1].at[i], i, 0
            ).wait_recv()
            load(i).start()

            @pl.when(i >= 2)
            def _():
                store(i - 2).wait()

            compute(owner(2 * i), tile.at[lax.rem(i, 2)])
            load(i).wait()
            tile.at[lax.rem(i, 2)][...] += landed[...]
            store(i).start()

        for i in (half_tiles - 2, half_tiles - 1):
            store(i).wait()
        for side in range(2):
            for copy in stage_copies(number, 1, side):
                copy.start()

    def combine(number, stage, side):
        plan, buffers = spreads[number]
        keep, landing = buffers[0], buffers[1 + stage]
        rows = side_rows(plan, side)

        def run(mine, other, sems):
            for copy in stage_copies(number, stage, side):
                copy.wait_recv()
            for mask in plan.masks(side, stage + 1):
                place = plan.place(mask, side, stage)
                load_mine = pltpu.make_async_copy(keep.at[mask // 2, rows], mine, sems.at[0])
                load_other = pltpu.make_async_copy(landing.at[place, rows], other, sems.at[1])
                load_mine.start()
                load_other.start()
                load_mine.wait()
                load_other.wait()
                mine[...] += other[...]
                store = pltpu.make_async_copy(mine, keep.at[mask // 2, rows], sems.at[2])
                store.start()
                store.wait()
            for copy in stage_copies(number, stage + 1, side):
                copy.start()

        shape = (plan.rows // 2, plan.cols)
        pl.run_scoped(
            run, pltpu.VMEM(shape, F32), pltpu.VMEM(shape, F32), pltpu.SemaphoreType.DMA((3,))
        )

    def end_spread(number):
        plan, _ = spreads[number]
        for side in range(2):
            for copy in stage_copies(number, bits - 1, side):
                copy.wait_recv()
            for stage in range(1, bits):
                for copy in stage_copies(number, stage, side):
                    copy.wait_send()


    def vector_copy(place, device_id):
        return pltpu.make_async_remote_copy(
            src_ref=vectors,
            dst_ref=vectors_in.at[place],
            send_sem=vec_send.at[place],
            recv_sem=vec_recv.at[place],
            device_id=device_id,
            device_id_type=MESH,
        )

    def sum_vectors_dp(bit):
        copy = vector_copy(bit, {"dp": partner(bit)})
        copy.start()
        copy.wait()
        vectors[...] += vectors_in[bit]

    def sum_vectors_mp():
        norms = pl.ds(0, 4)
        for hop in range(half - 1):
            copy = vector_copy(bits, {"mp": inner})

            @pl.when(level == hop)
            def _():
                copy.start()
                copy.wait_send()

            @pl.when(level == hop + 1)
            def _():
                copy.wait_recv()
                vectors[norms] += vectors_in[bits, norms]

        across = vector_copy(bits + 1, {"mp": inner})

        @pl.when(is_middle)
        def _():
            across.start()
            across.wait()
            vectors[norms] += vectors_in[bits + 1, norms]

        for hop in reversed(range(half - 1)):
            copy = vector_copy(bits + 2, {"mp": outer})

            @pl.when(level == hop + 1)
            def _():
                copy.start()
                copy.wait_send()

            @pl.when(level == hop)
            def _():
                copy.wait_recv()
                vectors[norms] = vectors_in[bits + 2, norms]


    first_lanes = lax.broadcasted_iota(jnp.int32, (CHUNK, LANES), 1)

    def swap_halves(x):
        return jnp.where(
            first_lanes < ROT // 2,
            pltpu.roll(x, LANES - ROT // 2, 1),
            pltpu.roll(x, ROT // 2, 1),
        )

    def turn(x, rows, sign):
        low = x[:, :LANES]
        low = low * cosine[rows] + sign * swap_halves(low) * sine[rows]
        return jnp.concatenate([low, x[:, LANES:]], axis=1)

    def store_part(c, part, sem):
        copy = pltpu.make_async_copy(part, parts.at[span(c * CHUNK, CHUNK)], sem)
        copy.start()
        copy.wait()

    def forward(
        qkv,
        up,
        load_up,
        load_qkv,
        down,
        dense,
        keys,
        values,
        key_grad,
        value_grad,
        token_chunk,
        cot_chunk,
        attn_chunk,
        mlp_chunk,
        hidden_chunk,
        hidden_grad_chunk,
        part,
        probs,
        queries,
        attended_chunk,
        attended_grad,
        w_sems,
        in_sems,
        out_chunk_sems,
        part_sem,
    ):
        load_down = pltpu.make_async_copy(down_weight, down, w_sems.at[0])
        load_dense = pltpu.make_async_copy(dense_weight, dense, w_sems.at[1])
        tile = min(512, inner_width)
        wide = min(512, width)

        def load_tokens(c):
            return pltpu.make_async_copy(
                tokens.at[span(c * CHUNK, CHUNK)], token_chunk, in_sems.at[0]
            )

        def load_cot(c):
            return pltpu.make_async_copy(
                cotangent.at[span(c * CHUNK, CHUNK)],
                cot_chunk.at[lax.rem(c, 2)],
                in_sems.at[1 + lax.rem(c, 2)],
            )

        def chunk_stores(c):
            pairs = (
                (attn_chunk, attn_entry),
                (mlp_chunk, mlp_entry),
                (attended_chunk, attended),
                (hidden_chunk, hidden),
                (hidden_grad_chunk, hidden_grad),
            )
            return [
                pltpu.make_async_copy(
                    source, target.at[span(c * CHUNK, CHUNK)], out_chunk_sems.at[i]
                )
                for i, (source, target) in enumerate(pairs)
            ]

        load_tokens(0).start()
        load_qkv.start()
        load_up.start()
        load_dense.start()
        load_cot(0).start()
        load_down.start()
        keys[...] = jnp.zeros_like(keys)
        values[...] = jnp.zeros_like(values)
        key_grad[...] = jnp.zeros_like(key_grad)
        value_grad[...] = jnp.zeros_like(value_grad)
        vectors[...] = jnp.zeros_like(vectors)

        @pl.loop(0, steps)
        def _(c):
            rows = span(c * CHUNK, CHUNK)
            cot = cot_chunk.at[lax.rem(c, 2)]
            load_tokens(c).wait()

            @pl.when(c > 0)
            def _():
                for copy in chunk_stores(c - 1):
                    copy.wait()

            @pl.loop(0, CHUNK // BLOCK)
            def _(b):
                block = span(b * BLOCK, BLOCK)
                hat, _ = normalize(token_chunk[block].astype(F32))
                attn_chunk[block] = (hat * attn_gain[...] + attn_shift[...]).astype(BF16)
                mlp_chunk[block] = (hat * mlp_gain[...] + mlp_shift[...]).astype(BF16)

            @pl.when(c + 1 < steps)
            def _():
                load_tokens(c + 1).start()
                load_cot(c + 1).start()

            @pl.when(c == 0)
            def _():
                load_qkv.wait()

            for h in range(local_heads):
                cols = slice(h * HEAD_DIM, (h + 1) * HEAD_DIM)
                base = h * 3 * HEAD_DIM

                def joined(i):
                    there = slice(base + i * HEAD_DIM, base + (i + 1) * HEAD_DIM)
                    return dot(attn_chunk[...], qkv[:, there]) + qkv_bias[:, there]

                queries[:, cols] = turn(joined(0), rows, 1.0).astype(BF16)
                keys[rows, cols] = turn(joined(1), rows, 1.0).astype(BF16)
                values[rows, cols] = joined(2).astype(BF16)

            place = lax.broadcasted_iota(jnp.int32, (CHUNK, count), 1)
            here = lax.broadcasted_iota(jnp.int32, (CHUNK, count), 0) + c * CHUNK
            allowed = (place >= start[rows, :1]) & (place <= here)
            for h in range(local_heads):
                cols = slice(h * HEAD_DIM, (h + 1) * HEAD_DIM)
                scores = dot_cols(queries[:, cols], keys[:, cols]) * scale
                scores = jnp.where(allowed, scores, -1e30)
                expo = jnp.exp(scores - jnp.max(scores, axis=-1, keepdims=True))
                prob = expo * (1.0 / jnp.sum(expo, axis=-1, keepdims=True))
                probs[h] = prob
                attended_chunk[:, cols] = dot(prob.astype(BF16), values[:, cols]).astype(BF16)

            @pl.when(c == 0)
            def _():
                load_up.wait()
                load_down.wait()

            load_cot(c).wait()

            @pl.loop(0, inner_width // tile)
            def _(t):
                cols = span(t * tile, tile)
                pre = dot(mlp_chunk[...], up[:, cols]) + up_bias[:, cols]
                value, slope = gelu_parts(pre)
                hidden_chunk[:, cols] = value.astype(BF16)
                grad = (slope * dot_cols(cot[...], down[cols, :])).astype(BF16)
                hidden_grad_chunk[:, cols] = grad
                vectors[UP_BIAS : UP_BIAS + 1, cols] += column_sum(grad.astype(F32))

            @pl.when(c == 0)
            def _():
                load_dense.wait()

            @pl.loop(0, width // wide)
            def _(t):
                cols = span(t * wide, wide)
                part[:, cols] = dot(hidden_chunk[...], down[:, cols]) + dot(
                    attended_chunk[...], dense[:, cols]
                )

            store_part(c, part, part_sem.at[0])

            @pl.when(c == 0)
            def _():
                begin_messages()

            for copy in chunk_stores(c):
                copy.start()

            service(2 * c)

            attended_grad[...] = dot_cols(cot[...], dense[...]).astype(BF16)
            for h in range(local_heads):
                cols = slice(h * HEAD_DIM, (h + 1) * HEAD_DIM)
                base = h * 3 * HEAD_DIM
                grad = attended_grad[:, cols]
                prob = probs[h]
                prob_grad = dot_cols(grad, values[:, cols])
                along = jnp.sum(prob * prob_grad, axis=-1, keepdims=True)
                score_grad = (prob * (prob_grad - along)).astype(BF16)
                query_grad = dot(score_grad, keys[:, cols]) * scale
                joined_grad[rows, base : base + HEAD_DIM] = turn(query_grad, rows, -1.0).astype(
                    BF16
                )
                key_grad[:, cols] += dot_rows(score_grad, queries[:, cols]) * scale
                value_grad[:, cols] += dot_rows(prob.astype(BF16), grad)

            @pl.loop(0, CHUNK // BLOCK)
            def _(b):
                block = span(b * BLOCK, BLOCK)
                vectors[OUT_BIAS : OUT_BIAS + 1, :width] += column_sum(cot[block].astype(F32))

            service(2 * c + 1)

        for copy in chunk_stores(steps - 1):
            copy.wait()

        @pl.loop(0, steps)
        def _(c):
            rows = span(c * CHUNK, CHUNK)
            for h in range(local_heads):
                cols = slice(h * HEAD_DIM, (h + 1) * HEAD_DIM)
                base = h * 3 * HEAD_DIM
                joined_grad[rows, base + HEAD_DIM : base + 2 * HEAD_DIM] = turn(
                    key_grad[rows, cols], rows, -1.0
                ).astype(BF16)
                joined_grad[rows, base + 2 * HEAD_DIM : base + 3 * HEAD_DIM] = value_grad[
                    rows, cols
                ].astype(BF16)

    def backward(qkv, up, grad_chunk, token_chunk, hat, part, in_sems, part_sem, first_slot):
        wide = min(512, width)

        def loads(c):
            rows = span(c * CHUNK, CHUNK)
            return [
                pltpu.make_async_copy(
                    hidden_grad.at[rows], grad_chunk.at[lax.rem(c, 2)], in_sems.at[lax.rem(c, 2), 0]
                ),
                pltpu.make_async_copy(
                    tokens.at[rows], token_chunk.at[lax.rem(c, 2)], in_sems.at[lax.rem(c, 2), 1]
                ),
            ]

        for copy in loads(0):
            copy.start()

        @pl.loop(0, steps)
        def _(c):
            rows = span(c * CHUNK, CHUNK)
            for copy in loads(c):
                copy.wait()

            @pl.when(c + 1 < steps)
            def _():
                for copy in loads(c + 1):
                    copy.start()

            @pl.loop(0, CHUNK // BLOCK)
            def _(b):
                block = span(b * BLOCK, BLOCK)
                hat[block] = normalize(token_chunk[lax.rem(c, 2), block].astype(F32))[0]

            vectors[QKV_BIAS : QKV_BIAS + 1, : 3 * heads_width] += column_sum(
                joined_grad[rows].astype(F32)
            )

            @pl.loop(0, width // wide)
            def _(t):
                cols = span(t * wide, wide)
                attn_grad = dot_cols(joined_grad[rows], qkv[cols, :])
                mlp_grad = dot_cols(grad_chunk[lax.rem(c, 2)], up[cols, :])
                part[:, cols] = attn_grad * attn_gain[:, cols] + mlp_grad * mlp_gain[:, cols]
                near = hat[:, cols]
                for row, value in (
                    (ATTN_GAIN, attn_grad * near),
                    (ATTN_SHIFT, attn_grad),
                    (MLP_GAIN, mlp_grad * near),
                    (MLP_SHIFT, mlp_grad),
                ):
                    vectors[row : row + 1, cols] += column_sum(value)

            store_part(steps + c, part, part_sem.at[0])
            service(first_slot + c)

    def fill(source, target, sem):
        return pltpu.make_async_copy(source, target, sem)

    def spread_columns(number, left_source, first_slot, split):
        plan, _ = spreads[number]
        depth = left_source.shape[1]

        def run(left, turned, right, tile, landed, sems):
            loads = [fill(left_source, left, sems.at[0]), fill(cotangent, right, sems.at[1])]
            for copy in loads:
                copy.start()
            for copy in loads:
                copy.wait()

            @pl.loop(0, depth // HEAD_DIM)
            def _(b):
                there = span(b * HEAD_DIM, HEAD_DIM)
                turned[there, :] = left[:, there].T

            def compute(where, target):
                right_cols = right[:, span(where * plan.cols, plan.cols)]
                block = min(512, depth)

                @pl.loop(0, depth // block)
                def _(b):
                    there = span(b * block, block)
                    target[there, :] = dot(turned[there, :], right_cols)

            tiles_out(number, compute, tile, sems)
            if split:
                service(first_slot)
            tiles_kept(number, compute, tile, landed, sems)
            service(first_slot + split)

        pl.run_scoped(
            run,
            pltpu.VMEM((count, depth), BF16),
            pltpu.VMEM((depth, count), BF16),
            pltpu.VMEM((count, width), BF16),
            pltpu.VMEM((2, plan.rows, plan.cols), F32),
            pltpu.VMEM((plan.rows, plan.cols), F32),
            pltpu.SemaphoreType.DMA((3,)),
        )

    def spread_rows(number, left_source, right_source, first_slot, split):
        plan, _ = spreads[number]

        def run(left, right, tile, landed, sems):
            loads = [fill(left_source, left, sems.at[0])]
            if right_source is not joined_grad:
                loads.append(fill(right_source, right, sems.at[1]))
            for copy in loads:
                copy.start()
            for copy in loads:
                copy.wait()
            use = joined_grad if right_source is joined_grad else right

            def compute(where, target):
                turned = left[:, span(where * plan.rows, plan.rows)].T
                block = min(512, plan.cols)

                @pl.loop(0, plan.cols // block)
                def _(b):
                    there = span(b * block, block)
                    target[:, there] = dot(turned, use[:, there])

            tiles_out(number, compute, tile, sems)
            if split:
                service(first_slot)
            tiles_kept(number, compute, tile, landed, sems)
            service(first_slot + split)

        right_shape = (16, LANES) if right_source is joined_grad else (count, plan.cols)
        pl.run_scoped(
            run,
            pltpu.VMEM((count, width), BF16),
            pltpu.VMEM(right_shape, BF16),
            pltpu.VMEM((2, plan.rows, plan.cols), F32),
            pltpu.VMEM((plan.rows, plan.cols), F32),
            pltpu.SemaphoreType.DMA((3,)),
        )

    QKV, DENSE, UP, DOWN = range(4)
    slots = [2 * steps]

    def take_slots(number):
        slots[0] += number
        return slots[0] - number

    def with_weights(qkv, up, w_sems):
        load_qkv = pltpu.make_async_copy(qkv_weight, qkv, w_sems.at[0])
        load_up = pltpu.make_async_copy(up_weight, up, w_sems.at[1])
        pl.run_scoped(
            functools.partial(forward, qkv, up, load_up, load_qkv),
            pltpu.VMEM(down_weight.shape, BF16),
            pltpu.VMEM(dense_weight.shape, BF16),
            pltpu.VMEM((count, heads_width), BF16),
            pltpu.VMEM((count, heads_width), BF16),
            pltpu.VMEM((count, heads_width), F32),
            pltpu.VMEM((count, heads_width), F32),
            pltpu.VMEM((CHUNK, width), BF16),
            pltpu.VMEM((2, CHUNK, width), BF16),
            pltpu.VMEM((CHUNK, width), BF16),
            pltpu.VMEM((CHUNK, width), BF16),
            pltpu.VMEM((CHUNK, inner_width), BF16),
            pltpu.VMEM((CHUNK, inner_width), BF16),
            pltpu.VMEM((CHUNK, width), F32),
            pltpu.VMEM((local_heads, CHUNK, count), F32),
            pltpu.VMEM((CHUNK, heads_width), BF16),
            pltpu.VMEM((CHUNK, heads_width), BF16),
            pltpu.VMEM((CHUNK, heads_width), BF16),
            pltpu.SemaphoreType.DMA((2,)),
            pltpu.SemaphoreType.DMA((3,)),
            pltpu.SemaphoreType.DMA((5,)),
            pltpu.SemaphoreType.DMA((1,)),
        )
        spread_columns(DOWN, hidden, take_slots(2), 1)
        spread_columns(DENSE, attended, take_slots(1), 0)
        first = take_slots(steps)
        pl.run_scoped(
            lambda *scratch: backward(qkv, up, *scratch, first),
            pltpu.VMEM((2, CHUNK, inner_width), BF16),
            pltpu.VMEM((2, CHUNK, width), BF16),
            pltpu.VMEM((CHUNK, width), F32),
            pltpu.VMEM((CHUNK, width), F32),
            pltpu.SemaphoreType.DMA((2, 2)),
            pltpu.SemaphoreType.DMA((1,)),
        )

    pl.run_scoped(
        with_weights,
        pltpu.VMEM(qkv_weight.shape, BF16),
        pltpu.VMEM(up_weight.shape, BF16),
        pltpu.SemaphoreType.DMA((2,)),
    )
    spread_rows(UP, mlp_entry, hidden_grad, take_slots(2), 1)
    spread_rows(QKV, attn_entry, joined_grad, take_slots(2), 1)
    for stage in range(1, bits - 1):
        for number in (DOWN, DENSE, UP, QKV):
            for side in range(2):
                combine(number, stage, side)
                if number != DENSE or side:
                    service(take_slots(1))
    for bit in range(bits):
        sum_vectors_dp(bit)
    service(take_slots(1))
    sum_vectors_mp()

    @pl.loop(slots[0], messages + half)
    def _(j):
        service(j)

    end_messages()
    for number in (DOWN, DENSE, UP, QKV):
        end_spread(number)
    store_vectors = fill(vectors, vectors_out, vec_send.at[0])
    store_vectors.start()
    store_vectors.wait()


def layer_call(mp_size, dp_size, operands):
    tokens, qkv, dense, up, down = (operands[i] for i in (0, 2, 3, 4, 5))
    count, width = tokens.shape
    inner_width, heads_width = up.shape[1], dense.shape[0]
    messages = 2 * (count // ROWS)
    bits = dp_size.bit_length() - 1
    owned = width // dp_size
    plans = (
        Spread(bits, owned, qkv.shape[1]),
        Spread(bits, heads_width, owned),
        Spread(bits, owned, inner_width),
        Spread(bits, inner_width, owned),
    )
    vector_width = max(width, inner_width, qkv.shape[1])
    anywhere = pl.BlockSpec(memory_space=pl.ANY)
    vmem = pl.BlockSpec(memory_space=pltpu.VMEM)
    shape = jax.ShapeDtypeStruct
    out_shape = [
        shape((count, width), BF16),
        shape((count, width), BF16),
        shape((VECTORS, vector_width), F32),
        shape((2 * count, width), F32),
        shape((count, width), BF16),
        shape((count, width), BF16),
        shape((count, heads_width), BF16),
        shape((count, inner_width), BF16),
        shape((count, inner_width), BF16),
    ]
    for plan in plans:
        out_shape += [shape(dims, F32) for dims in plan.shapes()]
    dma = pltpu.SemaphoreType.DMA
    scratch = [
        pltpu.VMEM((SLOTS, ROWS, width), F32),
        pltpu.VMEM((SLOTS, ROWS, width), F32),
        pltpu.VMEM((SLOTS, ROWS, width), F32),
        pltpu.VMEM((2, ROWS, width), BF16),
        pltpu.VMEM((2, ROWS, width), BF16),
        pltpu.VMEM((2, ROWS, width), BF16),
        pltpu.VMEM((VECTORS, vector_width), F32),
        pltpu.VMEM((bits + 3, VECTORS, vector_width), F32),
        pltpu.VMEM((count, qkv.shape[1]), BF16),
        dma((messages,)),
        dma((messages,)),
        dma((messages,)),
        dma((messages,)),
        dma((2,)),
        dma((2, 2)),
        dma((2,)),
        dma((bits + 3,)),
        dma((bits + 3,)),
    ]
    for plan in plans:
        scratch += [dma((plan.sems,)), dma((plan.sems,))]
    results = pl.pallas_call(
        functools.partial(layer_kernel, mp_size, plans),
        out_shape=tuple(out_shape),
        in_specs=[anywhere] * 6 + [vmem] * 10,
        out_specs=(anywhere,) * len(out_shape),
        scratch_shapes=scratch,
        compiler_params=pltpu.CompilerParams(
            collective_id=0, has_side_effects=True, vmem_limit_bytes=62 * 1024 * 1024
        ),
        cost_estimate=pl.CostEstimate(
            flops=6 * count * (width * (qkv.shape[1] + 2 * inner_width + heads_width)),
            bytes_accessed=300 << 20,
            transcendentals=0,
        ),
    )(*operands)
    layer_output, input_grad, vectors = results[:3]
    spread = list(results[9:])
    grads = []
    for plan in plans:
        buffers, spread = spread[: 1 + bits], spread[1 + bits :]
        grads.append(buffers[0][0] + buffers[bits][0])
    return layer_output, input_grad, vectors, grads


def per_device(
    mp_size,
    dp_size,
    tokens,
    lengths,
    attn_gain,
    attn_shift,
    mlp_gain,
    mlp_shift,
    qkv_weight,
    qkv_bias,
    dense_weight,
    up_weight,
    up_bias,
    down_weight,
    out_bias,
    cotangent,
):
    count, width = tokens.shape
    start = layout(lengths[0], count)
    cosine, sine = rotary_tables(start, count)
    start = jnp.broadcast_to(start[:, None], (count, LANES))
    layer_output, input_grad, vectors, grads = layer_call(
        mp_size,
        dp_size,
        (
            tokens,
            cotangent,
            qkv_weight,
            dense_weight,
            up_weight,
            down_weight,
            attn_gain[None],
            attn_shift[None],
            mlp_gain[None],
            mlp_shift[None],
            qkv_bias[None],
            up_bias[None],
            out_bias[None],
            cosine,
            sine,
            start,
        ),
    )
    qkv_grad, dense_grad, up_grad, down_grad = grads
    me = lax.axis_index("dp")

    def owned(row, total):
        return lax.dynamic_slice_in_dim(vectors[row], me * (total // dp_size), total // dp_size)

    return (
        layer_output,
        input_grad,
        owned(ATTN_GAIN, width),
        owned(ATTN_SHIFT, width),
        owned(MLP_GAIN, width),
        owned(MLP_SHIFT, width),
        qkv_grad,
        owned(QKV_BIAS, qkv_weight.shape[1]),
        dense_grad,
        up_grad,
        owned(UP_BIAS, up_weight.shape[1]),
        down_grad,
        owned(OUT_BIAS, width),
    )


def solution(mesh):
    in_specs = (
        P("dp", None),
        P("dp", None),
        P(),
        P(),
        P(),
        P(),
        P(None, "mp"),
        P("mp"),
        P("mp", None),
        P(None, "mp"),
        P("mp"),
        P("mp", None),
        P(),
        P("dp", None),
    )
    out_specs = (
        P("dp", None),
        P("dp", None),
        P("dp"),
        P("dp"),
        P("dp"),
        P("dp"),
        P("dp", "mp"),
        P(("mp", "dp")),
        P("mp", "dp"),
        P("dp", "mp"),
        P(("mp", "dp")),
        P("mp", "dp"),
        P("dp"),
    )
    function = functools.partial(per_device, mesh.shape["mp"], mesh.shape["dp"])
    return jax.shard_map(
        function, mesh=mesh, in_specs=in_specs, out_specs=out_specs, check_vma=False
    )
```

```python
import functools
import math

import jax
import jax.numpy as jnp
from jax import lax
from jax.experimental import pallas as pl
from jax.experimental.pallas import tpu as pltpu
from jax.sharding import PartitionSpec as P

HEAD_DIM = 256
ROT = 64
EPSILON = 1e-05
LANES = 128

MESH = pl.DeviceIdType.MESH
ROWS = 64
SLOTS = 6
AHEAD = 2
CHUNK = 256
BLOCK = 32

F32 = jnp.float32
BF16 = jnp.bfloat16

VECTORS = 8
ATTN_GAIN, ATTN_SHIFT, MLP_GAIN, MLP_SHIFT, OUT_BIAS, UP_BIAS, QKV_BIAS = range(7)


def sine_cosine(angle):
    turns = jnp.floor(angle * (2.0 / math.pi) + 0.5)
    rest = angle - turns * 1.5703125 - turns * 4.837512969970703e-4 - turns * 7.549789954891882e-8
    square = rest * rest
    sine = rest + rest * square * (
        -1.6666654611e-1 + square * (8.3321608736e-3 - square * 1.9515295891e-4)
    )
    cosine = (
        1.0
        - 0.5 * square
        + square
        * square
        * (4.166664568298827e-2 + square * (-1.388731625493765e-3 + square * 2.443315711809948e-5))
    )
    quarter = turns - 4.0 * jnp.floor(turns * 0.25)
    odd = (quarter == 1.0) | (quarter == 3.0)
    flip_sine = quarter >= 2.0
    flip_cosine = (quarter == 1.0) | (quarter == 2.0)
    near_sine = jnp.where(odd, cosine, sine)
    near_cosine = jnp.where(odd, sine, cosine)
    return (
        jnp.where(flip_sine, -near_sine, near_sine),
        jnp.where(flip_cosine, -near_cosine, near_cosine),
    )


def rotary_tables(place, start):
    lane = lax.broadcasted_iota(jnp.int32, place.shape, 1)
    half = ROT // 2
    step = jnp.where(lane < half, lane, lane - half).astype(F32)
    freqs = jnp.exp(step * (-2.0 * math.log(10000.0) / ROT))
    sine, cosine = sine_cosine((place - start).astype(F32) * freqs)
    cosine = jnp.where(lane < ROT, cosine, 1.0)
    sine = jnp.where(lane < half, -sine, jnp.where(lane < ROT, sine, 0.0))
    return cosine, sine


def normalize(rows):
    centred = rows - jnp.mean(rows, axis=-1, keepdims=True)
    factor = lax.rsqrt(jnp.mean(centred * centred, axis=-1, keepdims=True) + EPSILON)
    return centred * factor, factor


def gelu_parts(v):
    cdf = 0.5 + 0.5 * lax.erf(v * math.sqrt(0.5))
    return v * cdf, cdf + v * jnp.exp(-0.5 * v * v) * (1.0 / math.sqrt(2.0 * math.pi))


def dot(left, right):
    return jnp.dot(left, right, preferred_element_type=F32)


def dot_cols(left, right):
    return lax.dot_general(left, right, (((1,), (1,)), ((), ())), preferred_element_type=F32)


def dot_rows(left, right):
    return lax.dot_general(left, right, (((0,), (0,)), ((), ())), preferred_element_type=F32)


def column_sum(x):
    return jnp.sum(x, axis=0, keepdims=True)


def span(start, size):
    return pl.ds(pl.multiple_of(start, size), size)


class Spread:
    def __init__(self, bits, rows, cols):
        self.bits, self.rows, self.cols = bits, rows, cols
        self.tiles = 1 << bits
        self.orders = ([0] + list(range(1, bits)), [0] + list(range(bits - 1, 0, -1)))
        count = self.tiles // 2
        self.first = {}
        for stage in range(1, bits):
            for side in range(2):
                self.first[stage, side] = count
                count += self.tiles >> (stage + 1)
        self.sems = count

    def masks(self, side, stage):
        order = self.orders[side]
        return [m for m in range(self.tiles) if not any((m >> b) & 1 for b in order[:stage])]

    def place(self, mask, side, stage):
        return self.masks(side, stage + 1).index(mask)

    def shapes(self):
        shapes = [(self.tiles // 2, self.rows, self.cols)]
        for stage in range(self.bits):
            shapes.append((self.tiles >> (stage + 1), self.rows, self.cols))
        return shapes


def layer_kernel(mp_size, plans, *refs):
    refs = list(refs)

    def take(number):
        taken = refs[:number]
        del refs[:number]
        return taken

    tokens, cotangent, qkv_weight, dense_weight, up_weight, down_weight = take(6)
    attn_gain, attn_shift, mlp_gain, mlp_shift, qkv_bias, up_bias, out_bias = take(7)
    lengths = take(1)[0]
    layer_out, input_grad, vectors_out, parts = take(4)
    grads_out = take(len(plans))
    attn_entry, mlp_entry, attended, hidden, hidden_grad = take(5)
    spreads = [(plan, take(1 + plan.bits)) for plan in plans]
    from_outer, from_inner, sums, token_rows, cot_rows, out_rows = take(6)
    vectors, vectors_in, joined_grad, cosine, sine = take(5)
    send_in, send_out, recv_outer, recv_inner, part_sems, row_sems, out_sems = take(7)
    vec_send, vec_recv = take(2)
    spread_sems = [take(2) for _ in plans]

    count, width = tokens.shape
    inner_width = up_weight.shape[1]
    heads_width = dense_weight.shape[0]
    local_heads = heads_width // HEAD_DIM
    bits = plans[0].bits
    steps = count // CHUNK
    scale = 1.0 / math.sqrt(HEAD_DIM)
    branch_messages = count // ROWS
    messages = 2 * branch_messages
    chunk_messages = CHUNK // ROWS
    half = mp_size // 2

    index = lax.axis_index("mp")
    upper = index // half
    level = index * (1 - upper) + (mp_size - 1 - index) * upper
    inner = index + 1 - 2 * upper
    outer = index - 1 + 2 * upper
    lag = half - level
    ahead = min(AHEAD, SLOTS - 1 - half)
    is_middle = level == half - 1
    device = lax.axis_index("dp")

    def partner(bit):
        return device + (1 - 2 * ((device // (1 << bit)) % 2)) * (1 << bit)

    def owner(mask):
        total = 0
        for bit in range(bits):
            total = total + ((device // (1 << bit) + mask // (1 << bit)) % 2) * (1 << bit)
        return total

    barrier = pltpu.get_barrier_semaphore()
    pl.semaphore_signal(barrier, inc=1, device_id={"mp": inner}, device_id_type=MESH)
    for bit in range(bits):
        pl.semaphore_signal(barrier, inc=1, device_id={"dp": partner(bit)}, device_id_type=MESH)
    if half > 1:

        @pl.when(level > 0)
        def _():
            pl.semaphore_signal(barrier, inc=1, device_id={"mp": outer}, device_id_type=MESH)
            pl.semaphore_wait(barrier, 2 + bits)

        @pl.when(level == 0)
        def _():
            pl.semaphore_wait(barrier, 1 + bits)

    else:
        pl.semaphore_wait(barrier, 1 + bits)


    def slot(ref, k):
        return ref.at[lax.rem(k, SLOTS)]

    def message(ref, k):
        return ref.at[span(k * ROWS, ROWS)]

    def to_inner(k, source, landing, sem):
        return pltpu.make_async_remote_copy(
            src_ref=source,
            dst_ref=slot(landing, k),
            send_sem=send_in.at[k],
            recv_sem=sem.at[k],
            device_id={"mp": inner},
            device_id_type=MESH,
        )

    def to_outer(k, source):
        return pltpu.make_async_remote_copy(
            src_ref=slot(source, k),
            dst_ref=slot(from_inner, k),
            send_sem=send_out.at[k],
            recv_sem=recv_inner.at[k],
            device_id={"mp": outer},
            device_id_type=MESH,
        )

    def load_part(k):
        return pltpu.make_async_copy(message(parts, k), slot(sums, k), part_sems.at[lax.rem(k, 2)])

    def load_rows(k):
        row, place = lax.rem(k, branch_messages), lax.rem(k, 2)
        return [
            pltpu.make_async_copy(
                message(tokens, row), token_rows.at[place], row_sems.at[0, place]
            ),
            pltpu.make_async_copy(
                message(cotangent, row), cot_rows.at[place], row_sems.at[1, place]
            ),
        ]

    def store_rows(k, target):
        place = lax.rem(k, 2)
        return pltpu.make_async_copy(
            out_rows.at[place], message(target, lax.rem(k, branch_messages)), out_sems.at[place]
        )

    def send_ahead(k):
        if half > 1:

            @pl.when((level == 0) & (k < messages))
            def _():
                to_inner(k, message(parts, k), from_outer, recv_outer).start()

    def begin_messages():
        for k in range(ahead):
            send_ahead(k)
        for copy in load_rows(0):
            copy.start()
        if half > 1:

            @pl.when(level > 0)
            def _():
                load_part(0).start()

        else:
            load_part(0).start()

    def add_inward(j):
        @pl.when(j < messages)
        def _():
            load_part(j).wait()

            @pl.when(j + 1 < messages)
            def _():
                load_part(j + 1).start()

            mine = slot(sums, j)
            if half > 1:
                to_inner(j, mine, from_outer, recv_outer).wait_recv()
                mine[...] += slot(from_outer, j)[...]

            @pl.when(is_middle)
            def _():
                to_inner(j, mine, from_inner, recv_inner).start()

            if half > 2:

                @pl.when(level < half - 1)
                def _():
                    to_inner(j, mine, from_outer, recv_outer).start()

    def finish(k, source):
        place = lax.rem(k, 2)

        @pl.when(k < branch_messages)
        def _():
            @pl.loop(0, ROWS // BLOCK)
            def _(b):
                rows = span(b * BLOCK, BLOCK)
                out_rows[place, rows] = (
                    token_rows[place, rows].astype(F32) + source[rows] + out_bias[...]
                ).astype(BF16)

        @pl.when(k >= branch_messages)
        def _():
            @pl.loop(0, ROWS // BLOCK)
            def _(b):
                rows = span(b * BLOCK, BLOCK)
                hat, factor = normalize(token_rows[place, rows].astype(F32))
                entry = source[rows]
                part = (
                    entry
                    - jnp.mean(entry, axis=-1, keepdims=True)
                    - hat * jnp.mean(entry * hat, axis=-1, keepdims=True)
                )
                out_rows[place, rows] = (
                    cot_rows[place, rows].astype(F32) + factor * part
                ).astype(BF16)

    def pass_outward(k):
        @pl.when((k >= 0) & (k < messages))
        def _():
            landed = slot(from_inner, k)
            total = slot(sums, k)
            to_outer(k, sums).wait_recv()
            to_inner(k, total, from_inner, recv_inner).wait_send()

            @pl.when(is_middle)
            def _():
                total[...] += landed[...]

            if half > 1:

                @pl.when(level > 0)
                def _():
                    @pl.when(k >= 1)
                    def _():
                        to_outer(k - 1, sums).wait_send()

                    @pl.when(is_middle)
                    def _():
                        to_outer(k, sums).start()

                    if half > 2:

                        @pl.when(level < half - 1)
                        def _():
                            to_outer(k, from_inner).start()

            @pl.when(k + 1 < messages)
            def _():
                for copy in load_rows(k + 1):
                    copy.start()

            for copy in load_rows(k):
                copy.wait()

            @pl.when(k >= 2)
            def _():
                store_rows(k - 2, layer_out).wait()

            @pl.when(is_middle)
            def _():
                finish(k, total)

            if half > 1:

                @pl.when(level < half - 1)
                def _():
                    finish(k, landed)

            @pl.when(k < branch_messages)
            def _():
                store_rows(k, layer_out).start()

            @pl.when(k >= branch_messages)
            def _():
                store_rows(k, input_grad).start()

    def service(j):
        send_ahead(j + ahead)
        if half > 1:

            @pl.when(level > 0)
            def _():
                add_inward(j)

        else:
            add_inward(j)
        pass_outward(j - lag)

    def end_messages():
        if half > 1:

            @pl.when(level > 0)
            def _():
                to_outer(messages - 1, sums).wait_send()

        for k in (messages - 2, messages - 1):
            store_rows(k, input_grad).wait()


    def spread_copy(number, stage, side, source, target, sem, bit):
        sends, recvs = spread_sems[number]
        return pltpu.make_async_remote_copy(
            src_ref=source,
            dst_ref=target,
            send_sem=sends.at[sem],
            recv_sem=recvs.at[sem],
            device_id={"dp": partner(bit)},
            device_id_type=MESH,
        )

    def side_rows(plan, side):
        return pl.ds(side * (plan.rows // 2), plan.rows // 2)

    def stage_copies(number, stage, side):
        plan, buffers = spreads[number]
        keep, landing = buffers[0], buffers[1 + stage]
        bit = plan.orders[side][stage]
        copies = []
        for mask in plan.masks(side, stage):
            if (mask >> bit) & 1:
                place = plan.place(mask ^ (1 << bit), side, stage)
                copies.append(
                    spread_copy(
                        number,
                        stage,
                        side,
                        keep.at[mask // 2, side_rows(plan, side)],
                        landing.at[place, side_rows(plan, side)],
                        plan.first[stage, side] + place,
                        bit,
                    )
                )
        return copies

    def tiles_out(number, compute, tile, sems):
        plan, buffers = spreads[number]
        half_tiles = plan.tiles // 2

        def copy(i):
            return spread_copy(
                number, 0, 0, tile.at[lax.rem(i, 2)], buffers[1].at[i], i, 0
            )

        @pl.loop(0, half_tiles)
        def _(i):
            @pl.when(i >= 2)
            def _():
                copy(i - 2).wait_send()

            compute(owner(2 * i + 1), tile.at[lax.rem(i, 2)])
            copy(i).start()

        for i in (half_tiles - 2, half_tiles - 1):
            copy(i).wait_send()

    def tiles_kept(number, compute, tile, landed, sems):
        plan, buffers = spreads[number]
        half_tiles = plan.tiles // 2

        def load(i):
            return pltpu.make_async_copy(buffers[1].at[i], landed, sems.at[0])

        def store(i):
            return pltpu.make_async_copy(
                tile.at[lax.rem(i, 2)], buffers[0].at[i], sems.at[1 + lax.rem(i, 2)]
            )

        @pl.loop(0, half_tiles)
        def _(i):
            spread_copy(
                number, 0, 0, tile.at[0], buffers[1].at[i], i, 0
            ).wait_recv()
            load(i).start()

            @pl.when(i >= 2)
            def _():
                store(i - 2).wait()

            compute(owner(2 * i), tile.at[lax.rem(i, 2)])
            load(i).wait()
            tile.at[lax.rem(i, 2)][...] += landed[...]
            store(i).start()

        for i in (half_tiles - 2, half_tiles - 1):
            store(i).wait()
        for side in range(2):
            for copy in stage_copies(number, 1, side):
                copy.start()

    def combine(number, stage, side):
        plan, buffers = spreads[number]
        keep, landing = buffers[0], buffers[1 + stage]
        last = stage == bits - 1
        rows = plan.rows // 4

        def run(mine, other, sems):
            for copy in stage_copies(number, stage, side):
                copy.wait_recv()
            loads, stores = [], []
            for mask in plan.masks(side, stage + 1):
                place = plan.place(mask, side, stage)
                for piece in range(2):
                    there = pl.ds(side * (plan.rows // 2) + piece * rows, rows)
                    at = len(loads) % 2
                    kept = keep.at[mask // 2, there]
                    loads.append(
                        [
                            pltpu.make_async_copy(kept, mine.at[at], sems.at[0, at]),
                            pltpu.make_async_copy(
                                landing.at[place, there], other.at[at], sems.at[1, at]
                            ),
                        ]
                    )
                    target = grads_out[number].at[there] if last else kept
                    stores.append(pltpu.make_async_copy(mine.at[at], target, sems.at[2, at]))
            for copy in loads[0]:
                copy.start()
            for i, (load, store) in enumerate(zip(loads, stores)):
                if i + 1 < len(loads):
                    if i >= 1:
                        stores[i - 1].wait()
                    for copy in loads[i + 1]:
                        copy.start()
                for copy in load:
                    copy.wait()
                mine[i % 2] += other[i % 2]
                store.start()
            for store in stores[-2:]:
                store.wait()
            if not last:
                for copy in stage_copies(number, stage + 1, side):
                    copy.start()

        shape = (2, rows, plan.cols)
        pl.run_scoped(
            run, pltpu.VMEM(shape, F32), pltpu.VMEM(shape, F32), pltpu.SemaphoreType.DMA((3, 2))
        )

    def end_spread(number):
        plan, _ = spreads[number]
        for side in range(2):
            for stage in range(1, bits):
                for copy in stage_copies(number, stage, side):
                    copy.wait_send()


    def vector_copy(place, device_id):
        return pltpu.make_async_remote_copy(
            src_ref=vectors,
            dst_ref=vectors_in.at[place],
            send_sem=vec_send.at[place],
            recv_sem=vec_recv.at[place],
            device_id=device_id,
            device_id_type=MESH,
        )

    norms = pl.ds(0, 4)

    def inward_hop(hop):
        return vector_copy(bits + hop, {"mp": inner})

    def outward_hop(hop):
        return vector_copy(bits + half + hop, {"mp": outer})

    def vector_steps():
        steps = []

        def start_inward(hop):
            @pl.when(level == hop)
            def _():
                inward_hop(hop).start()

        def end_inward(hop):
            @pl.when(level == hop)
            def _():
                inward_hop(hop).wait_send()

            if hop < half - 1:

                @pl.when(level == hop + 1)
                def _():
                    inward_hop(hop).wait_recv()
                    vectors[norms] += vectors_in[bits + hop, norms]

            else:

                @pl.when(is_middle)
                def _():
                    inward_hop(hop).wait_recv()
                    vectors[norms] += vectors_in[bits + hop, norms]

        def start_outward(hop):
            @pl.when(level == hop + 1)
            def _():
                outward_hop(hop).start()

        def end_outward(hop):
            @pl.when(level == hop + 1)
            def _():
                outward_hop(hop).wait_send()

            @pl.when(level == hop)
            def _():
                outward_hop(hop).wait_recv()
                vectors[norms] = vectors_in[bits + half + hop, norms]

        def start_across(bit):
            vector_copy(bit, {"dp": partner(bit)}).start()

        def end_across(bit):
            vector_copy(bit, {"dp": partner(bit)}).wait()
            vectors[...] += vectors_in[bit]

        moves = [
            (functools.partial(start_inward, hop), functools.partial(end_inward, hop))
            for hop in range(half)
        ]
        moves += [
            (functools.partial(start_outward, hop), functools.partial(end_outward, hop))
            for hop in reversed(range(half - 1))
        ]
        moves += [
            (functools.partial(start_across, bit), functools.partial(end_across, bit))
            for bit in range(bits)
        ]

        def step(i):
            if i > 0:
                moves[i - 1][1]()
            if i < len(moves):
                moves[i][0]()

        return [functools.partial(step, i) for i in range(len(moves) + 1)]


    first_lanes = lax.broadcasted_iota(jnp.int32, (CHUNK, LANES), 1)

    def swap_halves(x):
        return jnp.where(
            first_lanes < ROT // 2,
            pltpu.roll(x, LANES - ROT // 2, 1),
            pltpu.roll(x, ROT // 2, 1),
        )

    def turn(x, rows, sign):
        low = x[:, :LANES]
        low = low * cosine[rows] + sign * swap_halves(low) * sine[rows]
        return jnp.concatenate([low, x[:, LANES:]], axis=1)

    def store_part(c, part, sem):
        copy = pltpu.make_async_copy(part, parts.at[span(c * CHUNK, CHUNK)], sem)
        copy.start()
        copy.wait()

    def forward(
        qkv,
        up,
        load_up,
        load_qkv,
        down,
        dense,
        keys,
        values,
        key_grad,
        value_grad,
        token_chunk,
        cot_chunk,
        attn_chunk,
        mlp_chunk,
        hidden_chunk,
        hidden_grad_chunk,
        part,
        probs,
        queries,
        attended_chunk,
        attended_grad,
        w_sems,
        in_sems,
        out_chunk_sems,
        part_sem,
    ):
        load_down = pltpu.make_async_copy(down_weight, down, w_sems.at[0])
        load_dense = pltpu.make_async_copy(dense_weight, dense, w_sems.at[1])
        tile = min(512, inner_width)
        wide = min(512, width)

        def load_tokens(c):
            return pltpu.make_async_copy(
                tokens.at[span(c * CHUNK, CHUNK)], token_chunk, in_sems.at[0]
            )

        def load_cot(c):
            return pltpu.make_async_copy(
                cotangent.at[span(c * CHUNK, CHUNK)],
                cot_chunk.at[lax.rem(c, 2)],
                in_sems.at[1 + lax.rem(c, 2)],
            )

        def chunk_stores(c):
            pairs = (
                (attn_chunk, attn_entry),
                (mlp_chunk, mlp_entry),
                (attended_chunk, attended),
                (hidden_chunk, hidden),
                (hidden_grad_chunk, hidden_grad),
            )
            return [
                pltpu.make_async_copy(
                    source, target.at[span(c * CHUNK, CHUNK)], out_chunk_sems.at[i]
                )
                for i, (source, target) in enumerate(pairs)
            ]

        load_tokens(0).start()
        load_qkv.start()
        load_up.start()
        load_dense.start()
        load_cot(0).start()
        load_down.start()
        keys[...] = jnp.zeros_like(keys)
        values[...] = jnp.zeros_like(values)
        key_grad[...] = jnp.zeros_like(key_grad)
        value_grad[...] = jnp.zeros_like(value_grad)
        vectors[...] = jnp.zeros_like(vectors)

        @pl.loop(0, steps)
        def _(c):
            rows = span(c * CHUNK, CHUNK)
            cot = cot_chunk.at[lax.rem(c, 2)]
            load_tokens(c).wait()

            @pl.when(c > 0)
            def _():
                for copy in chunk_stores(c - 1):
                    copy.wait()

            @pl.loop(0, CHUNK // BLOCK)
            def _(b):
                block = span(b * BLOCK, BLOCK)
                hat, _ = normalize(token_chunk[block].astype(F32))
                attn_chunk[block] = (hat * attn_gain[...] + attn_shift[...]).astype(BF16)
                mlp_chunk[block] = (hat * mlp_gain[...] + mlp_shift[...]).astype(BF16)

            @pl.when(c + 1 < steps)
            def _():
                load_tokens(c + 1).start()
                load_cot(c + 1).start()

            @pl.when(c == 0)
            def _():
                load_qkv.wait()

            spot = lax.broadcasted_iota(jnp.int32, (CHUNK, LANES), 0) + c * CHUNK
            begin = jnp.zeros((CHUNK, LANES), jnp.int32)
            end = jnp.int32(0)
            for i in range(lengths.shape[1]):
                end = end + lengths[0, i]
                begin = jnp.where(spot >= end, end, begin)
            cosine[rows], sine[rows] = rotary_tables(spot, begin)

            for h in range(local_heads):
                cols = slice(h * HEAD_DIM, (h + 1) * HEAD_DIM)
                base = h * 3 * HEAD_DIM

                def joined(i):
                    there = slice(base + i * HEAD_DIM, base + (i + 1) * HEAD_DIM)
                    return dot(attn_chunk[...], qkv[:, there]) + qkv_bias[:, there]

                queries[:, cols] = turn(joined(0), rows, 1.0).astype(BF16)
                keys[rows, cols] = turn(joined(1), rows, 1.0).astype(BF16)
                values[rows, cols] = joined(2).astype(BF16)

            place = lax.broadcasted_iota(jnp.int32, (CHUNK, count), 1)
            here = lax.broadcasted_iota(jnp.int32, (CHUNK, count), 0) + c * CHUNK
            allowed = (place >= begin[:, :1]) & (place <= here)
            for h in range(local_heads):
                cols = slice(h * HEAD_DIM, (h + 1) * HEAD_DIM)
                scores = dot_cols(queries[:, cols], keys[:, cols]) * scale
                scores = jnp.where(allowed, scores, -1e30)
                expo = jnp.exp(scores - jnp.max(scores, axis=-1, keepdims=True))
                prob = expo * (1.0 / jnp.sum(expo, axis=-1, keepdims=True))
                probs[h] = prob
                attended_chunk[:, cols] = dot(prob.astype(BF16), values[:, cols]).astype(BF16)

            @pl.when(c == 0)
            def _():
                load_up.wait()
                load_down.wait()

            load_cot(c).wait()

            @pl.loop(0, inner_width // tile)
            def _(t):
                cols = span(t * tile, tile)
                pre = dot(mlp_chunk[...], up[:, cols]) + up_bias[:, cols]
                value, slope = gelu_parts(pre)
                hidden_chunk[:, cols] = value.astype(BF16)
                grad = (slope * dot_cols(cot[...], down[cols, :])).astype(BF16)
                hidden_grad_chunk[:, cols] = grad
                vectors[UP_BIAS : UP_BIAS + 1, cols] += column_sum(grad.astype(F32))

            @pl.when(c == 0)
            def _():
                load_dense.wait()

            @pl.loop(0, width // wide)
            def _(t):
                cols = span(t * wide, wide)
                part[:, cols] = dot(hidden_chunk[...], down[:, cols]) + dot(
                    attended_chunk[...], dense[:, cols]
                )

            store_part(c, part, part_sem.at[0])

            @pl.when(c == 0)
            def _():
                begin_messages()

            for copy in chunk_stores(c):
                copy.start()

            service(2 * c)

            attended_grad[...] = dot_cols(cot[...], dense[...]).astype(BF16)
            for h in range(local_heads):
                cols = slice(h * HEAD_DIM, (h + 1) * HEAD_DIM)
                base = h * 3 * HEAD_DIM
                grad = attended_grad[:, cols]
                prob = probs[h]
                prob_grad = dot_cols(grad, values[:, cols])
                along = jnp.sum(prob * prob_grad, axis=-1, keepdims=True)
                score_grad = (prob * (prob_grad - along)).astype(BF16)
                query_grad = dot(score_grad, keys[:, cols]) * scale
                joined_grad[rows, base : base + HEAD_DIM] = turn(query_grad, rows, -1.0).astype(
                    BF16
                )
                key_grad[:, cols] += dot_rows(score_grad, queries[:, cols]) * scale
                value_grad[:, cols] += dot_rows(prob.astype(BF16), grad)

            @pl.loop(0, CHUNK // BLOCK)
            def _(b):
                block = span(b * BLOCK, BLOCK)
                vectors[OUT_BIAS : OUT_BIAS + 1, :width] += column_sum(cot[block].astype(F32))

            service(2 * c + 1)

        for copy in chunk_stores(steps - 1):
            copy.wait()

        @pl.loop(0, steps)
        def _(c):
            rows = span(c * CHUNK, CHUNK)
            for h in range(local_heads):
                cols = slice(h * HEAD_DIM, (h + 1) * HEAD_DIM)
                base = h * 3 * HEAD_DIM
                joined_grad[rows, base + HEAD_DIM : base + 2 * HEAD_DIM] = turn(
                    key_grad[rows, cols], rows, -1.0
                ).astype(BF16)
                joined_grad[rows, base + 2 * HEAD_DIM : base + 3 * HEAD_DIM] = value_grad[
                    rows, cols
                ].astype(BF16)

    def backward(qkv, up, grad_chunk, token_chunk, hat, part, in_sems, part_sem, first_slot):
        wide = min(512, width)

        def loads(c):
            rows = span(c * CHUNK, CHUNK)
            return [
                pltpu.make_async_copy(
                    hidden_grad.at[rows], grad_chunk.at[lax.rem(c, 2)], in_sems.at[lax.rem(c, 2), 0]
                ),
                pltpu.make_async_copy(
                    tokens.at[rows], token_chunk.at[lax.rem(c, 2)], in_sems.at[lax.rem(c, 2), 1]
                ),
            ]

        for copy in loads(0):
            copy.start()

        @pl.loop(0, steps)
        def _(c):
            rows = span(c * CHUNK, CHUNK)
            for copy in loads(c):
                copy.wait()

            @pl.when(c + 1 < steps)
            def _():
                for copy in loads(c + 1):
                    copy.start()

            @pl.loop(0, CHUNK // BLOCK)
            def _(b):
                block = span(b * BLOCK, BLOCK)
                hat[block] = normalize(token_chunk[lax.rem(c, 2), block].astype(F32))[0]

            vectors[QKV_BIAS : QKV_BIAS + 1, : 3 * heads_width] += column_sum(
                joined_grad[rows].astype(F32)
            )

            @pl.loop(0, width // wide)
            def _(t):
                cols = span(t * wide, wide)
                attn_grad = dot_cols(joined_grad[rows], qkv[cols, :])
                mlp_grad = dot_cols(grad_chunk[lax.rem(c, 2)], up[cols, :])
                part[:, cols] = attn_grad * attn_gain[:, cols] + mlp_grad * mlp_gain[:, cols]
                near = hat[:, cols]
                for row, value in (
                    (ATTN_GAIN, attn_grad * near),
                    (ATTN_SHIFT, attn_grad),
                    (MLP_GAIN, mlp_grad * near),
                    (MLP_SHIFT, mlp_grad),
                ):
                    vectors[row : row + 1, cols] += column_sum(value)

            store_part(steps + c, part, part_sem.at[0])
            service(first_slot + c)

    def fill(source, target, sem):
        return pltpu.make_async_copy(source, target, sem)

    def spread_columns(number, left_source, split):
        plan, _ = spreads[number]
        depth = left_source.shape[1]

        def run(left, turned, right, tile, landed, sems):
            loads = [fill(left_source, left, sems.at[0]), fill(cotangent, right, sems.at[1])]
            for copy in loads:
                copy.start()
            for copy in loads:
                copy.wait()

            @pl.loop(0, depth // HEAD_DIM)
            def _(b):
                there = span(b * HEAD_DIM, HEAD_DIM)
                turned[there, :] = left[:, there].T

            def compute(where, target):
                right_cols = right[:, span(where * plan.cols, plan.cols)]
                block = min(512, depth)

                @pl.loop(0, depth // block)
                def _(b):
                    there = span(b * block, block)
                    target[there, :] = dot(turned[there, :], right_cols)

            tiles_out(number, compute, tile, sems)
            if split:
                next_slot()
            tiles_kept(number, compute, tile, landed, sems)
            next_slot()

        pl.run_scoped(
            run,
            pltpu.VMEM((count, depth), BF16),
            pltpu.VMEM((depth, count), BF16),
            pltpu.VMEM((count, width), BF16),
            pltpu.VMEM((2, plan.rows, plan.cols), F32),
            pltpu.VMEM((plan.rows, plan.cols), F32),
            pltpu.SemaphoreType.DMA((3,)),
        )

    def spread_rows(number, left_source, right_source):
        plan, _ = spreads[number]
        resident = right_source is joined_grad

        def run(left, right, tile, landed, sems):
            loads = [fill(left_source, left, sems.at[0])]
            if not resident:
                loads.append(fill(right_source, right, sems.at[1]))
            for copy in loads:
                copy.start()
            for copy in loads:
                copy.wait()
            use = joined_grad if resident else right

            def compute(where, target):
                turned = left[:, span(where * plan.rows, plan.rows)].T
                block = min(512, plan.cols)

                @pl.loop(0, plan.cols // block)
                def _(b):
                    there = span(b * block, block)
                    target[:, there] = dot(turned, use[:, there])

            tiles_out(number, compute, tile, sems)
            next_slot()
            tiles_kept(number, compute, tile, landed, sems)
            next_slot()

        pl.run_scoped(
            run,
            pltpu.VMEM((count, width), BF16),
            pltpu.VMEM((16, LANES) if resident else (count, plan.cols), BF16),
            pltpu.VMEM((2, plan.rows, plan.cols), F32),
            pltpu.VMEM((plan.rows, plan.cols), F32),
            pltpu.SemaphoreType.DMA((3,)),
        )

    QKV, DENSE, UP, DOWN = range(4)
    slots = [2 * steps]
    waiting = vector_steps()

    def next_slot():
        service(slots[0])
        slots[0] += 1

    def with_weights(qkv, up, w_sems):
        load_qkv = pltpu.make_async_copy(qkv_weight, qkv, w_sems.at[0])
        load_up = pltpu.make_async_copy(up_weight, up, w_sems.at[1])
        pl.run_scoped(
            functools.partial(forward, qkv, up, load_up, load_qkv),
            pltpu.VMEM(down_weight.shape, BF16),
            pltpu.VMEM(dense_weight.shape, BF16),
            pltpu.VMEM((count, heads_width), BF16),
            pltpu.VMEM((count, heads_width), BF16),
            pltpu.VMEM((count, heads_width), F32),
            pltpu.VMEM((count, heads_width), F32),
            pltpu.VMEM((CHUNK, width), BF16),
            pltpu.VMEM((2, CHUNK, width), BF16),
            pltpu.VMEM((CHUNK, width), BF16),
            pltpu.VMEM((CHUNK, width), BF16),
            pltpu.VMEM((CHUNK, inner_width), BF16),
            pltpu.VMEM((CHUNK, inner_width), BF16),
            pltpu.VMEM((CHUNK, width), F32),
            pltpu.VMEM((local_heads, CHUNK, count), F32),
            pltpu.VMEM((CHUNK, heads_width), BF16),
            pltpu.VMEM((CHUNK, heads_width), BF16),
            pltpu.VMEM((CHUNK, heads_width), BF16),
            pltpu.SemaphoreType.DMA((2,)),
            pltpu.SemaphoreType.DMA((3,)),
            pltpu.SemaphoreType.DMA((5,)),
            pltpu.SemaphoreType.DMA((1,)),
        )
        spread_columns(DOWN, hidden, True)
        spread_rows(UP, mlp_entry, hidden_grad)
        first = slots[0]
        slots[0] += steps
        pl.run_scoped(
            lambda *scratch: backward(qkv, up, *scratch, first),
            pltpu.VMEM((2, CHUNK, inner_width), BF16),
            pltpu.VMEM((2, CHUNK, width), BF16),
            pltpu.VMEM((CHUNK, width), F32),
            pltpu.VMEM((CHUNK, width), F32),
            pltpu.SemaphoreType.DMA((2, 2)),
            pltpu.SemaphoreType.DMA((1,)),
        )

    pl.run_scoped(
        with_weights,
        pltpu.VMEM(qkv_weight.shape, BF16),
        pltpu.VMEM(up_weight.shape, BF16),
        pltpu.SemaphoreType.DMA((2,)),
    )

    work = [
        functools.partial(spread_columns, DENSE, attended, False),
        functools.partial(spread_rows, QKV, attn_entry, joined_grad),
    ]
    for stage in range(1, bits):
        for number in (DOWN, UP, DENSE, QKV):
            for sides in ((0,), (1,)) if number != DENSE and stage < bits - 1 else ((0, 1),):

                def task(number=number, stage=stage, sides=sides):
                    for side in sides:
                        combine(number, stage, side)
                    next_slot()

                work.append(task)
    done = 0
    for i, task in enumerate(work):
        while done * len(work) < (i + 1) * len(waiting) and done < len(waiting):
            waiting[done]()
            done += 1
        task()

    @pl.loop(slots[0], messages + half)
    def _(j):
        service(j)

    end_messages()
    for number in (DOWN, DENSE, UP, QKV):
        end_spread(number)
    store_vectors = fill(vectors, vectors_out, vec_send.at[0])
    store_vectors.start()
    store_vectors.wait()


def layer_call(mp_size, dp_size, operands):
    tokens, qkv, dense, up, down = (operands[i] for i in (0, 2, 3, 4, 5))
    count, width = tokens.shape
    inner_width, heads_width = up.shape[1], dense.shape[0]
    messages = 2 * (count // ROWS)
    bits = dp_size.bit_length() - 1
    owned = width // dp_size
    plans = (
        Spread(bits, owned, qkv.shape[1]),
        Spread(bits, heads_width, owned),
        Spread(bits, owned, inner_width),
        Spread(bits, inner_width, owned),
    )
    exchanges = bits + 2 * (mp_size // 2)
    vector_width = max(width, inner_width, qkv.shape[1])
    anywhere = pl.BlockSpec(memory_space=pl.ANY)
    vmem = pl.BlockSpec(memory_space=pltpu.VMEM)
    shape = jax.ShapeDtypeStruct
    out_shape = [
        shape((count, width), BF16),
        shape((count, width), BF16),
        shape((VECTORS, vector_width), F32),
        shape((2 * count, width), F32),
        *(shape((plan.rows, plan.cols), F32) for plan in plans),
        shape((count, width), BF16),
        shape((count, width), BF16),
        shape((count, heads_width), BF16),
        shape((count, inner_width), BF16),
        shape((count, inner_width), BF16),
    ]
    for plan in plans:
        out_shape += [shape(dims, F32) for dims in plan.shapes()]
    dma = pltpu.SemaphoreType.DMA
    scratch = [
        pltpu.VMEM((SLOTS, ROWS, width), F32),
        pltpu.VMEM((SLOTS, ROWS, width), F32),
        pltpu.VMEM((SLOTS, ROWS, width), F32),
        pltpu.VMEM((2, ROWS, width), BF16),
        pltpu.VMEM((2, ROWS, width), BF16),
        pltpu.VMEM((2, ROWS, width), BF16),
        pltpu.VMEM((VECTORS, vector_width), F32),
        pltpu.VMEM((exchanges, VECTORS, vector_width), F32),
        pltpu.VMEM((count, qkv.shape[1]), BF16),
        pltpu.VMEM((count, LANES), F32),
        pltpu.VMEM((count, LANES), F32),
        dma((messages,)),
        dma((messages,)),
        dma((messages,)),
        dma((messages,)),
        dma((2,)),
        dma((2, 2)),
        dma((2,)),
        dma((exchanges,)),
        dma((exchanges,)),
    ]
    for plan in plans:
        scratch += [dma((plan.sems,)), dma((plan.sems,))]
    results = pl.pallas_call(
        functools.partial(layer_kernel, mp_size, plans),
        out_shape=tuple(out_shape),
        in_specs=[anywhere] * 6 + [vmem] * 7 + [pl.BlockSpec(memory_space=pltpu.SMEM)],
        out_specs=(anywhere,) * len(out_shape),
        scratch_shapes=scratch,
        compiler_params=pltpu.CompilerParams(
            collective_id=0, has_side_effects=True, vmem_limit_bytes=62 * 1024 * 1024
        ),
        cost_estimate=pl.CostEstimate(
            flops=6 * count * (width * (qkv.shape[1] + 2 * inner_width + heads_width)),
            bytes_accessed=300 << 20,
            transcendentals=0,
        ),
    )(*operands)
    return results[:3], results[4 : 4 + len(plans)]


def hand_out(dp_size, totals, *refs):
    refs = list(refs)
    vectors = refs.pop(0)
    number = (len(refs) - 1 - len(totals)) // 3
    sources, refs = refs[:number], refs[number:]
    targets, refs = refs[:number], refs[number:]
    pieces, refs = refs[: len(totals)], refs[len(totals) :]
    held, sems = refs[:number], refs[number]
    loads = [pltpu.make_async_copy(a, b, sems.at[0, i]) for i, (a, b) in enumerate(zip(sources, held))]
    stores = [pltpu.make_async_copy(a, b, sems.at[1, i]) for i, (a, b) in enumerate(zip(held, targets))]
    for copy in loads:
        copy.start()
    width = vectors.shape[1]
    for row, (total, piece) in enumerate(zip(totals, pieces)):
        size = total // dp_size
        shift = lax.rem(width - lax.axis_index("dp") * size, width)
        piece[...] = pltpu.roll(vectors[...], shift, 1)[row : row + 1, :size]
    for load, store in zip(loads, stores):
        load.wait()
        store.start()
    for copy in stores:
        copy.wait()


def hand_out_call(dp_size, totals, vectors, arrays):
    anywhere = pl.BlockSpec(memory_space=pl.ANY)
    vmem = pl.BlockSpec(memory_space=pltpu.VMEM)
    shape = jax.ShapeDtypeStruct
    results = pl.pallas_call(
        functools.partial(hand_out, dp_size, totals),
        out_shape=[shape(array.shape, array.dtype) for array in arrays]
        + [shape((1, total // dp_size), F32) for total in totals],
        in_specs=[vmem] + [anywhere] * len(arrays),
        out_specs=[anywhere] * len(arrays) + [vmem] * len(totals),
        scratch_shapes=[pltpu.VMEM(array.shape, array.dtype) for array in arrays]
        + [pltpu.SemaphoreType.DMA((2, len(arrays)))],
        compiler_params=pltpu.CompilerParams(vmem_limit_bytes=62 * 1024 * 1024),
    )(vectors, *arrays)
    return results[: len(arrays)], [piece[0] for piece in results[len(arrays) :]]


def per_device(
    mp_size,
    dp_size,
    tokens,
    lengths,
    attn_gain,
    attn_shift,
    mlp_gain,
    mlp_shift,
    qkv_weight,
    qkv_bias,
    dense_weight,
    up_weight,
    up_bias,
    down_weight,
    out_bias,
    cotangent,
):
    width = tokens.shape[1]
    (layer_output, input_grad, vectors), grads = layer_call(
        mp_size,
        dp_size,
        (
            tokens,
            cotangent,
            qkv_weight,
            dense_weight,
            up_weight,
            down_weight,
            attn_gain[None],
            attn_shift[None],
            mlp_gain[None],
            mlp_shift[None],
            qkv_bias[None],
            up_bias[None],
            out_bias[None],
            lengths,
        ),
    )
    totals = (width,) * 5 + (up_weight.shape[1], qkv_weight.shape[1])
    arrays, pieces = hand_out_call(dp_size, totals, vectors, (layer_output, input_grad, *grads))
    layer_output, input_grad, qkv_grad, dense_grad, up_grad, down_grad = arrays
    attn_gain_grad, attn_shift_grad, mlp_gain_grad, mlp_shift_grad = pieces[:4]
    return (
        layer_output,
        input_grad,
        attn_gain_grad,
        attn_shift_grad,
        mlp_gain_grad,
        mlp_shift_grad,
        qkv_grad,
        pieces[QKV_BIAS],
        dense_grad,
        up_grad,
        pieces[UP_BIAS],
        down_grad,
        pieces[OUT_BIAS],
    )


def solution(mesh):
    in_specs = (
        P("dp", None),
        P("dp", None),
        P(),
        P(),
        P(),
        P(),
        P(None, "mp"),
        P("mp"),
        P("mp", None),
        P(None, "mp"),
        P("mp"),
        P("mp", None),
        P(),
        P("dp", None),
    )
    out_specs = (
        P("dp", None),
        P("dp", None),
        P("dp"),
        P("dp"),
        P("dp"),
        P("dp"),
        P("dp", "mp"),
        P(("mp", "dp")),
        P("mp", "dp"),
        P("dp", "mp"),
        P(("mp", "dp")),
        P("mp", "dp"),
        P("dp"),
    )
    function = functools.partial(per_device, mesh.shape["mp"], mesh.shape["dp"])
    return jax.shard_map(
        function, mesh=mesh, in_specs=in_specs, out_specs=out_specs, check_vma=False
    )
```

```python
import functools
import math

import jax
import jax.numpy as jnp
from jax import lax
from jax.experimental import pallas as pl
from jax.experimental.pallas import tpu as pltpu
from jax.sharding import PartitionSpec as P

HEAD_DIM = 256
ROT = 64
EPSILON = 1e-05
LANES = 128

MESH = pl.DeviceIdType.MESH
ROWS = 32
SLOTS = 10
AHEAD = 5
AHEAD_ODD = 5
PENDING = 3
LAG = 1
CHUNK = 256
BLOCK = 32

F32 = jnp.float32
BF16 = jnp.bfloat16

VECTORS = 8
ATTN_GAIN, ATTN_SHIFT, MLP_GAIN, MLP_SHIFT, OUT_BIAS, UP_BIAS, QKV_BIAS = range(7)


def sine_cosine(angle):
    turns = jnp.floor(angle * (2.0 / math.pi) + 0.5)
    rest = angle - turns * 1.5703125 - turns * 4.837512969970703e-4 - turns * 7.549789954891882e-8
    square = rest * rest
    sine = rest + rest * square * (
        -1.6666654611e-1 + square * (8.3321608736e-3 - square * 1.9515295891e-4)
    )
    cosine = (
        1.0
        - 0.5 * square
        + square
        * square
        * (4.166664568298827e-2 + square * (-1.388731625493765e-3 + square * 2.443315711809948e-5))
    )
    quarter = turns - 4.0 * jnp.floor(turns * 0.25)
    odd = (quarter == 1.0) | (quarter == 3.0)
    flip_sine = quarter >= 2.0
    flip_cosine = (quarter == 1.0) | (quarter == 2.0)
    near_sine = jnp.where(odd, cosine, sine)
    near_cosine = jnp.where(odd, sine, cosine)
    return (
        jnp.where(flip_sine, -near_sine, near_sine),
        jnp.where(flip_cosine, -near_cosine, near_cosine),
    )


def rotary_tables(place, start):
    lane = lax.broadcasted_iota(jnp.int32, place.shape, 1)
    half = ROT // 2
    step = jnp.where(lane < half, lane, lane - half).astype(F32)
    freqs = jnp.exp(step * (-2.0 * math.log(10000.0) / ROT))
    sine, cosine = sine_cosine((place - start).astype(F32) * freqs)
    cosine = jnp.where(lane < ROT, cosine, 1.0)
    sine = jnp.where(lane < half, -sine, jnp.where(lane < ROT, sine, 0.0))
    return cosine, sine


def normalize(rows):
    centred = rows - jnp.mean(rows, axis=-1, keepdims=True)
    factor = lax.rsqrt(jnp.mean(centred * centred, axis=-1, keepdims=True) + EPSILON)
    return centred * factor, factor


def gelu_parts(v):
    cdf = 0.5 + 0.5 * lax.erf(v * math.sqrt(0.5))
    return v * cdf, cdf + v * jnp.exp(-0.5 * v * v) * (1.0 / math.sqrt(2.0 * math.pi))


def dot(left, right):
    return jnp.dot(left, right, preferred_element_type=F32)


def dot_cols(left, right):
    return lax.dot_general(left, right, (((1,), (1,)), ((), ())), preferred_element_type=F32)


def dot_rows(left, right):
    return lax.dot_general(left, right, (((0,), (0,)), ((), ())), preferred_element_type=F32)


def column_sum(x):
    return jnp.sum(x, axis=0, keepdims=True)


def span(start, size):
    return pl.ds(pl.multiple_of(start, size), size)


class Spread:
    def __init__(self, bits, rows, cols):
        self.bits, self.rows, self.cols = bits, rows, cols
        self.tiles = 1 << bits
        self.orders = ([0] + list(range(1, bits)), [0] + list(range(bits - 1, 0, -1)))
        count = self.tiles // 2
        self.first = {}
        for stage in range(1, bits):
            for side in range(2):
                self.first[stage, side] = count
                count += self.tiles >> (stage + 1)
        self.sems = count

    def masks(self, side, stage):
        order = self.orders[side]
        return [m for m in range(self.tiles) if not any((m >> b) & 1 for b in order[:stage])]

    def place(self, mask, side, stage):
        return self.masks(side, stage + 1).index(mask)

    def shapes(self):
        shapes = [(self.tiles // 2, self.rows, self.cols)]
        for stage in range(self.bits):
            shapes.append((self.tiles >> (stage + 1), self.rows, self.cols))
        return shapes


def layer_kernel(mp_size, plans, *refs):
    refs = list(refs)

    def take(number):
        taken = refs[:number]
        del refs[:number]
        return taken

    tokens, cotangent, qkv_weight, dense_weight, up_weight, down_weight = take(6)
    attn_gain, attn_shift, mlp_gain, mlp_shift, qkv_bias, up_bias, out_bias = take(7)
    lengths = take(1)[0]
    layer_out, input_grad, vectors_out, parts = take(4)
    grads_out = take(len(plans))
    attn_entry, mlp_entry, attended, hidden, hidden_grad = take(5)
    spreads = [(plan, take(1 + plan.bits)) for plan in plans]
    from_outer, held, token_rows, cot_rows, out_rows = take(5)
    vectors, vectors_in, joined_grad, cosine, sine = take(5)
    send_in, send_out, recv_outer, recv_inner, part_sems, row_sems, out_sems = take(7)
    vec_send, vec_recv = take(2)
    spread_sems = [take(2) for _ in plans]

    count, width = tokens.shape
    inner_width = up_weight.shape[1]
    heads_width = dense_weight.shape[0]
    local_heads = heads_width // HEAD_DIM
    bits = plans[0].bits
    steps = count // CHUNK
    scale = 1.0 / math.sqrt(HEAD_DIM)
    branch_messages = count // ROWS
    messages = 2 * branch_messages
    chunk_messages = CHUNK // ROWS
    half = mp_size // 2

    index = lax.axis_index("mp")
    upper = index // half
    level = index * (1 - upper) + (mp_size - 1 - index) * upper
    inner = index + 1 - 2 * upper
    outer = index - 1 + 2 * upper
    lag = half - level + LAG
    ahead = min(AHEAD, SLOTS - 1 - LAG - half)
    is_middle = level == half - 1
    total_place = (1 - level // (half - 1)) * SLOTS if half > 1 else 0
    device = lax.axis_index("dp")
    ahead = ahead + (device % 2) * (min(AHEAD_ODD, SLOTS - 1 - LAG - half) - ahead)

    def partner(bit):
        return device + (1 - 2 * ((device // (1 << bit)) % 2)) * (1 << bit)

    def owner(mask):
        total = 0
        for bit in range(bits):
            total = total + ((device // (1 << bit) + mask // (1 << bit)) % 2) * (1 << bit)
        return total

    def meet():
        barrier = pltpu.get_barrier_semaphore()
        pl.semaphore_signal(barrier, inc=1, device_id={"mp": inner}, device_id_type=MESH)
        for bit in range(bits):
            pl.semaphore_signal(barrier, inc=1, device_id={"dp": partner(bit)}, device_id_type=MESH)
        if half > 1:

            @pl.when(level > 0)
            def _():
                pl.semaphore_signal(barrier, inc=1, device_id={"mp": outer}, device_id_type=MESH)
                pl.semaphore_wait(barrier, 2 + bits)

            @pl.when(level == 0)
            def _():
                pl.semaphore_wait(barrier, 1 + bits)

        else:
            pl.semaphore_wait(barrier, 1 + bits)


    def slot(ref, k):
        return ref.at[lax.rem(k, SLOTS)]

    def sums(k):
        return held.at[lax.rem(k, SLOTS)]

    def from_inner(k):
        return held.at[lax.rem(k, SLOTS) + SLOTS]

    def totals(k):
        return held.at[lax.rem(k, SLOTS) + total_place]

    def message(ref, k):
        return ref.at[span(k * ROWS, ROWS)]

    def to_inner(k, source, landing, sem):
        return pltpu.make_async_remote_copy(
            src_ref=source,
            dst_ref=landing,
            send_sem=send_in.at[k],
            recv_sem=sem.at[k],
            device_id={"mp": inner},
            device_id_type=MESH,
        )

    def to_outer(k):
        return pltpu.make_async_remote_copy(
            src_ref=totals(k),
            dst_ref=from_inner(k),
            send_sem=send_out.at[k],
            recv_sem=recv_inner.at[k],
            device_id={"mp": outer},
            device_id_type=MESH,
        )

    def load_part(k):
        return pltpu.make_async_copy(message(parts, k), sums(k), part_sems.at[lax.rem(k, 2)])

    def load_rows(k):
        row, place = lax.rem(k, branch_messages), lax.rem(k, 2)
        return [
            pltpu.make_async_copy(
                message(tokens, row), token_rows.at[place], row_sems.at[0, place]
            ),
            pltpu.make_async_copy(
                message(cotangent, row), cot_rows.at[place], row_sems.at[1, place]
            ),
        ]

    def store_rows(k, target):
        place = lax.rem(k, 2)
        return pltpu.make_async_copy(
            out_rows.at[place], message(target, lax.rem(k, branch_messages)), out_sems.at[place]
        )

    def send_ahead(k):
        if half > 1:

            @pl.when((level == 0) & (k < messages))
            def _():
                to_inner(k, message(parts, k), slot(from_outer, k), recv_outer).start()

    def begin_messages():
        @pl.loop(0, ahead)
        def _(k):
            send_ahead(k)

        for copy in load_rows(0):
            copy.start()
        if half > 1:

            @pl.when(level > 0)
            def _():
                load_part(0).start()

        else:
            load_part(0).start()

    def add_inward(j):
        @pl.when(j < messages)
        def _():
            load_part(j).wait()

            @pl.when(j + 1 < messages)
            def _():
                load_part(j + 1).start()

            mine = sums(j)
            if half > 1:
                to_inner(j, mine, slot(from_outer, j), recv_outer).wait_recv()
                mine[...] += slot(from_outer, j)[...]

            @pl.when(is_middle)
            def _():
                to_inner(j, mine, from_inner(j), recv_inner).start()

            if half > 2:

                @pl.when(level < half - 1)
                def _():
                    to_inner(j, mine, slot(from_outer, j), recv_outer).start()

    def finish(k):
        place = lax.rem(k, 2)
        source = totals(k)

        @pl.when(k < branch_messages)
        def _():
            @pl.loop(0, ROWS // BLOCK)
            def _(b):
                rows = span(b * BLOCK, BLOCK)
                out_rows[place, rows] = (
                    token_rows[place, rows].astype(F32) + source[rows] + out_bias[...]
                ).astype(BF16)

        @pl.when(k >= branch_messages)
        def _():
            @pl.loop(0, ROWS // BLOCK)
            def _(b):
                rows = span(b * BLOCK, BLOCK)
                hat, factor = normalize(token_rows[place, rows].astype(F32))
                entry = source[rows]
                part = (
                    entry
                    - jnp.mean(entry, axis=-1, keepdims=True)
                    - hat * jnp.mean(entry * hat, axis=-1, keepdims=True)
                )
                out_rows[place, rows] = (
                    cot_rows[place, rows].astype(F32) + factor * part
                ).astype(BF16)

    def pass_outward(k):
        @pl.when((k >= 0) & (k < messages))
        def _():
            to_inner(k, sums(k), from_inner(k), recv_inner).wait()

            @pl.when(is_middle)
            def _():
                sums(k)[...] += from_inner(k)[...]

            if half > 1:

                @pl.when(level > 0)
                def _():
                    @pl.when(k >= PENDING)
                    def _():
                        to_outer(k - PENDING).wait_send()

                    to_outer(k).start()

            @pl.when(k + 1 < messages)
            def _():
                for copy in load_rows(k + 1):
                    copy.start()

            for copy in load_rows(k):
                copy.wait()

            @pl.when(k >= 2)
            def _():
                store_rows(k - 2, layer_out).wait()

            finish(k)

            @pl.when(k < branch_messages)
            def _():
                store_rows(k, layer_out).start()

            @pl.when(k >= branch_messages)
            def _():
                store_rows(k, input_grad).start()

    def service(j):
        send_ahead(j + ahead)
        if half > 1:

            @pl.when(level > 0)
            def _():
                add_inward(j)

        else:
            add_inward(j)
        pass_outward(j - lag)

    def end_messages():
        if half > 1:

            @pl.when(level > 0)
            def _():
                for k in range(messages - PENDING, messages):
                    to_outer(k).wait_send()

        for k in (messages - 2, messages - 1):
            store_rows(k, input_grad).wait()


    def spread_copy(number, stage, side, source, target, sem, bit):
        sends, recvs = spread_sems[number]
        return pltpu.make_async_remote_copy(
            src_ref=source,
            dst_ref=target,
            send_sem=sends.at[sem],
            recv_sem=recvs.at[sem],
            device_id={"dp": partner(bit)},
            device_id_type=MESH,
        )

    def side_rows(plan, side):
        return pl.ds(side * (plan.rows // 2), plan.rows // 2)

    def stage_copies(number, stage, side):
        plan, buffers = spreads[number]
        keep, landing = buffers[0], buffers[1 + stage]
        bit = plan.orders[side][stage]
        copies = []
        for mask in plan.masks(side, stage):
            if (mask >> bit) & 1:
                place = plan.place(mask ^ (1 << bit), side, stage)
                copies.append(
                    spread_copy(
                        number,
                        stage,
                        side,
                        keep.at[mask // 2, side_rows(plan, side)],
                        landing.at[place, side_rows(plan, side)],
                        plan.first[stage, side] + place,
                        bit,
                    )
                )
        return copies

    def tiles_of(number, compute, sent, kept, landed, sems, first, each):
        plan, buffers = spreads[number]
        half_tiles = plan.tiles // 2
        every = max(1, half_tiles // 4)

        def copy(i):
            return spread_copy(number, 0, 0, sent.at[lax.rem(i, 2)], buffers[1].at[i], i, 0)

        def load(i):
            return pltpu.make_async_copy(buffers[1].at[i], landed, sems.at[0])

        def store(i):
            return pltpu.make_async_copy(
                kept.at[lax.rem(i, 2)], buffers[0].at[i], sems.at[1 + lax.rem(i, 2)]
            )

        def begin_add(i):
            copy(i).wait_recv()
            load(i).start()

        def end_add(i):
            load(i).wait()
            kept.at[lax.rem(i, 2)][...] += landed[...]
            store(i).start()

        @pl.loop(0, half_tiles)
        def _(i):
            @pl.when(i >= 2)
            def _():
                copy(i - 2).wait_send()

            compute(owner(2 * i + 1), sent.at[lax.rem(i, 2)])
            copy(i).start()

            @pl.when(i >= 1)
            def _():
                begin_add(i - 1)

            if each == 2:

                @pl.when(lax.rem(i, every) == every - 1)
                def _():
                    service(first + 2 * (i // every))

            @pl.when(i >= 2)
            def _():
                store(i - 2).wait()

            compute(owner(2 * i), kept.at[lax.rem(i, 2)])

            @pl.when(i >= 1)
            def _():
                end_add(i - 1)

            if each >= 1:

                @pl.when(lax.rem(i, every) == every - 1)
                def _():
                    service(first + each * (i // every) + each - 1)

        begin_add(half_tiles - 1)
        end_add(half_tiles - 1)
        for i in (half_tiles - 2, half_tiles - 1):
            copy(i).wait_send()
            store(i).wait()
        for side in range(2):
            for copies in stage_copies(number, 1, side):
                copies.start()

    def combine(number, stage, side):
        plan, buffers = spreads[number]
        keep, landing = buffers[0], buffers[1 + stage]
        last = stage == bits - 1
        rows = plan.rows // 4

        masks = plan.masks(side, stage + 1)

        def run(mine, other, sems):
            for copy in stage_copies(number, stage, side):
                copy.wait_recv()
            loads, stores = [], []
            for mask in masks:
                place = plan.place(mask, side, stage)
                for piece in range(2):
                    there = pl.ds(side * (plan.rows // 2) + piece * rows, rows)
                    at = len(loads)
                    kept = keep.at[mask // 2, there]
                    loads.append(
                        [
                            pltpu.make_async_copy(kept, mine.at[at], sems.at[0, at]),
                            pltpu.make_async_copy(
                                landing.at[place, there], other.at[at], sems.at[1, at]
                            ),
                        ]
                    )
                    target = grads_out[number].at[there] if last else kept
                    stores.append(pltpu.make_async_copy(mine.at[at], target, sems.at[2, at]))
            for load in loads:
                for copy in load:
                    copy.start()
            for i, (load, store) in enumerate(zip(loads, stores)):
                for copy in load:
                    copy.wait()
                mine[i] += other[i]
                store.start()
            for store in stores:
                store.wait()
            if not last:
                for copy in stage_copies(number, stage + 1, side):
                    copy.start()

        pieces = 2 * len(masks)
        shape = (pieces, rows, plan.cols)
        pl.run_scoped(
            run,
            pltpu.VMEM(shape, F32),
            pltpu.VMEM(shape, F32),
            pltpu.SemaphoreType.DMA((3, pieces)),
        )

    def end_spread(number):
        plan, _ = spreads[number]
        for side in range(2):
            for stage in range(1, bits):
                for copy in stage_copies(number, stage, side):
                    copy.wait_send()


    def vector_copy(place, device_id):
        return pltpu.make_async_remote_copy(
            src_ref=vectors,
            dst_ref=vectors_in.at[place],
            send_sem=vec_send.at[place],
            recv_sem=vec_recv.at[place],
            device_id=device_id,
            device_id_type=MESH,
        )

    norms = pl.ds(0, 4)

    def inward_hop(hop):
        return vector_copy(bits + hop, {"mp": inner})

    def outward_hop(hop):
        return vector_copy(bits + half + hop, {"mp": outer})

    def vector_steps():
        steps = []

        def start_inward(hop):
            @pl.when(level == hop)
            def _():
                inward_hop(hop).start()

        def end_inward(hop):
            @pl.when(level == hop)
            def _():
                inward_hop(hop).wait_send()

            if hop < half - 1:

                @pl.when(level == hop + 1)
                def _():
                    inward_hop(hop).wait_recv()
                    vectors[norms] += vectors_in[bits + hop, norms]

            else:

                @pl.when(is_middle)
                def _():
                    inward_hop(hop).wait_recv()
                    vectors[norms] += vectors_in[bits + hop, norms]

        def start_outward(hop):
            @pl.when(level == hop + 1)
            def _():
                outward_hop(hop).start()

        def end_outward(hop):
            @pl.when(level == hop + 1)
            def _():
                outward_hop(hop).wait_send()

            @pl.when(level == hop)
            def _():
                outward_hop(hop).wait_recv()
                vectors[norms] = vectors_in[bits + half + hop, norms]

        def start_across(bit):
            vector_copy(bit, {"dp": partner(bit)}).start()

        def end_across(bit):
            vector_copy(bit, {"dp": partner(bit)}).wait()
            vectors[...] += vectors_in[bit]

        moves = [
            (functools.partial(start_inward, hop), functools.partial(end_inward, hop))
            for hop in range(half)
        ]
        moves += [
            (functools.partial(start_outward, hop), functools.partial(end_outward, hop))
            for hop in reversed(range(half - 1))
        ]
        moves += [
            (functools.partial(start_across, bit), functools.partial(end_across, bit))
            for bit in range(bits)
        ]

        def step(i):
            if i > 0:
                moves[i - 1][1]()
            if i < len(moves):
                moves[i][0]()

        return [functools.partial(step, i) for i in range(len(moves) + 1)]


    first_lanes = lax.broadcasted_iota(jnp.int32, (CHUNK, LANES), 1)

    def swap_halves(x):
        return jnp.where(
            first_lanes < ROT // 2,
            pltpu.roll(x, LANES - ROT // 2, 1),
            pltpu.roll(x, ROT // 2, 1),
        )

    def turn(x, rows, sign):
        low = x[:, :LANES]
        low = low * cosine[rows] + sign * swap_halves(low) * sine[rows]
        return jnp.concatenate([low, x[:, LANES:]], axis=1)

    def store_part(c, part, sem):
        copy = pltpu.make_async_copy(part, parts.at[span(c * CHUNK, CHUNK)], sem)
        copy.start()
        copy.wait()

    def forward(
        qkv,
        up,
        load_up,
        load_qkv,
        down,
        dense,
        keys,
        values,
        key_grad,
        value_grad,
        token_chunk,
        cot_chunk,
        attn_chunk,
        mlp_chunk,
        hidden_chunk,
        hidden_grad_chunk,
        slope,
        part,
        probs,
        queries,
        attended_chunk,
        attended_grad,
        w_sems,
        in_sems,
        out_chunk_sems,
        part_sem,
    ):
        load_down = pltpu.make_async_copy(down_weight, down, w_sems.at[0])
        load_dense = pltpu.make_async_copy(dense_weight, dense, w_sems.at[1])
        tile = min(512, inner_width)
        wide = min(512, width)

        def load_tokens(c):
            return pltpu.make_async_copy(
                tokens.at[span(c * CHUNK, CHUNK)], token_chunk, in_sems.at[0]
            )

        def load_cot(c):
            return pltpu.make_async_copy(
                cotangent.at[span(c * CHUNK, CHUNK)],
                cot_chunk.at[lax.rem(c, 2)],
                in_sems.at[1 + lax.rem(c, 2)],
            )

        def chunk_stores(c):
            pairs = (
                (attn_chunk, attn_entry),
                (mlp_chunk, mlp_entry),
                (attended_chunk, attended),
                (hidden_chunk, hidden),
                (hidden_grad_chunk, hidden_grad),
            )
            return [
                pltpu.make_async_copy(
                    source, target.at[span(c * CHUNK, CHUNK)], out_chunk_sems.at[i]
                )
                for i, (source, target) in enumerate(pairs)
            ]

        load_tokens(0).start()
        load_qkv.start()
        load_up.start()
        load_down.start()
        load_dense.start()
        load_cot(0).start()
        meet()
        keys[...] = jnp.zeros_like(keys)
        values[...] = jnp.zeros_like(values)
        key_grad[...] = jnp.zeros_like(key_grad)
        value_grad[...] = jnp.zeros_like(value_grad)
        vectors[...] = jnp.zeros_like(vectors)

        def by_extent(c, function):
            low = 0
            while low < steps:
                high = min(steps, max(2 * low, 1))

                @pl.when((c >= low) & (c < high))
                def _():
                    function(high * CHUNK)

                low = high

        @pl.loop(0, steps)
        def _(c):
            rows = span(c * CHUNK, CHUNK)
            cot = cot_chunk.at[lax.rem(c, 2)]
            load_tokens(c).wait()

            @pl.when(c > 0)
            def _():
                for copy in chunk_stores(c - 1):
                    copy.wait()

            @pl.loop(0, CHUNK // BLOCK)
            def _(b):
                block = span(b * BLOCK, BLOCK)
                hat, _ = normalize(token_chunk[block].astype(F32))
                attn_chunk[block] = (hat * attn_gain[...] + attn_shift[...]).astype(BF16)
                mlp_chunk[block] = (hat * mlp_gain[...] + mlp_shift[...]).astype(BF16)

            @pl.when(c + 1 < steps)
            def _():
                load_tokens(c + 1).start()
                load_cot(c + 1).start()

            @pl.when(c == 0)
            def _():
                load_qkv.wait()

            spot = lax.broadcasted_iota(jnp.int32, (CHUNK, LANES), 0) + c * CHUNK
            begin = jnp.zeros((CHUNK, LANES), jnp.int32)
            end = jnp.int32(0)
            for i in range(lengths.shape[1]):
                end = end + lengths[0, i]
                begin = jnp.where(spot >= end, end, begin)
            cosine[rows], sine[rows] = rotary_tables(spot, begin)

            for h in range(local_heads):
                cols = slice(h * HEAD_DIM, (h + 1) * HEAD_DIM)
                base = h * 3 * HEAD_DIM

                def joined(i):
                    there = slice(base + i * HEAD_DIM, base + (i + 1) * HEAD_DIM)
                    return dot(attn_chunk[...], qkv[:, there]) + qkv_bias[:, there]

                queries[:, cols] = turn(joined(0), rows, 1.0).astype(BF16)
                keys[rows, cols] = turn(joined(1), rows, 1.0).astype(BF16)
                values[rows, cols] = joined(2).astype(BF16)

            def attend(extent):
                place = lax.broadcasted_iota(jnp.int32, (CHUNK, extent), 1)
                here = lax.broadcasted_iota(jnp.int32, (CHUNK, extent), 0) + c * CHUNK
                allowed = (place >= begin[:, :1]) & (place <= here)
                for h in range(local_heads):
                    cols = slice(h * HEAD_DIM, (h + 1) * HEAD_DIM)
                    scores = dot_cols(queries[:, cols], keys[:extent, cols]) * scale
                    scores = jnp.where(allowed, scores, -1e30)
                    expo = jnp.exp(scores - jnp.max(scores, axis=-1, keepdims=True))
                    prob = expo * (1.0 / jnp.sum(expo, axis=-1, keepdims=True))
                    probs[h, :, :extent] = prob
                    attended_chunk[:, cols] = dot(prob.astype(BF16), values[:extent, cols]).astype(
                        BF16
                    )

            by_extent(c, attend)

            @pl.when(c > 0)
            def _():
                service(c * 4 - 2)

            @pl.when(c == 0)
            def _():
                load_up.wait()

            @pl.loop(0, inner_width // tile)
            def _(t):
                cols = span(t * tile, tile)
                pre = dot(mlp_chunk[...], up[:, cols]) + up_bias[:, cols]
                value, derivative = gelu_parts(pre)
                hidden_chunk[:, cols] = value.astype(BF16)
                slope[:, cols] = derivative

            @pl.when(c == 0)
            def _():
                load_down.wait()
                load_dense.wait()

            @pl.loop(0, width // wide)
            def _(t):
                cols = span(t * wide, wide)
                part[:, cols] = dot(hidden_chunk[...], down[:, cols]) + dot(
                    attended_chunk[...], dense[:, cols]
                )

            store_part(c, part, part_sem.at[0])

            @pl.when(c == 0)
            def _():
                begin_messages()

            @pl.when(c > 0)
            def _():
                service(c * 4 - 1)

            load_cot(c).wait()

            @pl.loop(0, inner_width // tile)
            def _(t):
                cols = span(t * tile, tile)
                grad = (slope[:, cols] * dot_cols(cot[...], down[cols, :])).astype(BF16)
                hidden_grad_chunk[:, cols] = grad
                vectors[UP_BIAS : UP_BIAS + 1, cols] += column_sum(grad.astype(F32))

            for copy in chunk_stores(c):
                copy.start()

            service(c * 4)
            attended_grad[...] = dot_cols(cot[...], dense[...]).astype(BF16)

            def attend_back(extent):
                for h in range(local_heads):
                    cols = slice(h * HEAD_DIM, (h + 1) * HEAD_DIM)
                    base = h * 3 * HEAD_DIM
                    grad = attended_grad[:, cols]
                    prob = probs[h, :, :extent]
                    prob_grad = dot_cols(grad, values[:extent, cols])
                    along = jnp.sum(prob * prob_grad, axis=-1, keepdims=True)
                    score_grad = (prob * (prob_grad - along)).astype(BF16)
                    query_grad = dot(score_grad, keys[:extent, cols]) * scale
                    joined_grad[rows, base : base + HEAD_DIM] = turn(query_grad, rows, -1.0).astype(
                        BF16
                    )
                    key_grad[:extent, cols] += dot_rows(score_grad, queries[:, cols]) * scale
                    value_grad[:extent, cols] += dot_rows(prob.astype(BF16), grad)

            by_extent(c, attend_back)

            @pl.loop(0, CHUNK // BLOCK)
            def _(b):
                block = span(b * BLOCK, BLOCK)
                vectors[OUT_BIAS : OUT_BIAS + 1, :width] += column_sum(cot[block].astype(F32))

            service(c * 4 + 1)

        for copy in chunk_stores(steps - 1):
            copy.wait()

        @pl.loop(0, steps)
        def _(c):
            rows = span(c * CHUNK, CHUNK)
            for h in range(local_heads):
                cols = slice(h * HEAD_DIM, (h + 1) * HEAD_DIM)
                base = h * 3 * HEAD_DIM
                joined_grad[rows, base + HEAD_DIM : base + 2 * HEAD_DIM] = turn(
                    key_grad[rows, cols], rows, -1.0
                ).astype(BF16)
                joined_grad[rows, base + 2 * HEAD_DIM : base + 3 * HEAD_DIM] = value_grad[
                    rows, cols
                ].astype(BF16)

    def backward(qkv, up, grad_chunk, token_chunk, hat, part, in_sems, part_sem, first_slot):
        wide = min(512, width)

        def loads(c):
            rows = span(c * CHUNK, CHUNK)
            return [
                pltpu.make_async_copy(
                    hidden_grad.at[rows], grad_chunk.at[lax.rem(c, 2)], in_sems.at[lax.rem(c, 2), 0]
                ),
                pltpu.make_async_copy(
                    tokens.at[rows], token_chunk.at[lax.rem(c, 2)], in_sems.at[lax.rem(c, 2), 1]
                ),
            ]

        for copy in loads(0):
            copy.start()

        @pl.loop(0, steps)
        def _(c):
            rows = span(c * CHUNK, CHUNK)
            for copy in loads(c):
                copy.wait()

            @pl.when(c + 1 < steps)
            def _():
                for copy in loads(c + 1):
                    copy.start()

            @pl.loop(0, CHUNK // BLOCK)
            def _(b):
                block = span(b * BLOCK, BLOCK)
                hat[block] = normalize(token_chunk[lax.rem(c, 2), block].astype(F32))[0]

            vectors[QKV_BIAS : QKV_BIAS + 1, : 3 * heads_width] += column_sum(
                joined_grad[rows].astype(F32)
            )

            @pl.loop(0, width // wide)
            def _(t):
                cols = span(t * wide, wide)
                attn_grad = dot_cols(joined_grad[rows], qkv[cols, :])
                mlp_grad = dot_cols(grad_chunk[lax.rem(c, 2)], up[cols, :])
                part[:, cols] = attn_grad * attn_gain[:, cols] + mlp_grad * mlp_gain[:, cols]
                near = hat[:, cols]
                for row, value in (
                    (ATTN_GAIN, attn_grad * near),
                    (ATTN_SHIFT, attn_grad),
                    (MLP_GAIN, mlp_grad * near),
                    (MLP_SHIFT, mlp_grad),
                ):
                    vectors[row : row + 1, cols] += column_sum(value)

                @pl.when(t == width // wide // 2 - 1)
                def _():
                    service(first_slot + 2 * c)

            store_part(steps + c, part, part_sem.at[0])
            service(first_slot + 2 * c + 1)

    def fill(source, target, sem):
        return pltpu.make_async_copy(source, target, sem)

    def spread_columns(number, left_source, each):
        plan, _ = spreads[number]
        depth = left_source.shape[1]

        def run(left, turned, right, sent, kept, landed, sems):
            loads = [fill(left_source, left, sems.at[0]), fill(cotangent, right, sems.at[1])]
            for copy in loads:
                copy.start()
            for copy in loads:
                copy.wait()

            @pl.loop(0, depth // HEAD_DIM)
            def _(b):
                there = span(b * HEAD_DIM, HEAD_DIM)
                turned[there, :] = left[:, there].T

            def compute(where, target):
                right_cols = right[:, span(where * plan.cols, plan.cols)]
                block = min(512, depth)

                @pl.loop(0, depth // block)
                def _(b):
                    there = span(b * block, block)
                    target[there, :] = dot(turned[there, :], right_cols)

            tiles_of(number, compute, sent, kept, landed, sems, take_slots(4 * each), each)
            if not each:
                next_slot()

        pl.run_scoped(
            run,
            pltpu.VMEM((count, depth), BF16),
            pltpu.VMEM((depth, count), BF16),
            pltpu.VMEM((count, width), BF16),
            pltpu.VMEM((2, plan.rows, plan.cols), F32),
            pltpu.VMEM((2, plan.rows, plan.cols), F32),
            pltpu.VMEM((plan.rows, plan.cols), F32),
            pltpu.SemaphoreType.DMA((3,)),
        )

    def spread_rows(number, left_source, right_source, each):
        plan, _ = spreads[number]
        resident = right_source is joined_grad

        def run(left, right, sent, kept, landed, sems):
            loads = [fill(left_source, left, sems.at[0])]
            if not resident:
                loads.append(fill(right_source, right, sems.at[1]))
            for copy in loads:
                copy.start()
            for copy in loads:
                copy.wait()
            use = joined_grad if resident else right

            def compute(where, target):
                turned = left[:, span(where * plan.rows, plan.rows)].T
                block = min(512, plan.cols)

                @pl.loop(0, plan.cols // block)
                def _(b):
                    there = span(b * block, block)
                    target[:, there] = dot(turned, use[:, there])

            tiles_of(number, compute, sent, kept, landed, sems, take_slots(4 * each), each)

        pl.run_scoped(
            run,
            pltpu.VMEM((count, width), BF16),
            pltpu.VMEM((16, LANES) if resident else (count, plan.cols), BF16),
            pltpu.VMEM((2, plan.rows, plan.cols), F32),
            pltpu.VMEM((2, plan.rows, plan.cols), F32),
            pltpu.VMEM((plan.rows, plan.cols), F32),
            pltpu.SemaphoreType.DMA((3,)),
        )

    QKV, DENSE, UP, DOWN = range(4)
    slots = [4 * steps - 2]
    waiting = vector_steps()

    def take_slots(number):
        slots[0] += number
        return slots[0] - number

    def next_slot():
        service(take_slots(1))

    def with_weights(qkv, up, w_sems):
        load_qkv = pltpu.make_async_copy(qkv_weight, qkv, w_sems.at[0])
        load_up = pltpu.make_async_copy(up_weight, up, w_sems.at[1])
        pl.run_scoped(
            functools.partial(forward, qkv, up, load_up, load_qkv),
            pltpu.VMEM(down_weight.shape, BF16),
            pltpu.VMEM(dense_weight.shape, BF16),
            pltpu.VMEM((count, heads_width), BF16),
            pltpu.VMEM((count, heads_width), BF16),
            pltpu.VMEM((count, heads_width), F32),
            pltpu.VMEM((count, heads_width), F32),
            pltpu.VMEM((CHUNK, width), BF16),
            pltpu.VMEM((2, CHUNK, width), BF16),
            pltpu.VMEM((CHUNK, width), BF16),
            pltpu.VMEM((CHUNK, width), BF16),
            pltpu.VMEM((CHUNK, inner_width), BF16),
            pltpu.VMEM((CHUNK, inner_width), BF16),
            pltpu.VMEM((CHUNK, inner_width), F32),
            pltpu.VMEM((CHUNK, width), F32),
            pltpu.VMEM((local_heads, CHUNK, count), F32),
            pltpu.VMEM((CHUNK, heads_width), BF16),
            pltpu.VMEM((CHUNK, heads_width), BF16),
            pltpu.VMEM((CHUNK, heads_width), BF16),
            pltpu.SemaphoreType.DMA((2,)),
            pltpu.SemaphoreType.DMA((3,)),
            pltpu.SemaphoreType.DMA((5,)),
            pltpu.SemaphoreType.DMA((1,)),
        )
        spread_columns(DOWN, hidden, 2)
        spread_rows(UP, mlp_entry, hidden_grad, 1)
        first = take_slots(2 * steps)
        pl.run_scoped(
            lambda *scratch: backward(qkv, up, *scratch, first),
            pltpu.VMEM((2, CHUNK, inner_width), BF16),
            pltpu.VMEM((2, CHUNK, width), BF16),
            pltpu.VMEM((CHUNK, width), F32),
            pltpu.VMEM((CHUNK, width), F32),
            pltpu.SemaphoreType.DMA((2, 2)),
            pltpu.SemaphoreType.DMA((1,)),
        )

    pl.run_scoped(
        with_weights,
        pltpu.VMEM(qkv_weight.shape, BF16),
        pltpu.VMEM(up_weight.shape, BF16),
        pltpu.SemaphoreType.DMA((2,)),
    )

    def several(number):
        first = take_slots(number)

        @pl.loop(first, first + number)
        def _(k):
            service(k)

    def combines(number, stage):
        for side in range(2):
            combine(number, stage, side)
            next_slot()

    work = [
        functools.partial(spread_columns, DENSE, attended, 0),
        functools.partial(spread_rows, QKV, attn_entry, joined_grad, 2),
    ]
    for stage in range(1, bits):
        for number, pause in ((DOWN, 1), (UP, 2), (DENSE, 0), (QKV, 3)):
            work.append(functools.partial(combines, number, stage))
            if pause and (stage < bits - 1 or number in (DOWN, UP)):
                work.append(functools.partial(several, pause))
    done = 0
    for i, task in enumerate(work):
        while done * len(work) < (i + 1) * len(waiting) and done < len(waiting):
            waiting[done]()
            done += 1
        task()

    @pl.loop(slots[0], messages + half + LAG)
    def _(j):
        service(j)

    end_messages()
    for number in (DOWN, DENSE, UP, QKV):
        end_spread(number)
    store_vectors = fill(vectors, vectors_out, vec_send.at[0])
    store_vectors.start()
    store_vectors.wait()


def layer_call(mp_size, dp_size, operands):
    tokens, qkv, dense, up, down = (operands[i] for i in (0, 2, 3, 4, 5))
    count, width = tokens.shape
    inner_width, heads_width = up.shape[1], dense.shape[0]
    messages = 2 * (count // ROWS)
    bits = dp_size.bit_length() - 1
    owned = width // dp_size
    plans = (
        Spread(bits, owned, qkv.shape[1]),
        Spread(bits, heads_width, owned),
        Spread(bits, owned, inner_width),
        Spread(bits, inner_width, owned),
    )
    exchanges = bits + 2 * (mp_size // 2)
    vector_width = max(width, inner_width, qkv.shape[1])
    anywhere = pl.BlockSpec(memory_space=pl.ANY)
    vmem = pl.BlockSpec(memory_space=pltpu.VMEM)
    shape = jax.ShapeDtypeStruct
    out_shape = [
        shape((count, width), BF16),
        shape((count, width), BF16),
        shape((VECTORS, vector_width), F32),
        shape((2 * count, width), F32),
        *(shape((plan.rows, plan.cols), F32) for plan in plans),
        shape((count, width), BF16),
        shape((count, width), BF16),
        shape((count, heads_width), BF16),
        shape((count, inner_width), BF16),
        shape((count, inner_width), BF16),
    ]
    for plan in plans:
        out_shape += [shape(dims, F32) for dims in plan.shapes()]
    dma = pltpu.SemaphoreType.DMA
    scratch = [
        pltpu.VMEM((SLOTS, ROWS, width), F32),
        pltpu.VMEM((2 * SLOTS, ROWS, width), F32),
        pltpu.VMEM((2, ROWS, width), BF16),
        pltpu.VMEM((2, ROWS, width), BF16),
        pltpu.VMEM((2, ROWS, width), BF16),
        pltpu.VMEM((VECTORS, vector_width), F32),
        pltpu.VMEM((exchanges, VECTORS, vector_width), F32),
        pltpu.VMEM((count, qkv.shape[1]), BF16),
        pltpu.VMEM((count, LANES), F32),
        pltpu.VMEM((count, LANES), F32),
        dma((messages,)),
        dma((messages,)),
        dma((messages,)),
        dma((messages,)),
        dma((2,)),
        dma((2, 2)),
        dma((2,)),
        dma((exchanges,)),
        dma((exchanges,)),
    ]
    for plan in plans:
        scratch += [dma((plan.sems,)), dma((plan.sems,))]
    results = pl.pallas_call(
        functools.partial(layer_kernel, mp_size, plans),
        out_shape=tuple(out_shape),
        in_specs=[anywhere] * 6 + [vmem] * 7 + [pl.BlockSpec(memory_space=pltpu.SMEM)],
        out_specs=(anywhere,) * len(out_shape),
        scratch_shapes=scratch,
        compiler_params=pltpu.CompilerParams(
            collective_id=0, has_side_effects=True, vmem_limit_bytes=62 * 1024 * 1024
        ),
        cost_estimate=pl.CostEstimate(
            flops=6 * count * (width * (qkv.shape[1] + 2 * inner_width + heads_width)),
            bytes_accessed=300 << 20,
            transcendentals=0,
        ),
    )(*operands)
    return results[:3], results[4 : 4 + len(plans)]


def hand_out(dp_size, totals, *refs):
    refs = list(refs)
    vectors = refs.pop(0)
    number = (len(refs) - 1 - len(totals)) // 3
    sources, refs = refs[:number], refs[number:]
    targets, refs = refs[:number], refs[number:]
    pieces, refs = refs[: len(totals)], refs[len(totals) :]
    held, sems = refs[:number], refs[number]
    loads = [pltpu.make_async_copy(a, b, sems.at[0, i]) for i, (a, b) in enumerate(zip(sources, held))]
    stores = [pltpu.make_async_copy(a, b, sems.at[1, i]) for i, (a, b) in enumerate(zip(held, targets))]
    for copy in loads:
        copy.start()
    width = vectors.shape[1]
    for row, (total, piece) in enumerate(zip(totals, pieces)):
        size = total // dp_size
        shift = lax.rem(width - lax.axis_index("dp") * size, width)
        piece[...] = pltpu.roll(vectors[...], shift, 1)[row : row + 1, :size]
    for load, store in zip(loads, stores):
        load.wait()
        store.start()
    for copy in stores:
        copy.wait()


def hand_out_call(dp_size, totals, vectors, arrays):
    anywhere = pl.BlockSpec(memory_space=pl.ANY)
    vmem = pl.BlockSpec(memory_space=pltpu.VMEM)
    shape = jax.ShapeDtypeStruct
    results = pl.pallas_call(
        functools.partial(hand_out, dp_size, totals),
        out_shape=[shape(array.shape, array.dtype) for array in arrays]
        + [shape((1, total // dp_size), F32) for total in totals],
        in_specs=[vmem] + [anywhere] * len(arrays),
        out_specs=[anywhere] * len(arrays) + [vmem] * len(totals),
        scratch_shapes=[pltpu.VMEM(array.shape, array.dtype) for array in arrays]
        + [pltpu.SemaphoreType.DMA((2, len(arrays)))],
        compiler_params=pltpu.CompilerParams(vmem_limit_bytes=62 * 1024 * 1024),
    )(vectors, *arrays)
    return results[: len(arrays)], [piece[0] for piece in results[len(arrays) :]]


def per_device(
    mp_size,
    dp_size,
    tokens,
    lengths,
    attn_gain,
    attn_shift,
    mlp_gain,
    mlp_shift,
    qkv_weight,
    qkv_bias,
    dense_weight,
    up_weight,
    up_bias,
    down_weight,
    out_bias,
    cotangent,
):
    width = tokens.shape[1]
    (layer_output, input_grad, vectors), grads = layer_call(
        mp_size,
        dp_size,
        (
            tokens,
            cotangent,
            qkv_weight,
            dense_weight,
            up_weight,
            down_weight,
            attn_gain[None],
            attn_shift[None],
            mlp_gain[None],
            mlp_shift[None],
            qkv_bias[None],
            up_bias[None],
            out_bias[None],
            lengths,
        ),
    )
    totals = (width,) * 5 + (up_weight.shape[1], qkv_weight.shape[1])
    arrays, pieces = hand_out_call(dp_size, totals, vectors, (layer_output, input_grad, *grads))
    layer_output, input_grad, qkv_grad, dense_grad, up_grad, down_grad = arrays
    attn_gain_grad, attn_shift_grad, mlp_gain_grad, mlp_shift_grad = pieces[:4]
    return (
        layer_output,
        input_grad,
        attn_gain_grad,
        attn_shift_grad,
        mlp_gain_grad,
        mlp_shift_grad,
        qkv_grad,
        pieces[QKV_BIAS],
        dense_grad,
        up_grad,
        pieces[UP_BIAS],
        down_grad,
        pieces[OUT_BIAS],
    )


def solution(mesh):
    in_specs = (
        P("dp", None),
        P("dp", None),
        P(),
        P(),
        P(),
        P(),
        P(None, "mp"),
        P("mp"),
        P("mp", None),
        P(None, "mp"),
        P("mp"),
        P("mp", None),
        P(),
        P("dp", None),
    )
    out_specs = (
        P("dp", None),
        P("dp", None),
        P("dp"),
        P("dp"),
        P("dp"),
        P("dp"),
        P("dp", "mp"),
        P(("mp", "dp")),
        P("mp", "dp"),
        P("dp", "mp"),
        P(("mp", "dp")),
        P("mp", "dp"),
        P("dp"),
    )
    function = functools.partial(per_device, mesh.shape["mp"], mesh.shape["dp"])
    return jax.shard_map(
        function, mesh=mesh, in_specs=in_specs, out_specs=out_specs, check_vma=False
    )
```

```python
import functools
import math

import jax
import jax.numpy as jnp
from jax import lax
from jax.experimental import pallas as pl
from jax.experimental.pallas import tpu as pltpu
from jax.sharding import PartitionSpec as P

HEAD_DIM = 256
ROT = 64
EPSILON = 1e-05
LANES = 128

MESH = pl.DeviceIdType.MESH
ROWS = 32
SLOTS = 10
AHEAD = 5
AHEAD_ODD = 5
PENDING = 3
LAG = 1
CHUNK = 256
BLOCK = 32

F32 = jnp.float32
BF16 = jnp.bfloat16

VECTORS = 8
ATTN_GAIN, ATTN_SHIFT, MLP_GAIN, MLP_SHIFT, OUT_BIAS, UP_BIAS, QKV_BIAS = range(7)


def sine_cosine(angle):
    turns = jnp.floor(angle * (2.0 / math.pi) + 0.5)
    rest = angle - turns * 1.5703125 - turns * 4.837512969970703e-4 - turns * 7.549789954891882e-8
    square = rest * rest
    sine = rest + rest * square * (
        -1.6666654611e-1 + square * (8.3321608736e-3 - square * 1.9515295891e-4)
    )
    cosine = (
        1.0
        - 0.5 * square
        + square
        * square
        * (4.166664568298827e-2 + square * (-1.388731625493765e-3 + square * 2.443315711809948e-5))
    )
    quarter = turns - 4.0 * jnp.floor(turns * 0.25)
    odd = (quarter == 1.0) | (quarter == 3.0)
    flip_sine = quarter >= 2.0
    flip_cosine = (quarter == 1.0) | (quarter == 2.0)
    near_sine = jnp.where(odd, cosine, sine)
    near_cosine = jnp.where(odd, sine, cosine)
    return (
        jnp.where(flip_sine, -near_sine, near_sine),
        jnp.where(flip_cosine, -near_cosine, near_cosine),
    )


def rotary_tables(place, start):
    lane = lax.broadcasted_iota(jnp.int32, place.shape, 1)
    half = ROT // 2
    step = jnp.where(lane < half, lane, lane - half).astype(F32)
    freqs = jnp.exp(step * (-2.0 * math.log(10000.0) / ROT))
    sine, cosine = sine_cosine((place - start).astype(F32) * freqs)
    cosine = jnp.where(lane < ROT, cosine, 1.0)
    sine = jnp.where(lane < half, -sine, jnp.where(lane < ROT, sine, 0.0))
    return cosine, sine


def normalize(rows):
    centred = rows - jnp.mean(rows, axis=-1, keepdims=True)
    factor = lax.rsqrt(jnp.mean(centred * centred, axis=-1, keepdims=True) + EPSILON)
    return centred * factor, factor


def gelu_parts(v):
    cdf = 0.5 + 0.5 * lax.erf(v * math.sqrt(0.5))
    return v * cdf, cdf + v * jnp.exp(-0.5 * v * v) * (1.0 / math.sqrt(2.0 * math.pi))


def dot(left, right):
    return jnp.dot(left, right, preferred_element_type=F32)


def dot_cols(left, right):
    return lax.dot_general(left, right, (((1,), (1,)), ((), ())), preferred_element_type=F32)


def dot_rows(left, right):
    return lax.dot_general(left, right, (((0,), (0,)), ((), ())), preferred_element_type=F32)


def column_sum(x):
    return jnp.sum(x, axis=0, keepdims=True)


def span(start, size):
    return pl.ds(pl.multiple_of(start, size), size)


class Spread:
    def __init__(self, bits, rows, cols):
        self.bits, self.rows, self.cols = bits, rows, cols
        self.tiles = 1 << bits
        self.orders = ([0] + list(range(1, bits)), [0] + list(range(bits - 1, 0, -1)))
        count = self.tiles // 2
        self.first = {}
        for stage in range(1, bits):
            for side in range(2):
                self.first[stage, side] = count
                count += self.tiles >> (stage + 1)
        self.sems = count

    def masks(self, side, stage):
        order = self.orders[side]
        return [m for m in range(self.tiles) if not any((m >> b) & 1 for b in order[:stage])]

    def place(self, mask, side, stage):
        return self.masks(side, stage + 1).index(mask)

    def shapes(self):
        shapes = [(self.tiles // 2, self.rows, self.cols)]
        for stage in range(self.bits):
            shapes.append((self.tiles >> (stage + 1), self.rows, self.cols))
        return shapes


def layer_kernel(mp_size, plans, *refs):
    refs = list(refs)

    def take(number):
        taken = refs[:number]
        del refs[:number]
        return taken

    tokens, cotangent, qkv_weight, dense_weight, up_weight, down_weight = take(6)
    attn_gain, attn_shift, mlp_gain, mlp_shift, qkv_bias, up_bias, out_bias = take(7)
    lengths = take(1)[0]
    layer_out, input_grad, vectors_out, parts = take(4)
    grads_out = take(len(plans))
    attn_entry, mlp_entry, attended, hidden, hidden_grad = take(5)
    spreads = [(plan, take(1 + plan.bits)) for plan in plans]
    from_outer, held, token_rows, cot_rows, out_rows = take(5)
    vectors, vectors_in, joined_grad, cosine, sine = take(5)
    send_in, send_out, recv_outer, recv_inner, part_sems, row_sems, out_sems = take(7)
    vec_send, vec_recv = take(2)
    spread_sems = [take(2) for _ in plans]

    count, width = tokens.shape
    inner_width = up_weight.shape[1]
    heads_width = dense_weight.shape[0]
    local_heads = heads_width // HEAD_DIM
    bits = plans[0].bits
    steps = count // CHUNK
    scale = 1.0 / math.sqrt(HEAD_DIM)
    branch_messages = count // ROWS
    messages = 2 * branch_messages
    chunk_messages = CHUNK // ROWS
    half = mp_size // 2

    index = lax.axis_index("mp")
    upper = index // half
    level = index * (1 - upper) + (mp_size - 1 - index) * upper
    inner = index + 1 - 2 * upper
    outer = index - 1 + 2 * upper
    lag = half - level + LAG
    ahead = min(AHEAD, SLOTS - 1 - LAG - half)
    is_middle = level == half - 1
    total_place = (1 - level // (half - 1)) * SLOTS if half > 1 else 0
    device = lax.axis_index("dp")
    ahead = ahead + (device % 2) * (min(AHEAD_ODD, SLOTS - 1 - LAG - half) - ahead)

    def partner(bit):
        return device + (1 - 2 * ((device // (1 << bit)) % 2)) * (1 << bit)

    def owner(mask):
        total = 0
        for bit in range(bits):
            total = total + ((device // (1 << bit) + mask // (1 << bit)) % 2) * (1 << bit)
        return total

    def meet():
        barrier = pltpu.get_barrier_semaphore()
        pl.semaphore_signal(barrier, inc=1, device_id={"mp": inner}, device_id_type=MESH)
        for bit in range(bits):
            pl.semaphore_signal(barrier, inc=1, device_id={"dp": partner(bit)}, device_id_type=MESH)
        if half > 1:

            @pl.when(level > 0)
            def _():
                pl.semaphore_signal(barrier, inc=1, device_id={"mp": outer}, device_id_type=MESH)
                pl.semaphore_wait(barrier, 2 + bits)

            @pl.when(level == 0)
            def _():
                pl.semaphore_wait(barrier, 1 + bits)

        else:
            pl.semaphore_wait(barrier, 1 + bits)


    def slot(ref, k):
        return ref.at[lax.rem(k, SLOTS)]

    def sums(k):
        return held.at[lax.rem(k, SLOTS)]

    def from_inner(k):
        return held.at[lax.rem(k, SLOTS) + SLOTS]

    def totals(k):
        return held.at[lax.rem(k, SLOTS) + total_place]

    def message(ref, k):
        return ref.at[span(k * ROWS, ROWS)]

    def to_inner(k, source, landing, sem):
        return pltpu.make_async_remote_copy(
            src_ref=source,
            dst_ref=landing,
            send_sem=send_in.at[k],
            recv_sem=sem.at[k],
            device_id={"mp": inner},
            device_id_type=MESH,
        )

    def to_outer(k):
        return pltpu.make_async_remote_copy(
            src_ref=totals(k),
            dst_ref=from_inner(k),
            send_sem=send_out.at[k],
            recv_sem=recv_inner.at[k],
            device_id={"mp": outer},
            device_id_type=MESH,
        )

    def load_part(k):
        return pltpu.make_async_copy(message(parts, k), sums(k), part_sems.at[lax.rem(k, 2)])

    def load_rows(k):
        row, place = lax.rem(k, branch_messages), lax.rem(k, 2)
        return [
            pltpu.make_async_copy(
                message(tokens, row), token_rows.at[place], row_sems.at[0, place]
            ),
            pltpu.make_async_copy(
                message(cotangent, row), cot_rows.at[place], row_sems.at[1, place]
            ),
        ]

    def store_rows(k, target):
        place = lax.rem(k, 2)
        return pltpu.make_async_copy(
            out_rows.at[place], message(target, lax.rem(k, branch_messages)), out_sems.at[place]
        )

    def send_ahead(k):
        if half > 1:

            @pl.when((level == 0) & (k < messages))
            def _():
                to_inner(k, message(parts, k), slot(from_outer, k), recv_outer).start()

    def begin_messages():
        @pl.loop(0, ahead)
        def _(k):
            send_ahead(k)

        for copy in load_rows(0):
            copy.start()
        if half > 1:

            @pl.when(level > 0)
            def _():
                load_part(0).start()

        else:
            load_part(0).start()

    def add_inward(j):
        @pl.when(j < messages)
        def _():
            load_part(j).wait()

            @pl.when(j + 1 < messages)
            def _():
                load_part(j + 1).start()

            mine = sums(j)
            if half > 1:
                to_inner(j, mine, slot(from_outer, j), recv_outer).wait_recv()
                mine[...] += slot(from_outer, j)[...]

            @pl.when(is_middle)
            def _():
                to_inner(j, mine, from_inner(j), recv_inner).start()

            if half > 2:

                @pl.when(level < half - 1)
                def _():
                    to_inner(j, mine, slot(from_outer, j), recv_outer).start()

    def finish(k):
        place = lax.rem(k, 2)
        source = totals(k)

        @pl.when(k < branch_messages)
        def _():
            @pl.loop(0, ROWS // BLOCK)
            def _(b):
                rows = span(b * BLOCK, BLOCK)
                out_rows[place, rows] = (
                    token_rows[place, rows].astype(F32) + source[rows] + out_bias[...]
                ).astype(BF16)

        @pl.when(k >= branch_messages)
        def _():
            @pl.loop(0, ROWS // BLOCK)
            def _(b):
                rows = span(b * BLOCK, BLOCK)
                hat, factor = normalize(token_rows[place, rows].astype(F32))
                entry = source[rows]
                part = (
                    entry
                    - jnp.mean(entry, axis=-1, keepdims=True)
                    - hat * jnp.mean(entry * hat, axis=-1, keepdims=True)
                )
                out_rows[place, rows] = (
                    cot_rows[place, rows].astype(F32) + factor * part
                ).astype(BF16)

    def pass_outward(k):
        @pl.when((k >= 0) & (k < messages))
        def _():
            to_inner(k, sums(k), from_inner(k), recv_inner).wait()

            @pl.when(is_middle)
            def _():
                sums(k)[...] += from_inner(k)[...]

            if half > 1:

                @pl.when(level > 0)
                def _():
                    @pl.when(k >= PENDING)
                    def _():
                        to_outer(k - PENDING).wait_send()

                    to_outer(k).start()

            @pl.when(k + 1 < messages)
            def _():
                for copy in load_rows(k + 1):
                    copy.start()

            for copy in load_rows(k):
                copy.wait()

            @pl.when(k >= 2)
            def _():
                store_rows(k - 2, layer_out).wait()

            finish(k)

            @pl.when(k < branch_messages)
            def _():
                store_rows(k, layer_out).start()

            @pl.when(k >= branch_messages)
            def _():
                store_rows(k, input_grad).start()

    def service(j):
        send_ahead(j + ahead)
        if half > 1:

            @pl.when(level > 0)
            def _():
                add_inward(j)

        else:
            add_inward(j)
        pass_outward(j - lag)

    def end_messages():
        if half > 1:

            @pl.when(level > 0)
            def _():
                for k in range(messages - PENDING, messages):
                    to_outer(k).wait_send()

        for k in (messages - 2, messages - 1):
            store_rows(k, input_grad).wait()


    def spread_copy(number, stage, side, source, target, sem, bit):
        sends, recvs = spread_sems[number]
        return pltpu.make_async_remote_copy(
            src_ref=source,
            dst_ref=target,
            send_sem=sends.at[sem],
            recv_sem=recvs.at[sem],
            device_id={"dp": partner(bit)},
            device_id_type=MESH,
        )

    def side_rows(plan, side):
        return pl.ds(side * (plan.rows // 2), plan.rows // 2)

    def stage_copies(number, stage, side):
        plan, buffers = spreads[number]
        keep, landing = buffers[0], buffers[1 + stage]
        bit = plan.orders[side][stage]
        copies = []
        for mask in plan.masks(side, stage):
            if (mask >> bit) & 1:
                place = plan.place(mask ^ (1 << bit), side, stage)
                copies.append(
                    spread_copy(
                        number,
                        stage,
                        side,
                        keep.at[mask // 2, side_rows(plan, side)],
                        landing.at[place, side_rows(plan, side)],
                        plan.first[stage, side] + place,
                        bit,
                    )
                )
        return copies

    def tiles_of(number, compute, sent, kept, landed, sems, first, each):
        plan, buffers = spreads[number]
        half_tiles = plan.tiles // 2
        every = max(1, half_tiles // 4)

        def copy(i):
            return spread_copy(number, 0, 0, sent.at[lax.rem(i, 2)], buffers[1].at[i], i, 0)

        def load(i):
            return pltpu.make_async_copy(buffers[1].at[i], landed, sems.at[0])

        def store(i):
            return pltpu.make_async_copy(
                kept.at[lax.rem(i, 2)], buffers[0].at[i], sems.at[1 + lax.rem(i, 2)]
            )

        def begin_add(i):
            copy(i).wait_recv()
            load(i).start()

        def end_add(i):
            load(i).wait()
            kept.at[lax.rem(i, 2)][...] += landed[...]
            store(i).start()

        @pl.loop(0, half_tiles)
        def _(i):
            @pl.when(i >= 2)
            def _():
                copy(i - 2).wait_send()

            compute(owner(2 * i + 1), sent.at[lax.rem(i, 2)])
            copy(i).start()

            @pl.when(i >= 1)
            def _():
                begin_add(i - 1)

            if each == 2:

                @pl.when(lax.rem(i, every) == every - 1)
                def _():
                    service(first + 2 * (i // every))

            @pl.when(i >= 2)
            def _():
                store(i - 2).wait()

            compute(owner(2 * i), kept.at[lax.rem(i, 2)])

            @pl.when(i >= 1)
            def _():
                end_add(i - 1)

            if each >= 1:

                @pl.when(lax.rem(i, every) == every - 1)
                def _():
                    service(first + each * (i // every) + each - 1)

        begin_add(half_tiles - 1)
        end_add(half_tiles - 1)
        for i in (half_tiles - 2, half_tiles - 1):
            copy(i).wait_send()
            store(i).wait()
        for side in range(2):
            for copies in stage_copies(number, 1, side):
                copies.start()

    def combine(number, stage, side):
        plan, buffers = spreads[number]
        keep, landing = buffers[0], buffers[1 + stage]
        last = stage == bits - 1
        rows = plan.rows // 4

        masks = plan.masks(side, stage + 1)

        def run(mine, other, sems):
            for copy in stage_copies(number, stage, side):
                copy.wait_recv()
            loads, stores = [], []
            for mask in masks:
                place = plan.place(mask, side, stage)
                for piece in range(2):
                    there = pl.ds(side * (plan.rows // 2) + piece * rows, rows)
                    at = len(loads)
                    kept = keep.at[mask // 2, there]
                    loads.append(
                        [
                            pltpu.make_async_copy(kept, mine.at[at], sems.at[0, at]),
                            pltpu.make_async_copy(
                                landing.at[place, there], other.at[at], sems.at[1, at]
                            ),
                        ]
                    )
                    target = grads_out[number].at[there] if last else kept
                    stores.append(pltpu.make_async_copy(mine.at[at], target, sems.at[2, at]))
            for load in loads:
                for copy in load:
                    copy.start()
            for i, (load, store) in enumerate(zip(loads, stores)):
                for copy in load:
                    copy.wait()
                mine[i] += other[i]
                store.start()
            for store in stores:
                store.wait()
            if not last:
                for copy in stage_copies(number, stage + 1, side):
                    copy.start()

        pieces = 2 * len(masks)
        shape = (pieces, rows, plan.cols)
        pl.run_scoped(
            run,
            pltpu.VMEM(shape, F32),
            pltpu.VMEM(shape, F32),
            pltpu.SemaphoreType.DMA((3, pieces)),
        )

    def end_spread(number):
        plan, _ = spreads[number]
        for side in range(2):
            for stage in range(1, bits):
                for copy in stage_copies(number, stage, side):
                    copy.wait_send()


    def vector_copy(place, device_id):
        return pltpu.make_async_remote_copy(
            src_ref=vectors,
            dst_ref=vectors_in.at[place],
            send_sem=vec_send.at[place],
            recv_sem=vec_recv.at[place],
            device_id=device_id,
            device_id_type=MESH,
        )

    norms = pl.ds(0, 4)

    def inward_hop(hop):
        return vector_copy(bits + hop, {"mp": inner})

    def outward_hop(hop):
        return vector_copy(bits + half + hop, {"mp": outer})

    def vector_steps():
        steps = []

        def start_inward(hop):
            @pl.when(level == hop)
            def _():
                inward_hop(hop).start()

        def end_inward(hop):
            @pl.when(level == hop)
            def _():
                inward_hop(hop).wait_send()

            if hop < half - 1:

                @pl.when(level == hop + 1)
                def _():
                    inward_hop(hop).wait_recv()
                    vectors[norms] += vectors_in[bits + hop, norms]

            else:

                @pl.when(is_middle)
                def _():
                    inward_hop(hop).wait_recv()
                    vectors[norms] += vectors_in[bits + hop, norms]

        def start_outward(hop):
            @pl.when(level == hop + 1)
            def _():
                outward_hop(hop).start()

        def end_outward(hop):
            @pl.when(level == hop + 1)
            def _():
                outward_hop(hop).wait_send()

            @pl.when(level == hop)
            def _():
                outward_hop(hop).wait_recv()
                vectors[norms] = vectors_in[bits + half + hop, norms]

        def start_across(bit):
            vector_copy(bit, {"dp": partner(bit)}).start()

        def end_across(bit):
            vector_copy(bit, {"dp": partner(bit)}).wait()
            vectors[...] += vectors_in[bit]

        moves = [
            (functools.partial(start_inward, hop), functools.partial(end_inward, hop))
            for hop in range(half)
        ]
        moves += [
            (functools.partial(start_outward, hop), functools.partial(end_outward, hop))
            for hop in reversed(range(half - 1))
        ]
        moves += [
            (functools.partial(start_across, bit), functools.partial(end_across, bit))
            for bit in range(bits)
        ]

        def step(i):
            if i > 0:
                moves[i - 1][1]()
            if i < len(moves):
                moves[i][0]()

        return [functools.partial(step, i) for i in range(len(moves) + 1)]


    first_lanes = lax.broadcasted_iota(jnp.int32, (CHUNK, LANES), 1)

    def swap_halves(x):
        return jnp.where(
            first_lanes < ROT // 2,
            pltpu.roll(x, LANES - ROT // 2, 1),
            pltpu.roll(x, ROT // 2, 1),
        )

    def turn(x, rows, sign):
        low = x[:, :LANES]
        low = low * cosine[rows] + sign * swap_halves(low) * sine[rows]
        return jnp.concatenate([low, x[:, LANES:]], axis=1)

    def store_part(c, part, sem):
        copy = pltpu.make_async_copy(part, parts.at[span(c * CHUNK, CHUNK)], sem)
        copy.start()
        copy.wait()

    def forward(
        qkv,
        up,
        load_up,
        load_qkv,
        down,
        dense,
        keys,
        values,
        key_grad,
        value_grad,
        token_chunk,
        cot_chunk,
        attn_chunk,
        mlp_chunk,
        hidden_chunk,
        hidden_grad_chunk,
        slope,
        part,
        probs,
        queries,
        attended_chunk,
        attended_grad,
        w_sems,
        in_sems,
        out_chunk_sems,
        part_sem,
    ):
        load_down = pltpu.make_async_copy(down_weight, down, w_sems.at[0])
        load_dense = pltpu.make_async_copy(dense_weight, dense, w_sems.at[1])
        tile = min(512, inner_width)
        wide = min(512, width)

        def load_tokens(c):
            return pltpu.make_async_copy(
                tokens.at[span(c * CHUNK, CHUNK)], token_chunk, in_sems.at[0]
            )

        def load_cot(c):
            return pltpu.make_async_copy(
                cotangent.at[span(c * CHUNK, CHUNK)],
                cot_chunk.at[lax.rem(c, 2)],
                in_sems.at[1 + lax.rem(c, 2)],
            )

        def chunk_stores(c):
            pairs = (
                (attn_chunk, attn_entry),
                (mlp_chunk, mlp_entry),
                (attended_chunk, attended),
                (hidden_chunk, hidden),
                (hidden_grad_chunk, hidden_grad),
            )
            return [
                pltpu.make_async_copy(
                    source, target.at[span(c * CHUNK, CHUNK)], out_chunk_sems.at[i]
                )
                for i, (source, target) in enumerate(pairs)
            ]

        load_tokens(0).start()
        load_qkv.start()
        load_up.start()
        load_down.start()
        load_dense.start()
        load_cot(0).start()
        meet()
        keys[...] = jnp.zeros_like(keys)
        values[...] = jnp.zeros_like(values)
        key_grad[...] = jnp.zeros_like(key_grad)
        value_grad[...] = jnp.zeros_like(value_grad)
        vectors[...] = jnp.zeros_like(vectors)

        def by_extent(c, function):
            low = 0
            while low < steps:
                high = min(steps, max(2 * low, 1))

                @pl.when((c >= low) & (c < high))
                def _():
                    function(high * CHUNK)

                low = high

        @pl.loop(0, steps)
        def _(c):
            rows = span(c * CHUNK, CHUNK)
            cot = cot_chunk.at[lax.rem(c, 2)]
            load_tokens(c).wait()

            @pl.when(c > 0)
            def _():
                for copy in chunk_stores(c - 1):
                    copy.wait()

            @pl.loop(0, CHUNK // BLOCK)
            def _(b):
                block = span(b * BLOCK, BLOCK)
                hat, _ = normalize(token_chunk[block].astype(F32))
                attn_chunk[block] = (hat * attn_gain[...] + attn_shift[...]).astype(BF16)
                mlp_chunk[block] = (hat * mlp_gain[...] + mlp_shift[...]).astype(BF16)

            @pl.when(c + 1 < steps)
            def _():
                load_tokens(c + 1).start()
                load_cot(c + 1).start()

            @pl.when(c == 0)
            def _():
                load_qkv.wait()

            spot = lax.broadcasted_iota(jnp.int32, (CHUNK, LANES), 0) + c * CHUNK
            begin = jnp.zeros((CHUNK, LANES), jnp.int32)
            end = jnp.int32(0)
            for i in range(lengths.shape[1]):
                end = end + lengths[0, i]
                begin = jnp.where(spot >= end, end, begin)
            cosine[rows], sine[rows] = rotary_tables(spot, begin)

            for h in range(local_heads):
                cols = slice(h * HEAD_DIM, (h + 1) * HEAD_DIM)
                base = h * 3 * HEAD_DIM

                def joined(i):
                    there = slice(base + i * HEAD_DIM, base + (i + 1) * HEAD_DIM)
                    return dot(attn_chunk[...], qkv[:, there]) + qkv_bias[:, there]

                queries[:, cols] = turn(joined(0), rows, 1.0).astype(BF16)
                keys[rows, cols] = turn(joined(1), rows, 1.0).astype(BF16)
                values[rows, cols] = joined(2).astype(BF16)

            def attend(extent):
                place = lax.broadcasted_iota(jnp.int32, (CHUNK, extent), 1)
                here = lax.broadcasted_iota(jnp.int32, (CHUNK, extent), 0) + c * CHUNK
                allowed = (place >= begin[:, :1]) & (place <= here)
                for h in range(local_heads):
                    cols = slice(h * HEAD_DIM, (h + 1) * HEAD_DIM)
                    scores = dot_cols(queries[:, cols], keys[:extent, cols]) * scale
                    scores = jnp.where(allowed, scores, -1e30)
                    expo = jnp.exp(scores - jnp.max(scores, axis=-1, keepdims=True))
                    prob = expo * (1.0 / jnp.sum(expo, axis=-1, keepdims=True))
                    probs[h, :, :extent] = prob
                    attended_chunk[:, cols] = dot(prob.astype(BF16), values[:extent, cols]).astype(
                        BF16
                    )

            by_extent(c, attend)

            @pl.when(c > 0)
            def _():
                service(c * 4 - 2)

            @pl.when(c == 0)
            def _():
                load_up.wait()

            @pl.loop(0, inner_width // tile)
            def _(t):
                cols = span(t * tile, tile)
                pre = dot(mlp_chunk[...], up[:, cols]) + up_bias[:, cols]
                value, derivative = gelu_parts(pre)
                hidden_chunk[:, cols] = value.astype(BF16)
                slope[:, cols] = derivative

            @pl.when(c == 0)
            def _():
                load_down.wait()
                load_dense.wait()

            @pl.loop(0, width // wide)
            def _(t):
                cols = span(t * wide, wide)
                part[:, cols] = dot(hidden_chunk[...], down[:, cols]) + dot(
                    attended_chunk[...], dense[:, cols]
                )

            store_part(c, part, part_sem.at[0])

            @pl.when(c == 0)
            def _():
                begin_messages()

            @pl.when(c > 0)
            def _():
                service(c * 4 - 1)

            load_cot(c).wait()

            @pl.loop(0, inner_width // tile)
            def _(t):
                cols = span(t * tile, tile)
                grad = (slope[:, cols] * dot_cols(cot[...], down[cols, :])).astype(BF16)
                hidden_grad_chunk[:, cols] = grad
                vectors[UP_BIAS : UP_BIAS + 1, cols] += column_sum(grad.astype(F32))

            for copy in chunk_stores(c):
                copy.start()

            service(c * 4)
            attended_grad[...] = dot_cols(cot[...], dense[...]).astype(BF16)

            def attend_back(extent):
                for h in range(local_heads):
                    cols = slice(h * HEAD_DIM, (h + 1) * HEAD_DIM)
                    base = h * 3 * HEAD_DIM
                    grad = attended_grad[:, cols]
                    prob = probs[h, :, :extent]
                    prob_grad = dot_cols(grad, values[:extent, cols])
                    along = jnp.sum(prob * prob_grad, axis=-1, keepdims=True)
                    score_grad = (prob * (prob_grad - along)).astype(BF16)
                    query_grad = dot(score_grad, keys[:extent, cols]) * scale
                    joined_grad[rows, base : base + HEAD_DIM] = turn(query_grad, rows, -1.0).astype(
                        BF16
                    )
                    key_grad[:extent, cols] += dot_rows(score_grad, queries[:, cols]) * scale
                    value_grad[:extent, cols] += dot_rows(prob.astype(BF16), grad)

            by_extent(c, attend_back)

            @pl.loop(0, CHUNK // BLOCK)
            def _(b):
                block = span(b * BLOCK, BLOCK)
                vectors[OUT_BIAS : OUT_BIAS + 1, :width] += column_sum(cot[block].astype(F32))

            service(c * 4 + 1)

        for copy in chunk_stores(steps - 1):
            copy.wait()

        @pl.loop(0, steps)
        def _(c):
            rows = span(c * CHUNK, CHUNK)
            for h in range(local_heads):
                cols = slice(h * HEAD_DIM, (h + 1) * HEAD_DIM)
                base = h * 3 * HEAD_DIM
                joined_grad[rows, base + HEAD_DIM : base + 2 * HEAD_DIM] = turn(
                    key_grad[rows, cols], rows, -1.0
                ).astype(BF16)
                joined_grad[rows, base + 2 * HEAD_DIM : base + 3 * HEAD_DIM] = value_grad[
                    rows, cols
                ].astype(BF16)

    def backward(qkv, up, grad_chunk, token_chunk, hat, part, in_sems, part_sem, first_slot):
        wide = min(512, width)

        def loads(c):
            rows = span(c * CHUNK, CHUNK)
            return [
                pltpu.make_async_copy(
                    hidden_grad.at[rows], grad_chunk.at[lax.rem(c, 2)], in_sems.at[lax.rem(c, 2), 0]
                ),
                pltpu.make_async_copy(
                    tokens.at[rows], token_chunk.at[lax.rem(c, 2)], in_sems.at[lax.rem(c, 2), 1]
                ),
            ]

        for copy in loads(0):
            copy.start()

        @pl.loop(0, steps)
        def _(c):
            rows = span(c * CHUNK, CHUNK)
            for copy in loads(c):
                copy.wait()

            @pl.when(c + 1 < steps)
            def _():
                for copy in loads(c + 1):
                    copy.start()

            @pl.loop(0, CHUNK // BLOCK)
            def _(b):
                block = span(b * BLOCK, BLOCK)
                hat[block] = normalize(token_chunk[lax.rem(c, 2), block].astype(F32))[0]

            vectors[QKV_BIAS : QKV_BIAS + 1, : 3 * heads_width] += column_sum(
                joined_grad[rows].astype(F32)
            )

            @pl.loop(0, width // wide)
            def _(t):
                cols = span(t * wide, wide)
                attn_grad = dot_cols(joined_grad[rows], qkv[cols, :])
                mlp_grad = dot_cols(grad_chunk[lax.rem(c, 2)], up[cols, :])
                part[:, cols] = attn_grad * attn_gain[:, cols] + mlp_grad * mlp_gain[:, cols]
                near = hat[:, cols]
                for row, value in (
                    (ATTN_GAIN, attn_grad * near),
                    (ATTN_SHIFT, attn_grad),
                    (MLP_GAIN, mlp_grad * near),
                    (MLP_SHIFT, mlp_grad),
                ):
                    vectors[row : row + 1, cols] += column_sum(value)

                @pl.when(t == width // wide // 2 - 1)
                def _():
                    service(first_slot + 2 * c)

            store_part(steps + c, part, part_sem.at[0])
            service(first_slot + 2 * c + 1)

    def fill(source, target, sem):
        return pltpu.make_async_copy(source, target, sem)

    def spread_columns(number, left_source, each):
        plan, _ = spreads[number]
        depth = left_source.shape[1]

        def run(left, turned, right, sent, kept, landed, sems):
            loads = [fill(left_source, left, sems.at[0]), fill(cotangent, right, sems.at[1])]
            for copy in loads:
                copy.start()
            for copy in loads:
                copy.wait()

            @pl.loop(0, depth // HEAD_DIM)
            def _(b):
                there = span(b * HEAD_DIM, HEAD_DIM)
                turned[there, :] = left[:, there].T

            def compute(where, target):
                right_cols = right[:, span(where * plan.cols, plan.cols)]
                block = min(512, depth)

                @pl.loop(0, depth // block)
                def _(b):
                    there = span(b * block, block)
                    target[there, :] = dot(turned[there, :], right_cols)

            tiles_of(number, compute, sent, kept, landed, sems, take_slots(4 * each), each)
            if not each:
                next_slot()

        pl.run_scoped(
            run,
            pltpu.VMEM((count, depth), BF16),
            pltpu.VMEM((depth, count), BF16),
            pltpu.VMEM((count, width), BF16),
            pltpu.VMEM((2, plan.rows, plan.cols), F32),
            pltpu.VMEM((2, plan.rows, plan.cols), F32),
            pltpu.VMEM((plan.rows, plan.cols), F32),
            pltpu.SemaphoreType.DMA((3,)),
        )

    def spread_rows(number, left_source, right_source, each):
        plan, _ = spreads[number]
        resident = right_source is joined_grad

        def run(left, right, sent, kept, landed, sems):
            loads = [fill(left_source, left, sems.at[0])]
            if not resident:
                loads.append(fill(right_source, right, sems.at[1]))
            for copy in loads:
                copy.start()
            for copy in loads:
                copy.wait()
            use = joined_grad if resident else right

            def compute(where, target):
                turned = left[:, span(where * plan.rows, plan.rows)].T
                block = min(512, plan.cols)

                @pl.loop(0, plan.cols // block)
                def _(b):
                    there = span(b * block, block)
                    target[:, there] = dot(turned, use[:, there])

            tiles_of(number, compute, sent, kept, landed, sems, take_slots(4 * each), each)

        pl.run_scoped(
            run,
            pltpu.VMEM((count, width), BF16),
            pltpu.VMEM((16, LANES) if resident else (count, plan.cols), BF16),
            pltpu.VMEM((2, plan.rows, plan.cols), F32),
            pltpu.VMEM((2, plan.rows, plan.cols), F32),
            pltpu.VMEM((plan.rows, plan.cols), F32),
            pltpu.SemaphoreType.DMA((3,)),
        )

    QKV, DENSE, UP, DOWN = range(4)
    slots = [4 * steps - 2]
    waiting = vector_steps()

    def take_slots(number):
        slots[0] += number
        return slots[0] - number

    def next_slot():
        service(take_slots(1))

    def with_weights(qkv, up, w_sems):
        load_qkv = pltpu.make_async_copy(qkv_weight, qkv, w_sems.at[0])
        load_up = pltpu.make_async_copy(up_weight, up, w_sems.at[1])
        pl.run_scoped(
            functools.partial(forward, qkv, up, load_up, load_qkv),
            pltpu.VMEM(down_weight.shape, BF16),
            pltpu.VMEM(dense_weight.shape, BF16),
            pltpu.VMEM((count, heads_width), BF16),
            pltpu.VMEM((count, heads_width), BF16),
            pltpu.VMEM((count, heads_width), F32),
            pltpu.VMEM((count, heads_width), F32),
            pltpu.VMEM((CHUNK, width), BF16),
            pltpu.VMEM((2, CHUNK, width), BF16),
            pltpu.VMEM((CHUNK, width), BF16),
            pltpu.VMEM((CHUNK, width), BF16),
            pltpu.VMEM((CHUNK, inner_width), BF16),
            pltpu.VMEM((CHUNK, inner_width), BF16),
            pltpu.VMEM((CHUNK, inner_width), F32),
            pltpu.VMEM((CHUNK, width), F32),
            pltpu.VMEM((local_heads, CHUNK, count), F32),
            pltpu.VMEM((CHUNK, heads_width), BF16),
            pltpu.VMEM((CHUNK, heads_width), BF16),
            pltpu.VMEM((CHUNK, heads_width), BF16),
            pltpu.SemaphoreType.DMA((2,)),
            pltpu.SemaphoreType.DMA((3,)),
            pltpu.SemaphoreType.DMA((5,)),
            pltpu.SemaphoreType.DMA((1,)),
        )
        spread_columns(DOWN, hidden, 2)
        spread_rows(UP, mlp_entry, hidden_grad, 1)
        first = take_slots(2 * steps)
        pl.run_scoped(
            lambda *scratch: backward(qkv, up, *scratch, first),
            pltpu.VMEM((2, CHUNK, inner_width), BF16),
            pltpu.VMEM((2, CHUNK, width), BF16),
            pltpu.VMEM((CHUNK, width), F32),
            pltpu.VMEM((CHUNK, width), F32),
            pltpu.SemaphoreType.DMA((2, 2)),
            pltpu.SemaphoreType.DMA((1,)),
        )

    pl.run_scoped(
        with_weights,
        pltpu.VMEM(qkv_weight.shape, BF16),
        pltpu.VMEM(up_weight.shape, BF16),
        pltpu.SemaphoreType.DMA((2,)),
    )

    def several(number):
        first = take_slots(number)

        @pl.loop(first, first + number)
        def _(k):
            service(k)

    def combines(number, stage):
        for side in range(2):
            combine(number, stage, side)
            next_slot()

    work = [
        functools.partial(spread_columns, DENSE, attended, 0),
        functools.partial(spread_rows, QKV, attn_entry, joined_grad, 2),
    ]
    for stage in range(1, bits):
        for number, pause in ((DOWN, 1), (UP, 2), (DENSE, 0), (QKV, 3)):
            work.append(functools.partial(combines, number, stage))
            if pause and (stage < bits - 1 or number in (DOWN, UP)):
                work.append(functools.partial(several, pause))
    last = len(work) - 6
    hops = len(waiting) - 1 - bits
    places = [i * (last * 2 // 3) // hops for i in range(hops)]
    places += [last + i * 6 // bits for i in range(bits)] + [len(work)]
    for i, task in enumerate(work + [lambda: None]):
        for place, step in zip(places, waiting):
            if place == i:
                step()
        task()

    @pl.loop(slots[0], messages + half + LAG)
    def _(j):
        service(j)

    end_messages()
    for number in (DOWN, DENSE, UP, QKV):
        end_spread(number)
    store_vectors = fill(vectors, vectors_out, vec_send.at[0])
    store_vectors.start()
    store_vectors.wait()


def layer_call(mp_size, dp_size, operands):
    tokens, qkv, dense, up, down = (operands[i] for i in (0, 2, 3, 4, 5))
    count, width = tokens.shape
    inner_width, heads_width = up.shape[1], dense.shape[0]
    messages = 2 * (count // ROWS)
    bits = dp_size.bit_length() - 1
    owned = width // dp_size
    plans = (
        Spread(bits, owned, qkv.shape[1]),
        Spread(bits, heads_width, owned),
        Spread(bits, owned, inner_width),
        Spread(bits, inner_width, owned),
    )
    exchanges = bits + 2 * (mp_size // 2)
    vector_width = max(width, inner_width, qkv.shape[1])
    anywhere = pl.BlockSpec(memory_space=pl.ANY)
    vmem = pl.BlockSpec(memory_space=pltpu.VMEM)
    shape = jax.ShapeDtypeStruct
    out_shape = [
        shape((count, width), BF16),
        shape((count, width), BF16),
        shape((VECTORS, vector_width), F32),
        shape((2 * count, width), F32),
        *(shape((plan.rows, plan.cols), F32) for plan in plans),
        shape((count, width), BF16),
        shape((count, width), BF16),
        shape((count, heads_width), BF16),
        shape((count, inner_width), BF16),
        shape((count, inner_width), BF16),
    ]
    for plan in plans:
        out_shape += [shape(dims, F32) for dims in plan.shapes()]
    dma = pltpu.SemaphoreType.DMA
    scratch = [
        pltpu.VMEM((SLOTS, ROWS, width), F32),
        pltpu.VMEM((2 * SLOTS, ROWS, width), F32),
        pltpu.VMEM((2, ROWS, width), BF16),
        pltpu.VMEM((2, ROWS, width), BF16),
        pltpu.VMEM((2, ROWS, width), BF16),
        pltpu.VMEM((VECTORS, vector_width), F32),
        pltpu.VMEM((exchanges, VECTORS, vector_width), F32),
        pltpu.VMEM((count, qkv.shape[1]), BF16),
        pltpu.VMEM((count, LANES), F32),
        pltpu.VMEM((count, LANES), F32),
        dma((messages,)),
        dma((messages,)),
        dma((messages,)),
        dma((messages,)),
        dma((2,)),
        dma((2, 2)),
        dma((2,)),
        dma((exchanges,)),
        dma((exchanges,)),
    ]
    for plan in plans:
        scratch += [dma((plan.sems,)), dma((plan.sems,))]
    results = pl.pallas_call(
        functools.partial(layer_kernel, mp_size, plans),
        out_shape=tuple(out_shape),
        in_specs=[anywhere] * 6 + [vmem] * 7 + [pl.BlockSpec(memory_space=pltpu.SMEM)],
        out_specs=(anywhere,) * len(out_shape),
        scratch_shapes=scratch,
        compiler_params=pltpu.CompilerParams(
            collective_id=0, has_side_effects=True, vmem_limit_bytes=62 * 1024 * 1024
        ),
        cost_estimate=pl.CostEstimate(
            flops=6 * count * (width * (qkv.shape[1] + 2 * inner_width + heads_width)),
            bytes_accessed=300 << 20,
            transcendentals=0,
        ),
    )(*operands)
    return results[:3], results[4 : 4 + len(plans)]


def hand_out(dp_size, totals, *refs):
    refs = list(refs)
    vectors = refs.pop(0)
    number = (len(refs) - 1 - len(totals)) // 3
    sources, refs = refs[:number], refs[number:]
    targets, refs = refs[:number], refs[number:]
    pieces, refs = refs[: len(totals)], refs[len(totals) :]
    held, sems = refs[:number], refs[number]
    loads = [pltpu.make_async_copy(a, b, sems.at[0, i]) for i, (a, b) in enumerate(zip(sources, held))]
    stores = [pltpu.make_async_copy(a, b, sems.at[1, i]) for i, (a, b) in enumerate(zip(held, targets))]
    for copy in loads:
        copy.start()
    width = vectors.shape[1]
    for row, (total, piece) in enumerate(zip(totals, pieces)):
        size = total // dp_size
        shift = lax.rem(width - lax.axis_index("dp") * size, width)
        piece[...] = pltpu.roll(vectors[...], shift, 1)[row : row + 1, :size]
    for load, store in zip(loads, stores):
        load.wait()
        store.start()
    for copy in stores:
        copy.wait()


def hand_out_call(dp_size, totals, vectors, arrays):
    anywhere = pl.BlockSpec(memory_space=pl.ANY)
    vmem = pl.BlockSpec(memory_space=pltpu.VMEM)
    shape = jax.ShapeDtypeStruct
    results = pl.pallas_call(
        functools.partial(hand_out, dp_size, totals),
        out_shape=[shape(array.shape, array.dtype) for array in arrays]
        + [shape((1, total // dp_size), F32) for total in totals],
        in_specs=[vmem] + [anywhere] * len(arrays),
        out_specs=[anywhere] * len(arrays) + [vmem] * len(totals),
        scratch_shapes=[pltpu.VMEM(array.shape, array.dtype) for array in arrays]
        + [pltpu.SemaphoreType.DMA((2, len(arrays)))],
        compiler_params=pltpu.CompilerParams(vmem_limit_bytes=62 * 1024 * 1024),
    )(vectors, *arrays)
    return results[: len(arrays)], [piece[0] for piece in results[len(arrays) :]]


def per_device(
    mp_size,
    dp_size,
    tokens,
    lengths,
    attn_gain,
    attn_shift,
    mlp_gain,
    mlp_shift,
    qkv_weight,
    qkv_bias,
    dense_weight,
    up_weight,
    up_bias,
    down_weight,
    out_bias,
    cotangent,
):
    width = tokens.shape[1]
    (layer_output, input_grad, vectors), grads = layer_call(
        mp_size,
        dp_size,
        (
            tokens,
            cotangent,
            qkv_weight,
            dense_weight,
            up_weight,
            down_weight,
            attn_gain[None],
            attn_shift[None],
            mlp_gain[None],
            mlp_shift[None],
            qkv_bias[None],
            up_bias[None],
            out_bias[None],
            lengths,
        ),
    )
    totals = (width,) * 5 + (up_weight.shape[1], qkv_weight.shape[1])
    arrays, pieces = hand_out_call(dp_size, totals, vectors, (layer_output, input_grad, *grads))
    layer_output, input_grad, qkv_grad, dense_grad, up_grad, down_grad = arrays
    attn_gain_grad, attn_shift_grad, mlp_gain_grad, mlp_shift_grad = pieces[:4]
    return (
        layer_output,
        input_grad,
        attn_gain_grad,
        attn_shift_grad,
        mlp_gain_grad,
        mlp_shift_grad,
        qkv_grad,
        pieces[QKV_BIAS],
        dense_grad,
        up_grad,
        pieces[UP_BIAS],
        down_grad,
        pieces[OUT_BIAS],
    )


def solution(mesh):
    in_specs = (
        P("dp", None),
        P("dp", None),
        P(),
        P(),
        P(),
        P(),
        P(None, "mp"),
        P("mp"),
        P("mp", None),
        P(None, "mp"),
        P("mp"),
        P("mp", None),
        P(),
        P("dp", None),
    )
    out_specs = (
        P("dp", None),
        P("dp", None),
        P("dp"),
        P("dp"),
        P("dp"),
        P("dp"),
        P("dp", "mp"),
        P(("mp", "dp")),
        P("mp", "dp"),
        P("dp", "mp"),
        P(("mp", "dp")),
        P("mp", "dp"),
        P("dp"),
    )
    function = functools.partial(per_device, mesh.shape["mp"], mesh.shape["dp"])
    return jax.shard_map(
        function, mesh=mesh, in_specs=in_specs, out_specs=out_specs, check_vma=False
    )
```

```python
import functools
import math

import jax
import jax.numpy as jnp
from jax import lax
from jax.experimental import pallas as pl
from jax.experimental.pallas import tpu as pltpu
from jax.sharding import PartitionSpec as P

HEAD_DIM = 256
ROT = 64
EPSILON = 1e-05
LANES = 128

MESH = pl.DeviceIdType.MESH
ROWS = 32
SLOTS = 10
AHEAD = 5
AHEAD_ODD = 5
PENDING = 3
LAG = 1
CHUNK = 256
BLOCK = 32

F32 = jnp.float32
BF16 = jnp.bfloat16

VECTORS = 8
ATTN_GAIN, ATTN_SHIFT, MLP_GAIN, MLP_SHIFT, OUT_BIAS, UP_BIAS, QKV_BIAS = range(7)


def sine_cosine(angle):
    turns = jnp.floor(angle * (2.0 / math.pi) + 0.5)
    rest = angle - turns * 1.5703125 - turns * 4.837512969970703e-4 - turns * 7.549789954891882e-8
    square = rest * rest
    sine = rest + rest * square * (
        -1.6666654611e-1 + square * (8.3321608736e-3 - square * 1.9515295891e-4)
    )
    cosine = (
        1.0
        - 0.5 * square
        + square
        * square
        * (4.166664568298827e-2 + square * (-1.388731625493765e-3 + square * 2.443315711809948e-5))
    )
    quarter = turns - 4.0 * jnp.floor(turns * 0.25)
    odd = (quarter == 1.0) | (quarter == 3.0)
    flip_sine = quarter >= 2.0
    flip_cosine = (quarter == 1.0) | (quarter == 2.0)
    near_sine = jnp.where(odd, cosine, sine)
    near_cosine = jnp.where(odd, sine, cosine)
    return (
        jnp.where(flip_sine, -near_sine, near_sine),
        jnp.where(flip_cosine, -near_cosine, near_cosine),
    )


def rotary_tables(place, start):
    lane = lax.broadcasted_iota(jnp.int32, place.shape, 1)
    half = ROT // 2
    step = jnp.where(lane < half, lane, lane - half).astype(F32)
    freqs = jnp.exp(step * (-2.0 * math.log(10000.0) / ROT))
    sine, cosine = sine_cosine((place - start).astype(F32) * freqs)
    cosine = jnp.where(lane < ROT, cosine, 1.0)
    sine = jnp.where(lane < half, -sine, jnp.where(lane < ROT, sine, 0.0))
    return cosine, sine


def normalize(rows):
    centred = rows - jnp.mean(rows, axis=-1, keepdims=True)
    factor = lax.rsqrt(jnp.mean(centred * centred, axis=-1, keepdims=True) + EPSILON)
    return centred * factor, factor


def gelu_parts(v):
    cdf = 0.5 + 0.5 * lax.erf(v * math.sqrt(0.5))
    return v * cdf, cdf + v * jnp.exp(-0.5 * v * v) * (1.0 / math.sqrt(2.0 * math.pi))


def dot(left, right):
    return jnp.dot(left, right, preferred_element_type=F32)


def dot_cols(left, right):
    return lax.dot_general(left, right, (((1,), (1,)), ((), ())), preferred_element_type=F32)


def dot_rows(left, right):
    return lax.dot_general(left, right, (((0,), (0,)), ((), ())), preferred_element_type=F32)


def column_sum(x):
    return jnp.sum(x, axis=0, keepdims=True)


def span(start, size):
    return pl.ds(pl.multiple_of(start, size), size)


class Spread:
    def __init__(self, bits, rows, cols):
        self.bits, self.rows, self.cols = bits, rows, cols
        self.tiles = 1 << bits
        self.orders = ([0] + list(range(1, bits)), [0] + list(range(bits - 1, 0, -1)))
        count = self.tiles // 2
        self.first = {}
        for stage in range(1, bits):
            for side in range(2):
                self.first[stage, side] = count
                count += self.tiles >> (stage + 1)
        self.sems = count

    def masks(self, side, stage):
        order = self.orders[side]
        return [m for m in range(self.tiles) if not any((m >> b) & 1 for b in order[:stage])]

    def place(self, mask, side, stage):
        return self.masks(side, stage + 1).index(mask)

    def shapes(self):
        shapes = [(self.tiles // 2, self.rows, self.cols)]
        for stage in range(self.bits):
            shapes.append((self.tiles >> (stage + 1), self.rows, self.cols))
        return shapes


def layer_kernel(mp_size, plans, *refs):
    refs = list(refs)

    def take(number):
        taken = refs[:number]
        del refs[:number]
        return taken

    tokens, cotangent, qkv_weight, dense_weight, up_weight, down_weight = take(6)
    attn_gain, attn_shift, mlp_gain, mlp_shift, qkv_bias, up_bias, out_bias = take(7)
    lengths = take(1)[0]
    layer_out, input_grad, vectors_out, parts = take(4)
    grads_out = take(len(plans))
    attn_entry, mlp_entry, attended, hidden, hidden_grad = take(5)
    spreads = [(plan, take(1 + plan.bits)) for plan in plans]
    from_outer, held, token_rows, cot_rows, out_rows = take(5)
    vectors, vectors_in, joined_grad, cosine, sine = take(5)
    send_in, send_out, recv_outer, recv_inner, part_sems, row_sems, out_sems = take(7)
    vec_send, vec_recv = take(2)
    spread_sems = [take(2) for _ in plans]

    count, width = tokens.shape
    inner_width = up_weight.shape[1]
    heads_width = dense_weight.shape[0]
    local_heads = heads_width // HEAD_DIM
    bits = plans[0].bits
    steps = count // CHUNK
    scale = 1.0 / math.sqrt(HEAD_DIM)
    branch_messages = count // ROWS
    messages = 2 * branch_messages
    chunk_messages = CHUNK // ROWS
    half = mp_size // 2

    index = lax.axis_index("mp")
    upper = index // half
    level = index * (1 - upper) + (mp_size - 1 - index) * upper
    inner = index + 1 - 2 * upper
    outer = index - 1 + 2 * upper
    lag = half - level + LAG
    ahead = min(AHEAD, SLOTS - 1 - LAG - half)
    is_middle = level == half - 1
    total_place = (1 - level // (half - 1)) * SLOTS if half > 1 else 0
    device = lax.axis_index("dp")
    ahead = ahead + (device % 2) * (min(AHEAD_ODD, SLOTS - 1 - LAG - half) - ahead)

    def partner(bit):
        return device + (1 - 2 * ((device // (1 << bit)) % 2)) * (1 << bit)

    def owner(mask):
        total = 0
        for bit in range(bits):
            total = total + ((device // (1 << bit) + mask // (1 << bit)) % 2) * (1 << bit)
        return total

    def meet():
        barrier = pltpu.get_barrier_semaphore()
        pl.semaphore_signal(barrier, inc=1, device_id={"mp": inner}, device_id_type=MESH)
        for bit in range(bits):
            pl.semaphore_signal(barrier, inc=1, device_id={"dp": partner(bit)}, device_id_type=MESH)
        if half > 1:

            @pl.when(level > 0)
            def _():
                pl.semaphore_signal(barrier, inc=1, device_id={"mp": outer}, device_id_type=MESH)
                pl.semaphore_wait(barrier, 2 + bits)

            @pl.when(level == 0)
            def _():
                pl.semaphore_wait(barrier, 1 + bits)

        else:
            pl.semaphore_wait(barrier, 1 + bits)


    def slot(ref, k):
        return ref.at[lax.rem(k, SLOTS)]

    def sums(k):
        return held.at[lax.rem(k, SLOTS)]

    def from_inner(k):
        return held.at[lax.rem(k, SLOTS) + SLOTS]

    def totals(k):
        return held.at[lax.rem(k, SLOTS) + total_place]

    def message(ref, k):
        return ref.at[span(k * ROWS, ROWS)]

    def to_inner(k, source, landing, sem):
        return pltpu.make_async_remote_copy(
            src_ref=source,
            dst_ref=landing,
            send_sem=send_in.at[k],
            recv_sem=sem.at[k],
            device_id={"mp": inner},
            device_id_type=MESH,
        )

    def to_outer(k):
        return pltpu.make_async_remote_copy(
            src_ref=totals(k),
            dst_ref=from_inner(k),
            send_sem=send_out.at[k],
            recv_sem=recv_inner.at[k],
            device_id={"mp": outer},
            device_id_type=MESH,
        )

    def load_part(k):
        return pltpu.make_async_copy(message(parts, k), sums(k), part_sems.at[lax.rem(k, 2)])

    def load_rows(k):
        row, place = lax.rem(k, branch_messages), lax.rem(k, 2)
        return [
            pltpu.make_async_copy(
                message(tokens, row), token_rows.at[place], row_sems.at[0, place]
            ),
            pltpu.make_async_copy(
                message(cotangent, row), cot_rows.at[place], row_sems.at[1, place]
            ),
        ]

    def store_rows(k, target):
        place = lax.rem(k, 2)
        return pltpu.make_async_copy(
            out_rows.at[place], message(target, lax.rem(k, branch_messages)), out_sems.at[place]
        )

    def send_ahead(k):
        if half > 1:

            @pl.when((level == 0) & (k < messages))
            def _():
                to_inner(k, message(parts, k), slot(from_outer, k), recv_outer).start()

    def begin_messages():
        @pl.loop(0, ahead)
        def _(k):
            send_ahead(k)

        for copy in load_rows(0):
            copy.start()
        if half > 1:

            @pl.when(level > 0)
            def _():
                load_part(0).start()

        else:
            load_part(0).start()

    def add_inward(j):
        @pl.when(j < messages)
        def _():
            load_part(j).wait()

            @pl.when(j + 1 < messages)
            def _():
                load_part(j + 1).start()

            mine = sums(j)
            if half > 1:
                to_inner(j, mine, slot(from_outer, j), recv_outer).wait_recv()
                mine[...] += slot(from_outer, j)[...]

            @pl.when(is_middle)
            def _():
                to_inner(j, mine, from_inner(j), recv_inner).start()

            if half > 2:

                @pl.when(level < half - 1)
                def _():
                    to_inner(j, mine, slot(from_outer, j), recv_outer).start()

    def finish(k):
        place = lax.rem(k, 2)
        source = totals(k)

        @pl.when(k < branch_messages)
        def _():
            @pl.loop(0, ROWS // BLOCK)
            def _(b):
                rows = span(b * BLOCK, BLOCK)
                out_rows[place, rows] = (
                    token_rows[place, rows].astype(F32) + source[rows] + out_bias[...]
                ).astype(BF16)

        @pl.when(k >= branch_messages)
        def _():
            @pl.loop(0, ROWS // BLOCK)
            def _(b):
                rows = span(b * BLOCK, BLOCK)
                hat, factor = normalize(token_rows[place, rows].astype(F32))
                entry = source[rows]
                part = (
                    entry
                    - jnp.mean(entry, axis=-1, keepdims=True)
                    - hat * jnp.mean(entry * hat, axis=-1, keepdims=True)
                )
                out_rows[place, rows] = (
                    cot_rows[place, rows].astype(F32) + factor * part
                ).astype(BF16)

    def pass_outward(k):
        @pl.when((k >= 0) & (k < messages))
        def _():
            to_inner(k, sums(k), from_inner(k), recv_inner).wait()

            @pl.when(is_middle)
            def _():
                sums(k)[...] += from_inner(k)[...]

            if half > 1:

                @pl.when(level > 0)
                def _():
                    @pl.when(k >= PENDING)
                    def _():
                        to_outer(k - PENDING).wait_send()

                    to_outer(k).start()

            @pl.when(k + 1 < messages)
            def _():
                for copy in load_rows(k + 1):
                    copy.start()

            for copy in load_rows(k):
                copy.wait()

            @pl.when(k >= 2)
            def _():
                store_rows(k - 2, layer_out).wait()

            finish(k)

            @pl.when(k < branch_messages)
            def _():
                store_rows(k, layer_out).start()

            @pl.when(k >= branch_messages)
            def _():
                store_rows(k, input_grad).start()

    def service(j):
        send_ahead(j + ahead)
        if half > 1:

            @pl.when(level > 0)
            def _():
                add_inward(j)

        else:
            add_inward(j)
        pass_outward(j - lag)

    def end_messages():
        if half > 1:

            @pl.when(level > 0)
            def _():
                for k in range(messages - PENDING, messages):
                    to_outer(k).wait_send()

        for k in (messages - 2, messages - 1):
            store_rows(k, input_grad).wait()


    def spread_copy(number, stage, side, source, target, sem, bit):
        sends, recvs = spread_sems[number]
        return pltpu.make_async_remote_copy(
            src_ref=source,
            dst_ref=target,
            send_sem=sends.at[sem],
            recv_sem=recvs.at[sem],
            device_id={"dp": partner(bit)},
            device_id_type=MESH,
        )

    def side_rows(plan, side):
        return pl.ds(side * (plan.rows // 2), plan.rows // 2)

    def stage_copies(number, stage, side):
        plan, buffers = spreads[number]
        keep, landing = buffers[0], buffers[1 + stage]
        bit = plan.orders[side][stage]
        copies = []
        for mask in plan.masks(side, stage):
            if (mask >> bit) & 1:
                place = plan.place(mask ^ (1 << bit), side, stage)
                copies.append(
                    spread_copy(
                        number,
                        stage,
                        side,
                        keep.at[mask // 2, side_rows(plan, side)],
                        landing.at[place, side_rows(plan, side)],
                        plan.first[stage, side] + place,
                        bit,
                    )
                )
        return copies

    def tiles_of(number, compute, sent, kept, landed, sems, first, each):
        plan, buffers = spreads[number]
        half_tiles = plan.tiles // 2
        every = max(1, half_tiles // 4)

        def copy(i):
            return spread_copy(number, 0, 0, sent.at[lax.rem(i, 2)], buffers[1].at[i], i, 0)

        def load(i):
            return pltpu.make_async_copy(buffers[1].at[i], landed, sems.at[0])

        def store(i):
            return pltpu.make_async_copy(
                kept.at[lax.rem(i, 2)], buffers[0].at[i], sems.at[1 + lax.rem(i, 2)]
            )

        def begin_add(i):
            copy(i).wait_recv()
            load(i).start()

        def end_add(i):
            load(i).wait()
            kept.at[lax.rem(i, 2)][...] += landed[...]
            store(i).start()

        @pl.loop(0, half_tiles)
        def _(i):
            @pl.when(i >= 2)
            def _():
                copy(i - 2).wait_send()

            compute(owner(2 * i + 1), sent.at[lax.rem(i, 2)])
            copy(i).start()

            @pl.when(i >= 1)
            def _():
                begin_add(i - 1)

            if each == 2:

                @pl.when(lax.rem(i, every) == every - 1)
                def _():
                    service(first + 2 * (i // every))

            @pl.when(i >= 2)
            def _():
                store(i - 2).wait()

            compute(owner(2 * i), kept.at[lax.rem(i, 2)])

            @pl.when(i >= 1)
            def _():
                end_add(i - 1)

            if each >= 1:

                @pl.when(lax.rem(i, every) == every - 1)
                def _():
                    service(first + each * (i // every) + each - 1)

        begin_add(half_tiles - 1)
        end_add(half_tiles - 1)
        for i in (half_tiles - 2, half_tiles - 1):
            copy(i).wait_send()
            store(i).wait()
        for side in range(2):
            for copies in stage_copies(number, 1, side):
                copies.start()

    def combine(number, stage, side):
        plan, buffers = spreads[number]
        keep, landing = buffers[0], buffers[1 + stage]
        last = stage == bits - 1
        rows = plan.rows // 4

        masks = plan.masks(side, stage + 1)

        def run(mine, other, sems):
            for copy in stage_copies(number, stage, side):
                copy.wait_recv()
            loads, stores = [], []
            for mask in masks:
                place = plan.place(mask, side, stage)
                for piece in range(2):
                    there = pl.ds(side * (plan.rows // 2) + piece * rows, rows)
                    at = len(loads)
                    kept = keep.at[mask // 2, there]
                    loads.append(
                        [
                            pltpu.make_async_copy(kept, mine.at[at], sems.at[0, at]),
                            pltpu.make_async_copy(
                                landing.at[place, there], other.at[at], sems.at[1, at]
                            ),
                        ]
                    )
                    target = grads_out[number].at[there] if last else kept
                    stores.append(pltpu.make_async_copy(mine.at[at], target, sems.at[2, at]))
            for load in loads:
                for copy in load:
                    copy.start()
            for i, (load, store) in enumerate(zip(loads, stores)):
                for copy in load:
                    copy.wait()
                mine[i] += other[i]
                store.start()
            for store in stores:
                store.wait()
            if not last:
                for copy in stage_copies(number, stage + 1, side):
                    copy.start()

        pieces = 2 * len(masks)
        shape = (pieces, rows, plan.cols)
        pl.run_scoped(
            run,
            pltpu.VMEM(shape, F32),
            pltpu.VMEM(shape, F32),
            pltpu.SemaphoreType.DMA((3, pieces)),
        )

    def end_spread(number):
        plan, _ = spreads[number]
        for side in range(2):
            for stage in range(1, bits):
                for copy in stage_copies(number, stage, side):
                    copy.wait_send()


    def vector_copy(place, device_id):
        return pltpu.make_async_remote_copy(
            src_ref=vectors,
            dst_ref=vectors_in.at[place],
            send_sem=vec_send.at[place],
            recv_sem=vec_recv.at[place],
            device_id=device_id,
            device_id_type=MESH,
        )

    norms = pl.ds(0, 4)

    def inward_hop(hop):
        return vector_copy(bits + hop, {"mp": inner})

    def outward_hop(hop):
        return vector_copy(bits + half + hop, {"mp": outer})

    def vector_steps():
        steps = []

        def start_inward(hop):
            @pl.when(level == hop)
            def _():
                inward_hop(hop).start()

        def end_inward(hop):
            @pl.when(level == hop)
            def _():
                inward_hop(hop).wait_send()

            if hop < half - 1:

                @pl.when(level == hop + 1)
                def _():
                    inward_hop(hop).wait_recv()
                    vectors[norms] += vectors_in[bits + hop, norms]

            else:

                @pl.when(is_middle)
                def _():
                    inward_hop(hop).wait_recv()
                    vectors[norms] += vectors_in[bits + hop, norms]

        def start_outward(hop):
            @pl.when(level == hop + 1)
            def _():
                outward_hop(hop).start()

        def end_outward(hop):
            @pl.when(level == hop + 1)
            def _():
                outward_hop(hop).wait_send()

            @pl.when(level == hop)
            def _():
                outward_hop(hop).wait_recv()
                vectors[norms] = vectors_in[bits + half + hop, norms]

        def start_across(bit):
            vector_copy(bit, {"dp": partner(bit)}).start()

        def end_across(bit):
            vector_copy(bit, {"dp": partner(bit)}).wait()
            vectors[...] += vectors_in[bit]

        moves = [
            (functools.partial(start_inward, hop), functools.partial(end_inward, hop))
            for hop in range(half)
        ]
        moves += [
            (functools.partial(start_outward, hop), functools.partial(end_outward, hop))
            for hop in reversed(range(half - 1))
        ]
        moves += [
            (functools.partial(start_across, bit), functools.partial(end_across, bit))
            for bit in range(bits)
        ]

        def step(i):
            if i > 0:
                moves[i - 1][1]()
            if i < len(moves):
                moves[i][0]()

        return [functools.partial(step, i) for i in range(len(moves) + 1)]


    first_lanes = lax.broadcasted_iota(jnp.int32, (CHUNK, LANES), 1)

    def swap_halves(x):
        return jnp.where(
            first_lanes < ROT // 2,
            pltpu.roll(x, LANES - ROT // 2, 1),
            pltpu.roll(x, ROT // 2, 1),
        )

    def turn(x, rows, sign):
        low = x[:, :LANES]
        low = low * cosine[rows] + sign * swap_halves(low) * sine[rows]
        return jnp.concatenate([low, x[:, LANES:]], axis=1)

    def store_part(c, part, sem):
        copy = pltpu.make_async_copy(part, parts.at[span(c * CHUNK, CHUNK)], sem)
        copy.start()
        copy.wait()

    def forward(
        qkv,
        up,
        load_up,
        load_qkv,
        down,
        dense,
        keys,
        values,
        key_grad,
        value_grad,
        token_chunk,
        cot_chunk,
        attn_chunk,
        mlp_chunk,
        hidden_chunk,
        hidden_grad_chunk,
        slope,
        part,
        probs,
        queries,
        attended_chunk,
        attended_grad,
        w_sems,
        in_sems,
        out_chunk_sems,
        part_sem,
    ):
        load_down = pltpu.make_async_copy(down_weight, down, w_sems.at[0])
        load_dense = pltpu.make_async_copy(dense_weight, dense, w_sems.at[1])
        tile = min(512, inner_width)
        wide = min(512, width)

        def load_tokens(c):
            return pltpu.make_async_copy(
                tokens.at[span(c * CHUNK, CHUNK)], token_chunk, in_sems.at[0]
            )

        def load_cot(c):
            return pltpu.make_async_copy(
                cotangent.at[span(c * CHUNK, CHUNK)],
                cot_chunk.at[lax.rem(c, 2)],
                in_sems.at[1 + lax.rem(c, 2)],
            )

        def chunk_stores(c):
            pairs = (
                (attn_chunk, attn_entry),
                (mlp_chunk, mlp_entry),
                (attended_chunk, attended),
                (hidden_chunk, hidden),
                (hidden_grad_chunk, hidden_grad),
            )
            return [
                pltpu.make_async_copy(
                    source, target.at[span(c * CHUNK, CHUNK)], out_chunk_sems.at[i]
                )
                for i, (source, target) in enumerate(pairs)
            ]

        load_tokens(0).start()
        load_qkv.start()
        load_up.start()
        load_down.start()
        load_dense.start()
        meet()
        keys[...] = jnp.zeros_like(keys)
        values[...] = jnp.zeros_like(values)
        key_grad[...] = jnp.zeros_like(key_grad)
        value_grad[...] = jnp.zeros_like(value_grad)
        vectors[...] = jnp.zeros_like(vectors)

        def by_extent(c, function):
            low = 0
            while low < steps:
                high = min(steps, max(2 * low, 1))

                @pl.when((c >= low) & (c < high))
                def _():
                    function(high * CHUNK)

                low = high

        @pl.loop(0, steps)
        def _(c):
            rows = span(c * CHUNK, CHUNK)
            cot = cot_chunk.at[lax.rem(c, 2)]
            load_tokens(c).wait()

            @pl.when(c > 0)
            def _():
                for copy in chunk_stores(c - 1):
                    copy.wait()

            @pl.loop(0, CHUNK // BLOCK)
            def _(b):
                block = span(b * BLOCK, BLOCK)
                hat, _ = normalize(token_chunk[block].astype(F32))
                attn_chunk[block] = (hat * attn_gain[...] + attn_shift[...]).astype(BF16)
                mlp_chunk[block] = (hat * mlp_gain[...] + mlp_shift[...]).astype(BF16)

            @pl.when(c == 0)
            def _():
                load_qkv.wait()

            spot = lax.broadcasted_iota(jnp.int32, (CHUNK, LANES), 0) + c * CHUNK
            begin = jnp.zeros((CHUNK, LANES), jnp.int32)
            end = jnp.int32(0)
            for i in range(lengths.shape[1]):
                end = end + lengths[0, i]
                begin = jnp.where(spot >= end, end, begin)
            cosine[rows], sine[rows] = rotary_tables(spot, begin)

            for h in range(local_heads):
                cols = slice(h * HEAD_DIM, (h + 1) * HEAD_DIM)
                base = h * 3 * HEAD_DIM

                def joined(i):
                    there = slice(base + i * HEAD_DIM, base + (i + 1) * HEAD_DIM)
                    return dot(attn_chunk[...], qkv[:, there]) + qkv_bias[:, there]

                queries[:, cols] = turn(joined(0), rows, 1.0).astype(BF16)
                keys[rows, cols] = turn(joined(1), rows, 1.0).astype(BF16)
                values[rows, cols] = joined(2).astype(BF16)

            def attend(extent):
                place = lax.broadcasted_iota(jnp.int32, (CHUNK, extent), 1)
                here = lax.broadcasted_iota(jnp.int32, (CHUNK, extent), 0) + c * CHUNK
                allowed = (place >= begin[:, :1]) & (place <= here)
                for h in range(local_heads):
                    cols = slice(h * HEAD_DIM, (h + 1) * HEAD_DIM)
                    scores = dot_cols(queries[:, cols], keys[:extent, cols]) * scale
                    scores = jnp.where(allowed, scores, -1e30)
                    expo = jnp.exp(scores - jnp.max(scores, axis=-1, keepdims=True))
                    prob = expo * (1.0 / jnp.sum(expo, axis=-1, keepdims=True))
                    probs[h, :, :extent] = prob
                    attended_chunk[:, cols] = dot(prob.astype(BF16), values[:extent, cols]).astype(
                        BF16
                    )

            by_extent(c, attend)

            @pl.when(c > 0)
            def _():
                service(c * 4 - 2)

            @pl.when(c == 0)
            def _():
                load_up.wait()

            @pl.loop(0, inner_width // tile)
            def _(t):
                cols = span(t * tile, tile)
                pre = dot(mlp_chunk[...], up[:, cols]) + up_bias[:, cols]
                value, derivative = gelu_parts(pre)
                hidden_chunk[:, cols] = value.astype(BF16)
                slope[:, cols] = derivative

            @pl.when(c == 0)
            def _():
                load_down.wait()
                load_dense.wait()
                load_cot(0).start()

            @pl.loop(0, width // wide)
            def _(t):
                cols = span(t * wide, wide)
                part[:, cols] = dot(hidden_chunk[...], down[:, cols]) + dot(
                    attended_chunk[...], dense[:, cols]
                )

            store_part(c, part, part_sem.at[0])

            @pl.when(c == 0)
            def _():
                begin_messages()

            @pl.when(c > 0)
            def _():
                service(c * 4 - 1)

            load_cot(c).wait()

            @pl.when(c + 1 < steps)
            def _():
                load_tokens(c + 1).start()
                load_cot(c + 1).start()

            @pl.loop(0, inner_width // tile)
            def _(t):
                cols = span(t * tile, tile)
                grad = (slope[:, cols] * dot_cols(cot[...], down[cols, :])).astype(BF16)
                hidden_grad_chunk[:, cols] = grad
                vectors[UP_BIAS : UP_BIAS + 1, cols] += column_sum(grad.astype(F32))

            for copy in chunk_stores(c):
                copy.start()

            service(c * 4)
            attended_grad[...] = dot_cols(cot[...], dense[...]).astype(BF16)

            def attend_back(extent):
                for h in range(local_heads):
                    cols = slice(h * HEAD_DIM, (h + 1) * HEAD_DIM)
                    base = h * 3 * HEAD_DIM
                    grad = attended_grad[:, cols]
                    prob = probs[h, :, :extent]
                    prob_grad = dot_cols(grad, values[:extent, cols])
                    along = jnp.sum(prob * prob_grad, axis=-1, keepdims=True)
                    score_grad = (prob * (prob_grad - along)).astype(BF16)
                    query_grad = dot(score_grad, keys[:extent, cols]) * scale
                    joined_grad[rows, base : base + HEAD_DIM] = turn(query_grad, rows, -1.0).astype(
                        BF16
                    )
                    key_grad[:extent, cols] += dot_rows(score_grad, queries[:, cols]) * scale
                    value_grad[:extent, cols] += dot_rows(prob.astype(BF16), grad)

            by_extent(c, attend_back)

            @pl.loop(0, CHUNK // BLOCK)
            def _(b):
                block = span(b * BLOCK, BLOCK)
                vectors[OUT_BIAS : OUT_BIAS + 1, :width] += column_sum(cot[block].astype(F32))

            service(c * 4 + 1)

        for copy in chunk_stores(steps - 1):
            copy.wait()

        @pl.loop(0, steps)
        def _(c):
            rows = span(c * CHUNK, CHUNK)
            for h in range(local_heads):
                cols = slice(h * HEAD_DIM, (h + 1) * HEAD_DIM)
                base = h * 3 * HEAD_DIM
                joined_grad[rows, base + HEAD_DIM : base + 2 * HEAD_DIM] = turn(
                    key_grad[rows, cols], rows, -1.0
                ).astype(BF16)
                joined_grad[rows, base + 2 * HEAD_DIM : base + 3 * HEAD_DIM] = value_grad[
                    rows, cols
                ].astype(BF16)

    def backward(qkv, up, grad_chunk, token_chunk, hat, part, in_sems, part_sem, first_slot):
        wide = min(512, width)

        def loads(c):
            rows = span(c * CHUNK, CHUNK)
            return [
                pltpu.make_async_copy(
                    hidden_grad.at[rows], grad_chunk.at[lax.rem(c, 2)], in_sems.at[lax.rem(c, 2), 0]
                ),
                pltpu.make_async_copy(
                    tokens.at[rows], token_chunk.at[lax.rem(c, 2)], in_sems.at[lax.rem(c, 2), 1]
                ),
            ]

        for copy in loads(0):
            copy.start()

        @pl.loop(0, steps)
        def _(c):
            rows = span(c * CHUNK, CHUNK)
            for copy in loads(c):
                copy.wait()

            @pl.when(c + 1 < steps)
            def _():
                for copy in loads(c + 1):
                    copy.start()

            @pl.loop(0, CHUNK // BLOCK)
            def _(b):
                block = span(b * BLOCK, BLOCK)
                hat[block] = normalize(token_chunk[lax.rem(c, 2), block].astype(F32))[0]

            vectors[QKV_BIAS : QKV_BIAS + 1, : 3 * heads_width] += column_sum(
                joined_grad[rows].astype(F32)
            )

            @pl.loop(0, width // wide)
            def _(t):
                cols = span(t * wide, wide)
                attn_grad = dot_cols(joined_grad[rows], qkv[cols, :])
                mlp_grad = dot_cols(grad_chunk[lax.rem(c, 2)], up[cols, :])
                part[:, cols] = attn_grad * attn_gain[:, cols] + mlp_grad * mlp_gain[:, cols]
                near = hat[:, cols]
                for row, value in (
                    (ATTN_GAIN, attn_grad * near),
                    (ATTN_SHIFT, attn_grad),
                    (MLP_GAIN, mlp_grad * near),
                    (MLP_SHIFT, mlp_grad),
                ):
                    vectors[row : row + 1, cols] += column_sum(value)

                @pl.when(t == width // wide // 2 - 1)
                def _():
                    service(first_slot + 2 * c)

            store_part(steps + c, part, part_sem.at[0])
            service(first_slot + 2 * c + 1)

    def fill(source, target, sem):
        return pltpu.make_async_copy(source, target, sem)

    def spread_columns(number, left_source, each):
        plan, _ = spreads[number]
        depth = left_source.shape[1]

        def run(left, turned, right, sent, kept, landed, sems):
            loads = [fill(left_source, left, sems.at[0]), fill(cotangent, right, sems.at[1])]
            for copy in loads:
                copy.start()
            for copy in loads:
                copy.wait()

            @pl.loop(0, depth // HEAD_DIM)
            def _(b):
                there = span(b * HEAD_DIM, HEAD_DIM)
                turned[there, :] = left[:, there].T

            def compute(where, target):
                right_cols = right[:, span(where * plan.cols, plan.cols)]
                block = min(512, depth)

                @pl.loop(0, depth // block)
                def _(b):
                    there = span(b * block, block)
                    target[there, :] = dot(turned[there, :], right_cols)

            tiles_of(number, compute, sent, kept, landed, sems, take_slots(4 * each), each)
            if not each:
                next_slot()

        pl.run_scoped(
            run,
            pltpu.VMEM((count, depth), BF16),
            pltpu.VMEM((depth, count), BF16),
            pltpu.VMEM((count, width), BF16),
            pltpu.VMEM((2, plan.rows, plan.cols), F32),
            pltpu.VMEM((2, plan.rows, plan.cols), F32),
            pltpu.VMEM((plan.rows, plan.cols), F32),
            pltpu.SemaphoreType.DMA((3,)),
        )

    def spread_rows(number, left_source, right_source, each):
        plan, _ = spreads[number]
        resident = right_source is joined_grad

        def run(left, right, sent, kept, landed, sems):
            loads = [fill(left_source, left, sems.at[0])]
            if not resident:
                loads.append(fill(right_source, right, sems.at[1]))
            for copy in loads:
                copy.start()
            for copy in loads:
                copy.wait()
            use = joined_grad if resident else right

            def compute(where, target):
                turned = left[:, span(where * plan.rows, plan.rows)].T
                block = min(512, plan.cols)

                @pl.loop(0, plan.cols // block)
                def _(b):
                    there = span(b * block, block)
                    target[:, there] = dot(turned, use[:, there])

            tiles_of(number, compute, sent, kept, landed, sems, take_slots(4 * each), each)

        pl.run_scoped(
            run,
            pltpu.VMEM((count, width), BF16),
            pltpu.VMEM((16, LANES) if resident else (count, plan.cols), BF16),
            pltpu.VMEM((2, plan.rows, plan.cols), F32),
            pltpu.VMEM((2, plan.rows, plan.cols), F32),
            pltpu.VMEM((plan.rows, plan.cols), F32),
            pltpu.SemaphoreType.DMA((3,)),
        )

    QKV, DENSE, UP, DOWN = range(4)
    slots = [4 * steps - 2]
    waiting = vector_steps()

    def take_slots(number):
        slots[0] += number
        return slots[0] - number

    def next_slot():
        service(take_slots(1))

    def with_weights(qkv, up, w_sems):
        load_qkv = pltpu.make_async_copy(qkv_weight, qkv, w_sems.at[0])
        load_up = pltpu.make_async_copy(up_weight, up, w_sems.at[1])
        pl.run_scoped(
            functools.partial(forward, qkv, up, load_up, load_qkv),
            pltpu.VMEM(down_weight.shape, BF16),
            pltpu.VMEM(dense_weight.shape, BF16),
            pltpu.VMEM((count, heads_width), BF16),
            pltpu.VMEM((count, heads_width), BF16),
            pltpu.VMEM((count, heads_width), F32),
            pltpu.VMEM((count, heads_width), F32),
            pltpu.VMEM((CHUNK, width), BF16),
            pltpu.VMEM((2, CHUNK, width), BF16),
            pltpu.VMEM((CHUNK, width), BF16),
            pltpu.VMEM((CHUNK, width), BF16),
            pltpu.VMEM((CHUNK, inner_width), BF16),
            pltpu.VMEM((CHUNK, inner_width), BF16),
            pltpu.VMEM((CHUNK, inner_width), F32),
            pltpu.VMEM((CHUNK, width), F32),
            pltpu.VMEM((local_heads, CHUNK, count), F32),
            pltpu.VMEM((CHUNK, heads_width), BF16),
            pltpu.VMEM((CHUNK, heads_width), BF16),
            pltpu.VMEM((CHUNK, heads_width), BF16),
            pltpu.SemaphoreType.DMA((2,)),
            pltpu.SemaphoreType.DMA((3,)),
            pltpu.SemaphoreType.DMA((5,)),
            pltpu.SemaphoreType.DMA((1,)),
        )
        spread_columns(DOWN, hidden, 2)
        spread_rows(UP, mlp_entry, hidden_grad, 1)
        first = take_slots(2 * steps)
        pl.run_scoped(
            lambda *scratch: backward(qkv, up, *scratch, first),
            pltpu.VMEM((2, CHUNK, inner_width), BF16),
            pltpu.VMEM((2, CHUNK, width), BF16),
            pltpu.VMEM((CHUNK, width), F32),
            pltpu.VMEM((CHUNK, width), F32),
            pltpu.SemaphoreType.DMA((2, 2)),
            pltpu.SemaphoreType.DMA((1,)),
        )

    pl.run_scoped(
        with_weights,
        pltpu.VMEM(qkv_weight.shape, BF16),
        pltpu.VMEM(up_weight.shape, BF16),
        pltpu.SemaphoreType.DMA((2,)),
    )

    def several(number):
        first = take_slots(number)

        @pl.loop(first, first + number)
        def _(k):
            service(k)

    def combines(number, stage):
        for side in range(2):
            combine(number, stage, side)
            next_slot()

    work = [
        functools.partial(spread_columns, DENSE, attended, 0),
        functools.partial(spread_rows, QKV, attn_entry, joined_grad, 2),
    ]
    for stage in range(1, bits):
        for number, pause in ((DOWN, 1), (UP, 2), (DENSE, 0), (QKV, 3)):
            work.append(functools.partial(combines, number, stage))
            if pause and (stage < bits - 1 or number in (DOWN, UP)):
                work.append(functools.partial(several, pause))
    last = len(work) - 6
    hops = len(waiting) - 1 - bits
    places = [i * (last * 2 // 3) // hops for i in range(hops)]
    places += [last + i * 6 // bits for i in range(bits)] + [len(work)]
    for i, task in enumerate(work + [lambda: None]):
        for place, step in zip(places, waiting):
            if place == i:
                step()
        task()

    @pl.loop(slots[0], messages + half + LAG)
    def _(j):
        service(j)

    end_messages()
    for number in (DOWN, DENSE, UP, QKV):
        end_spread(number)
    store_vectors = fill(vectors, vectors_out, vec_send.at[0])
    store_vectors.start()
    store_vectors.wait()


def layer_call(mp_size, dp_size, operands):
    tokens, qkv, dense, up, down = (operands[i] for i in (0, 2, 3, 4, 5))
    count, width = tokens.shape
    inner_width, heads_width = up.shape[1], dense.shape[0]
    messages = 2 * (count // ROWS)
    bits = dp_size.bit_length() - 1
    owned = width // dp_size
    plans = (
        Spread(bits, owned, qkv.shape[1]),
        Spread(bits, heads_width, owned),
        Spread(bits, owned, inner_width),
        Spread(bits, inner_width, owned),
    )
    exchanges = bits + 2 * (mp_size // 2)
    vector_width = max(width, inner_width, qkv.shape[1])
    anywhere = pl.BlockSpec(memory_space=pl.ANY)
    vmem = pl.BlockSpec(memory_space=pltpu.VMEM)
    shape = jax.ShapeDtypeStruct
    out_shape = [
        shape((count, width), BF16),
        shape((count, width), BF16),
        shape((VECTORS, vector_width), F32),
        shape((2 * count, width), F32),
        *(shape((plan.rows, plan.cols), F32) for plan in plans),
        shape((count, width), BF16),
        shape((count, width), BF16),
        shape((count, heads_width), BF16),
        shape((count, inner_width), BF16),
        shape((count, inner_width), BF16),
    ]
    for plan in plans:
        out_shape += [shape(dims, F32) for dims in plan.shapes()]
    dma = pltpu.SemaphoreType.DMA
    scratch = [
        pltpu.VMEM((SLOTS, ROWS, width), F32),
        pltpu.VMEM((2 * SLOTS, ROWS, width), F32),
        pltpu.VMEM((2, ROWS, width), BF16),
        pltpu.VMEM((2, ROWS, width), BF16),
        pltpu.VMEM((2, ROWS, width), BF16),
        pltpu.VMEM((VECTORS, vector_width), F32),
        pltpu.VMEM((exchanges, VECTORS, vector_width), F32),
        pltpu.VMEM((count, qkv.shape[1]), BF16),
        pltpu.VMEM((count, LANES), F32),
        pltpu.VMEM((count, LANES), F32),
        dma((messages,)),
        dma((messages,)),
        dma((messages,)),
        dma((messages,)),
        dma((2,)),
        dma((2, 2)),
        dma((2,)),
        dma((exchanges,)),
        dma((exchanges,)),
    ]
    for plan in plans:
        scratch += [dma((plan.sems,)), dma((plan.sems,))]
    results = pl.pallas_call(
        functools.partial(layer_kernel, mp_size, plans),
        out_shape=tuple(out_shape),
        in_specs=[anywhere] * 6 + [vmem] * 7 + [pl.BlockSpec(memory_space=pltpu.SMEM)],
        out_specs=(anywhere,) * len(out_shape),
        scratch_shapes=scratch,
        compiler_params=pltpu.CompilerParams(
            collective_id=0, has_side_effects=True, vmem_limit_bytes=62 * 1024 * 1024
        ),
        cost_estimate=pl.CostEstimate(
            flops=6 * count * (width * (qkv.shape[1] + 2 * inner_width + heads_width)),
            bytes_accessed=300 << 20,
            transcendentals=0,
        ),
    )(*operands)
    return results[:3], results[4 : 4 + len(plans)]


def hand_out(dp_size, totals, *refs):
    refs = list(refs)
    vectors = refs.pop(0)
    number = (len(refs) - 1 - len(totals)) // 3
    sources, refs = refs[:number], refs[number:]
    targets, refs = refs[:number], refs[number:]
    pieces, refs = refs[: len(totals)], refs[len(totals) :]
    held, sems = refs[:number], refs[number]
    loads = [pltpu.make_async_copy(a, b, sems.at[0, i]) for i, (a, b) in enumerate(zip(sources, held))]
    stores = [pltpu.make_async_copy(a, b, sems.at[1, i]) for i, (a, b) in enumerate(zip(held, targets))]
    for copy in loads:
        copy.start()
    width = vectors.shape[1]
    for row, (total, piece) in enumerate(zip(totals, pieces)):
        size = total // dp_size
        shift = lax.rem(width - lax.axis_index("dp") * size, width)
        piece[...] = pltpu.roll(vectors[...], shift, 1)[row : row + 1, :size]
    for load, store in zip(loads, stores):
        load.wait()
        store.start()
    for copy in stores:
        copy.wait()


def hand_out_call(dp_size, totals, vectors, arrays):
    anywhere = pl.BlockSpec(memory_space=pl.ANY)
    vmem = pl.BlockSpec(memory_space=pltpu.VMEM)
    shape = jax.ShapeDtypeStruct
    results = pl.pallas_call(
        functools.partial(hand_out, dp_size, totals),
        out_shape=[shape(array.shape, array.dtype) for array in arrays]
        + [shape((1, total // dp_size), F32) for total in totals],
        in_specs=[vmem] + [anywhere] * len(arrays),
        out_specs=[anywhere] * len(arrays) + [vmem] * len(totals),
        scratch_shapes=[pltpu.VMEM(array.shape, array.dtype) for array in arrays]
        + [pltpu.SemaphoreType.DMA((2, len(arrays)))],
        compiler_params=pltpu.CompilerParams(vmem_limit_bytes=62 * 1024 * 1024),
    )(vectors, *arrays)
    return results[: len(arrays)], [piece[0] for piece in results[len(arrays) :]]


def per_device(
    mp_size,
    dp_size,
    tokens,
    lengths,
    attn_gain,
    attn_shift,
    mlp_gain,
    mlp_shift,
    qkv_weight,
    qkv_bias,
    dense_weight,
    up_weight,
    up_bias,
    down_weight,
    out_bias,
    cotangent,
):
    width = tokens.shape[1]
    (layer_output, input_grad, vectors), grads = layer_call(
        mp_size,
        dp_size,
        (
            tokens,
            cotangent,
            qkv_weight,
            dense_weight,
            up_weight,
            down_weight,
            attn_gain[None],
            attn_shift[None],
            mlp_gain[None],
            mlp_shift[None],
            qkv_bias[None],
            up_bias[None],
            out_bias[None],
            lengths,
        ),
    )
    totals = (width,) * 5 + (up_weight.shape[1], qkv_weight.shape[1])
    arrays, pieces = hand_out_call(dp_size, totals, vectors, (layer_output, input_grad, *grads))
    layer_output, input_grad, qkv_grad, dense_grad, up_grad, down_grad = arrays
    attn_gain_grad, attn_shift_grad, mlp_gain_grad, mlp_shift_grad = pieces[:4]
    return (
        layer_output,
        input_grad,
        attn_gain_grad,
        attn_shift_grad,
        mlp_gain_grad,
        mlp_shift_grad,
        qkv_grad,
        pieces[QKV_BIAS],
        dense_grad,
        up_grad,
        pieces[UP_BIAS],
        down_grad,
        pieces[OUT_BIAS],
    )


def solution(mesh):
    in_specs = (
        P("dp", None),
        P("dp", None),
        P(),
        P(),
        P(),
        P(),
        P(None, "mp"),
        P("mp"),
        P("mp", None),
        P(None, "mp"),
        P("mp"),
        P("mp", None),
        P(),
        P("dp", None),
    )
    out_specs = (
        P("dp", None),
        P("dp", None),
        P("dp"),
        P("dp"),
        P("dp"),
        P("dp"),
        P("dp", "mp"),
        P(("mp", "dp")),
        P("mp", "dp"),
        P("dp", "mp"),
        P(("mp", "dp")),
        P("mp", "dp"),
        P("dp"),
    )
    function = functools.partial(per_device, mesh.shape["mp"], mesh.shape["dp"])
    return jax.shard_map(
        function, mesh=mesh, in_specs=in_specs, out_specs=out_specs, check_vma=False
    )
```
